256 devices in a mesh: gx: 8 (over x, core), gy: 4 (over z_hi), gz: 8 (over y, z_lo).
Axes of the slice: x: 4, y: 4, z: 8 (z_hi: 4, z_lo: 2; z = z_hi * 2 + z_lo), core: 2. Of those that a mesh axis runs over, the one named last changes fastest.
Arguments:
- positions: float32 [3, 16384], P(None, ('gx', 'gy', 'gz')), as said below
- atom_features: float32 [16384, 256], P(('gx', 'gy', 'gz')), may hold values from -6 to 6
- species: int32 [16384], P(('gx', 'gy', 'gz')), may hold values from 0 to 3
- edge_neighbor: int32 [16384, 128], P(('gx', 'gy', 'gz')), may hold values from 0 to 1338, as said below
- edge_live: int32 [16384, 128], P(('gx', 'gy', 'gz')), may hold values from 0 to 1, as said below
- send_list: int32 [6912, 48], P(('gx', 'gy', 'gz')), may hold values from 0 to 63, as said below
- species_scale: float32 [4], replicated, may hold values from 0.5 to 2
- species_shift: float32 [4], replicated, may hold values from -4 to 4
- w_center: bfloat16 [256, 256], replicated, may hold values from -0.375 to 0.375
- w_neighbor: bfloat16 [256, 256], replicated, may hold values from -0.375 to 0.375
- w_basis: bfloat16 [8, 256], replicated, may hold values from -2 to 2
- w_env: bfloat16 [256, 192], replicated, may hold values from -0.375 to 0.375
- w_latent: bfloat16 [448, 256], replicated, may hold values from -0.25 to 0.25
- w_out: bfloat16 [256, 128], replicated, may hold values from -0.375 to 0.375
- w_final: float32 [128], replicated, may hold values from -0.125 to 0.125
Outputs:
- atom_energy: float32 [16384], P(('gx', 'gy', 'gz'))
- forces: float32 [3, 16384], P(None, ('gx', 'gy', 'gz'))
- feature_grad: float32 [16384, 256], P(('gx', 'gy', 'gz'))
The draws below stay inside these ranges and needn't reach their ends.
Inputs may be any that keep to these rules, and one draw needn't show every extreme that they name: `edge_neighbor`: row a names the 128 neighbour slots of atom a, whose device is a // 64: an index into that device's local list (owned atoms, then ghost cell c entry g at 64 + c * 48 + g); never the atom itself, never ghost cell 13, and a ghost entry only if the sender listed a real atom there. Pairs are at most three lattice sites apart along each axis. `edge_live`: slots with 0 still name another atom. `send_list`: row 27 e + c lists local indices of owned atoms of device e sent in travel direction c; a direction's list holds the atoms of the box of lattice sites that it covers (3 layers along each axis where the direction moves, the whole cell along the others), and entries past that box's size, and all of cell 13, are arbitrary owned atoms. `positions`: each device's atoms lie inside its own cell, and any two atoms, ghost images included, are at least 1.7 apart.
All inputs are finite; a program needn't handle non-finite values.
Results may differ from the reference program's by a relative error of at most 0.011.
Values may be sent and summed in bfloat16 or wider, within the bound.
A program may use at most 64 MiB of HBM per device.

```python
import math
import jax
import jax.numpy as jnp
import numpy as np
from jax import lax

SIDE = 4
DEPTH = 4
REACH = 3
NBR = 128
NB = 8
SPEC = 4
BLK = 4
HF = 256
LAT = 256
CH = 64
OUTW = 128
A_DEV = 64
G = 48
ATOMS = 16384
N_GX = 8
N_GY = 4
N_GZ = 8


lattice_spacing = 2.15


def offset_table():
    span = np.arange(-3, 4)
    stacked = np.stack(np.meshgrid(span, span, span, indexing='ij'), -1).reshape(-1, 3)
    squared = (stacked * stacked).sum(1)
    return stacked[(squared > 0) & (squared <= 9)]


def lattice_layout(key):
    devices = N_GX * N_GY * N_GZ
    order_keys = jax.random.split(jax.random.fold_in(key, 11), devices)

    def permute(subkey):
        return jax.random.permutation(subkey, A_DEV)
    order = jax.vmap(permute)(order_keys).astype(jnp.int32)
    device_rows = jnp.arange(devices, dtype=jnp.int32)[:, None]
    inverse = jnp.zeros((devices, A_DEV), jnp.int32).at[device_rows, order].set(jnp.arange(A_DEV, dtype=jnp.int32)[None, :])
    richness = jax.random.randint(jax.random.fold_in(key, 12), (devices, 1), 0, 5)
    picker = jax.random.randint(jax.random.fold_in(key, 13), (devices, A_DEV), 0, 16)
    flavor = jax.random.randint(jax.random.fold_in(key, 14), (devices, A_DEV), 0, 2)
    kinds = jnp.where(picker < 2 * richness, 2 + flavor, flavor).astype(jnp.int32)
    return (order, inverse, kinds)


def edge_table(key):
    order, inverse, kinds = lattice_layout(key)
    devices = N_GX * N_GY * N_GZ
    offsets = jnp.asarray(offset_table(), dtype=jnp.int32)
    listed = offsets.shape[0]
    spare_count = NBR - listed
    spare_pick = jax.random.randint(jax.random.fold_in(key, 21), (devices, A_DEV, spare_count), 0, listed).astype(jnp.int32)
    base_pick = jnp.broadcast_to(jnp.arange(listed, dtype=jnp.int32), (devices, A_DEV, listed))
    candidate = jnp.concatenate([base_pick, spare_pick], axis=2)
    scores = jax.random.randint(jax.random.fold_in(key, 22), (devices, A_DEV, NBR), 0, 1 << 20) * NBR + jnp.arange(NBR, dtype=jnp.int32)
    shuffle = jnp.argsort(scores, axis=2).astype(jnp.int32)
    picked = jnp.take_along_axis(candidate, shuffle, axis=2)
    is_spare = shuffle >= listed
    chosen = offsets[picked]
    cell_sizes = jnp.array([SIDE, SIDE, DEPTH], dtype=jnp.int32)
    site_coords = jnp.stack([order // (SIDE * DEPTH), order // DEPTH % SIDE, order % DEPTH], axis=-1)
    target = site_coords[:, :, None, :] + chosen
    step_out = (target + cell_sizes) // cell_sizes - 1
    wrapped = target - step_out * cell_sizes
    device_ids = jnp.arange(devices, dtype=jnp.int32)
    home_cell = jnp.stack([device_ids // (N_GY * N_GZ), device_ids // N_GZ % N_GY, device_ids % N_GZ], axis=-1)
    grid_dims = jnp.array([N_GX, N_GY, N_GZ], dtype=jnp.int32)
    other_cell = (home_cell[:, None, None, :] + step_out) % grid_dims
    other_id = (other_cell[..., 0] * N_GY + other_cell[..., 1]) * N_GZ + other_cell[..., 2]
    other_site = (wrapped[..., 0] * SIDE + wrapped[..., 1]) * DEPTH + wrapped[..., 2]
    other_atom = inverse[other_id, other_site]
    other_kind = kinds[other_id, other_atom]
    travel = -step_out
    cell_index = (travel[..., 0] + 1) * 9 + (travel[..., 1] + 1) * 3 + travel[..., 2] + 1
    lengths = jnp.where(travel != 0, REACH, cell_sizes)
    lowest = jnp.where(travel == 1, cell_sizes - REACH, 0)
    inner_pos = wrapped - lowest
    slot_rank = (inner_pos[..., 0] * lengths[..., 1] + inner_pos[..., 1]) * lengths[..., 2] + inner_pos[..., 2]
    inside = jnp.all(step_out == 0, axis=-1)
    neighbor = jnp.where(inside, other_atom, A_DEV + cell_index * G + slot_rank)
    limits = jnp.array([9, 8, 6, 5], dtype=jnp.int32)
    reach_sq = jnp.sum(chosen * chosen, axis=-1)
    allowed = (limits[kinds[:, :, None]] + limits[other_kind]) // 2
    live_mask = jnp.where(is_spare, 0, (reach_sq <= allowed).astype(jnp.int32))
    return (neighbor.reshape(devices * A_DEV, NBR).astype(jnp.int32), live_mask.reshape(devices * A_DEV, NBR).astype(jnp.int32))


def draw_positions(key, part):
    order, inverse, kinds = lattice_layout(key)
    key = jax.random.fold_in(key, 3)
    site_coords = jnp.stack([order // (SIDE * DEPTH), order // DEPTH % SIDE, order % DEPTH]).astype(jnp.float32) + 0.5
    jitter = jax.random.uniform(key, site_coords.shape, jnp.float32, -0.1, 0.1)
    return ((site_coords + jitter) * lattice_spacing).reshape(3, -1)


def draw_species(key, part):
    order, inverse, kinds = lattice_layout(key)
    key = jax.random.fold_in(key, 4)
    return kinds.reshape(-1)


def draw_edge_neighbor(key, part):
    neighbor, live_mask = edge_table(key)
    key = jax.random.fold_in(key, 5)
    return neighbor


def draw_edge_live(key, part):
    neighbor, live_mask = edge_table(key)
    key = jax.random.fold_in(key, 6)
    return live_mask


def draw_send_list(key, part):
    order, inverse, kinds = lattice_layout(key)
    key = jax.random.fold_in(key, 7)
    devices = N_GX * N_GY * N_GZ
    cell_index = jnp.arange(27, dtype=jnp.int32)
    travel = jnp.stack([cell_index // 9 - 1, cell_index // 3 % 3 - 1, cell_index % 3 - 1], axis=-1)
    cell_sizes = jnp.array([SIDE, SIDE, DEPTH], dtype=jnp.int32)
    lengths = jnp.where(travel != 0, REACH, cell_sizes)
    lowest = jnp.where(travel == 1, cell_sizes - REACH, 0)
    entry = jnp.arange(G, dtype=jnp.int32)[None, :]
    box_size = (lengths[:, 0] * lengths[:, 1] * lengths[:, 2])[:, None]
    step_x = entry // (lengths[:, 1:2] * lengths[:, 2:3])
    step_y = entry // lengths[:, 2:3] % lengths[:, 1:2]
    step_z = entry % lengths[:, 2:3]
    site_index = ((lowest[:, 0:1] + step_x) * SIDE + lowest[:, 1:2] + step_y) * DEPTH + lowest[:, 2:3] + step_z
    valid = (entry < box_size) & (cell_index[:, None] != 13)
    site_index = jnp.clip(site_index, 0, A_DEV - 1)
    listed_atoms = inverse[:, site_index]
    filler = jax.random.randint(key, (devices, 27, G), 0, A_DEV).astype(jnp.int32)
    return jnp.where(valid[None], listed_atoms, filler).reshape(devices * 27, G).astype(jnp.int32)


def level_of(key, extent, shards, smallest, high):
    def one(axis_at, parts):
        steps = jax.random.uniform(jax.random.fold_in(jax.random.fold_in(key, 6), axis_at), (parts,), jnp.float32, smallest / len(shards), high / len(shards))
        return jnp.repeat(jnp.exp(steps), extent[axis_at] // parts).reshape((-1,) + (1,) * (len(extent) - axis_at - 1))

    gain = one(*shards[0])
    for cut in shards[1:]:
        gain = gain * one(*cut)
    return gain


def scatter_about(own_key, shape, scale, limit, cuts=(), kind=jnp.bfloat16):
    entries = scale * jax.random.normal(own_key, shape, jnp.float32)
    if cuts:
        entries = entries * level_of(own_key, shape, cuts, -0.22, 0.18)
    return jnp.clip(entries, -limit, limit).astype(kind)


def setup_inputs(seed: int = 0) -> dict:
    seeds = jax.random.split(jax.random.key(seed), 16)
    positions = draw_positions(jax.random.fold_in(seeds[15], 71), 0)
    atom_features = scatter_about(seeds[1], (ATOMS, HF), 1.0, 6.0, ((0, 256),), jnp.float32)
    species = draw_species(jax.random.fold_in(seeds[15], 71), 0)
    edge_neighbor = draw_edge_neighbor(jax.random.fold_in(seeds[15], 71), 0)
    edge_live = draw_edge_live(jax.random.fold_in(seeds[15], 71), 0)
    send_list = draw_send_list(jax.random.fold_in(seeds[15], 71), 0)
    species_scale = jnp.clip(jnp.exp(jax.random.uniform(seeds[6], (SPEC,), jnp.float32, math.log(0.5), math.log(2.0))), 0.5, 2.0)
    species_shift = scatter_about(seeds[7], (SPEC,), 1.0, 4.0, (), jnp.float32)
    w_center = scatter_about(seeds[8], (HF, LAT), HF ** -0.5, 0.375)
    w_neighbor = scatter_about(seeds[9], (HF, LAT), HF ** -0.5, 0.375)
    w_basis = scatter_about(seeds[10], (NB, LAT), NB ** -0.5, 2.0)
    w_env = scatter_about(seeds[11], (LAT, 3 * CH), LAT ** -0.5, 0.375)
    w_latent = scatter_about(seeds[12], (LAT + 3 * CH, LAT), (LAT + 3 * CH) ** -0.5, 0.25)
    w_out = scatter_about(seeds[13], (LAT, OUTW), LAT ** -0.5, 0.375)
    w_final = scatter_about(seeds[14], (OUTW,), (16 * OUTW) ** -0.5, 0.125, (), jnp.float32)
    return dict(positions=positions, atom_features=atom_features, species=species, edge_neighbor=edge_neighbor, edge_live=edge_live, send_list=send_list, species_scale=species_scale, species_shift=species_shift, w_center=w_center, w_neighbor=w_neighbor, w_basis=w_basis, w_env=w_env, w_latent=w_latent, w_out=w_out, w_final=w_final)


cut_radius = 6.0
lattice_spacing = 2.15
env_norm = 0.125

def harmonics(unit_x, unit_y, unit_z):
    sqrt_three = math.sqrt(3.0)
    sqrt_five = math.sqrt(5.0)
    sqrt_fifteen = math.sqrt(15.0)
    degree_one = jnp.stack([sqrt_three * unit_x, sqrt_three * unit_y, sqrt_three * unit_z])
    degree_two = jnp.stack([sqrt_fifteen * unit_x * unit_y, sqrt_fifteen * unit_y * unit_z, 0.5 * sqrt_five * (3.0 * unit_z * unit_z - 1.0), sqrt_fifteen * unit_x * unit_z, 0.5 * sqrt_fifteen * (unit_x * unit_x - unit_y * unit_y)])
    return (degree_one, degree_two)

def edge_sums(all_coords, neighbor_proj, center_proj, first_row, neighbor, live_mask, w_basis, w_env, w_latent, w_out, w_final):
    block_size, slot_count = neighbor.shape
    latent_width = center_proj.shape[1]
    channels = w_env.shape[1] // 3
    basis_count = w_basis.shape[0]
    center_coords = lax.dynamic_slice_in_dim(all_coords, first_row, block_size, 1)
    flat_index = neighbor.reshape(-1)
    other_coords = jnp.take(all_coords, flat_index, axis=1).reshape(3, block_size, slot_count)
    relative = other_coords - center_coords[:, :, None]
    distance = jnp.sqrt(lax.optimization_barrier(jnp.sum(relative * relative, axis=0)))
    unit_vec = relative / distance[None]
    scaled = distance / cut_radius
    polynomial = 1.0 - 28.0 * scaled ** 6 + 48.0 * scaled ** 7 - 21.0 * scaled ** 8
    envelope = jnp.where(scaled < 1.0, polynomial, 0.0) * live_mask.astype(jnp.float32)
    frequency = jnp.arange(1, basis_count + 1).astype(jnp.float32) * (math.pi / cut_radius)
    bessel = math.sqrt(2.0 / cut_radius) * jnp.sin(distance[:, :, None] * frequency) / distance[:, :, None]
    radial = jnp.dot(bessel.reshape(-1, basis_count).astype(jnp.bfloat16), w_basis, preferred_element_type=jnp.float32)
    preact = jnp.take(neighbor_proj, flat_index, axis=0) + radial + jnp.repeat(center_proj, slot_count, axis=0)
    env_flat = envelope.reshape(-1, 1)
    latent = env_flat * jax.nn.silu(preact)
    latent_half = latent.astype(jnp.bfloat16)
    weights = jnp.dot(latent_half, w_env, preferred_element_type=jnp.float32).reshape(block_size, slot_count, 3, channels)
    degree_one, degree_two = harmonics(unit_vec[0], unit_vec[1], unit_vec[2])
    weight_zero = weights[:, :, 0]
    weight_one = weights[:, :, 1]
    weight_two = weights[:, :, 2]
    env_zero = env_norm * lax.optimization_barrier(jnp.sum(weight_zero, axis=1))
    env_one = env_norm * lax.optimization_barrier(jnp.sum(degree_one[:, :, :, None] * weight_one[None], axis=2))
    env_two = env_norm * lax.optimization_barrier(jnp.sum(degree_two[:, :, :, None] * weight_two[None], axis=2))
    scalar_zero = weight_zero * env_zero[:, None, :]
    scalar_one = weight_one * lax.optimization_barrier(jnp.sum(degree_one[:, :, :, None] * env_one[:, :, None, :], axis=0))
    scalar_two = weight_two * lax.optimization_barrier(jnp.sum(degree_two[:, :, :, None] * env_two[:, :, None, :], axis=0))
    scalars = jnp.concatenate([scalar_zero, scalar_one, scalar_two], axis=2).reshape(block_size * slot_count, 3 * channels)
    update = jax.nn.silu(jnp.dot(latent_half, w_latent[:latent_width], preferred_element_type=jnp.float32) + jnp.dot(scalars.astype(jnp.bfloat16), w_latent[latent_width:], preferred_element_type=jnp.float32))
    refined = latent + env_flat * update
    hidden = jax.nn.silu(jnp.dot(refined.astype(jnp.bfloat16), w_out, preferred_element_type=jnp.float32))
    edge_energy = envelope * lax.optimization_barrier(jnp.sum(hidden * w_final, axis=1)).reshape(block_size, slot_count)
    return lax.optimization_barrier(jnp.sum(edge_energy, axis=1))

def local_terms(own_coords, own_features, ghost_coords, ghost_features, species, neighbor, live_mask, species_scale, species_shift, w_center, w_neighbor, w_basis, w_env, w_latent, w_out, w_final, block_size):
    atom_count = own_coords.shape[1]
    all_coords = jnp.concatenate([own_coords, ghost_coords], axis=1)
    all_features = jnp.concatenate([own_features, ghost_features.astype(jnp.float32)], axis=0)

    def project(features_all):
        rounded = features_all.astype(jnp.bfloat16)
        return (jnp.dot(rounded[:atom_count], w_center, preferred_element_type=jnp.float32), jnp.dot(rounded, w_neighbor, preferred_element_type=jnp.float32))
    (center_proj, neighbor_proj), project_back = jax.vjp(project, all_features)
    kinds = jnp.arange(species_scale.shape[0], dtype=jnp.int32)
    matches = species[:, None] == kinds[None, :]
    atom_scale = lax.optimization_barrier(jnp.sum(jnp.where(matches, species_scale[None, :], 0.0), axis=1))
    atom_shift = lax.optimization_barrier(jnp.sum(jnp.where(matches, species_shift[None, :], 0.0), axis=1))

    def block_step(totals, block_index):
        coord_grad, proj_grad = totals
        first_row = block_index * block_size
        center_block = lax.dynamic_slice_in_dim(center_proj, first_row, block_size, 0)
        neighbor_block = lax.dynamic_slice_in_dim(neighbor, first_row, block_size, 0)
        live_block = lax.dynamic_slice_in_dim(live_mask, first_row, block_size, 0)
        scale_block = lax.dynamic_slice_in_dim(atom_scale, first_row, block_size, 0)

        def energy_of(coords_all, proj_all, center_rows):
            return edge_sums(coords_all, proj_all, center_rows, first_row, neighbor_block, live_block, w_basis, w_env, w_latent, w_out, w_final)
        sums, energy_back = jax.vjp(energy_of, all_coords, neighbor_proj, center_block)
        grad_coords, grad_proj, grad_center = energy_back(scale_block)
        return ((coord_grad + grad_coords, proj_grad + grad_proj), (sums, grad_center))
    start_totals = (jnp.zeros(all_coords.shape, jnp.float32), jnp.zeros(neighbor_proj.shape, jnp.float32))
    (coord_grad, proj_grad), (sums, center_grad) = lax.scan(block_step, start_totals, jnp.arange(atom_count // block_size, dtype=jnp.int32))
    atom_energy = atom_scale * sums.reshape(-1) + atom_shift
    feature_grad, = project_back((center_grad.reshape(atom_count, -1), proj_grad))
    return (atom_energy, coord_grad[:, :atom_count], coord_grad[:, atom_count:], feature_grad[:atom_count], feature_grad[atom_count:])

def reference(positions, atom_features, species, edge_neighbor, edge_live, send_list, species_scale, species_shift, w_center, w_neighbor, w_basis, w_env, w_latent, w_out, w_final):
    devices = N_GX * N_GY * N_GZ
    lists = send_list.reshape(devices, 27, G)
    cell_index = jnp.arange(27, dtype=jnp.int32)
    travel = jnp.stack([cell_index // 9 - 1, cell_index // 3 % 3 - 1, cell_index % 3 - 1])
    cell_size = jnp.array([SIDE, SIDE, DEPTH], dtype=jnp.float32) * lattice_spacing
    shift_table = travel.astype(jnp.float32) * cell_size[:, None]

    def per_device(totals, device):
        coord_total, feature_total = totals
        gx_index = device // (N_GY * N_GZ)
        gy_index = device // N_GZ % N_GY
        gz_index = device % N_GZ
        source = ((gx_index - travel[0]) % N_GX * N_GY + (gy_index - travel[1]) % N_GY) * N_GZ + (gz_index - travel[2]) % N_GZ
        ghost_rows = (source[:, None] * A_DEV + lists[source, cell_index]).reshape(-1).astype(jnp.int32)
        ghost_features = atom_features[ghost_rows]
        ghost_coords = (positions[:, ghost_rows].reshape(3, 27, G) - shift_table[:, :, None]).reshape(3, 27 * G)
        first_atom = (device * A_DEV).astype(jnp.int32)
        own_rows = first_atom + jnp.arange(A_DEV, dtype=jnp.int32)
        own_coords = lax.dynamic_slice_in_dim(positions, first_atom, A_DEV, 1)
        own_features = lax.dynamic_slice_in_dim(atom_features, first_atom, A_DEV, 0)
        own_species = lax.dynamic_slice_in_dim(species, first_atom, A_DEV, 0)
        own_neighbor = lax.dynamic_slice_in_dim(edge_neighbor, first_atom, A_DEV, 0)
        own_live = lax.dynamic_slice_in_dim(edge_live, first_atom, A_DEV, 0)
        energy, own_cgrad, ghost_cgrad, own_fgrad, ghost_fgrad = local_terms(own_coords, own_features, ghost_coords, ghost_features, own_species, own_neighbor, own_live, species_scale, species_shift, w_center, w_neighbor, w_basis, w_env, w_latent, w_out, w_final, BLK)
        coord_total = coord_total.at[:, own_rows].add(own_cgrad).at[:, ghost_rows].add(ghost_cgrad)
        feature_total = feature_total.at[own_rows].add(own_fgrad).at[ghost_rows].add(ghost_fgrad)
        return ((coord_total, feature_total), energy)
    start_totals = (jnp.zeros(positions.shape, jnp.float32), jnp.zeros(atom_features.shape, jnp.float32))
    (coord_total, feature_total), energies = lax.scan(per_device, start_totals, jnp.arange(devices, dtype=jnp.int32))
    return (energies.reshape(-1), -coord_total, feature_total)
```

```python
import functools
import math

import jax
import jax.numpy as jnp
from jax import lax
from jax.experimental import pallas as pl
from jax.experimental.pallas import tpu as pltpu
from jax.sharding import PartitionSpec as P

SIDE = 4
REACH = 3
SPACING = 2.15
CUT = 6.0
ENV_NORM = 0.125
ATOMS = 64
SLOTS = 128
GHOST = 48
WIDTH = 256
CHANNELS = 64
OUT_WIDTH = 128
BASIS = 8
LIST = 1024
HEAD = 896
BASIS_AT = 1000
CENTER_AT = 1008
GROUP = 8
MESSAGE = 64

f32 = jnp.float32
bf16 = jnp.bfloat16
i32 = jnp.int32

DIRECTIONS = [
    (tx, ty, tz)
    for tx in (-1, 0, 1)
    for ty in (-1, 0, 1)
    for tz in (-1, 0, 1)
    if (tx, ty, tz) != (0, 0, 0)
]
CELLS = [9 * (tx + 1) + 3 * (ty + 1) + tz + 1 for tx, ty, tz in DIRECTIONS]
SIZES = [math.prod(REACH if t else SIDE for t in d) for d in DIRECTIONS]
STARTS = [ATOMS + sum(SIZES[:i]) for i in range(26)]
assert STARTS[-1] + SIZES[-1] == BASIS_AT


def nn(a, b):
    return jnp.dot(a, b, preferred_element_type=f32)


def nt(a, b):
    return lax.dot_general(a, b, (((1,), (1,)), ((), ())), preferred_element_type=f32)


def lanes_of(shape):
    return lax.broadcasted_iota(i32, shape, len(shape) - 1)


def rows_of(shape):
    return lax.broadcasted_iota(i32, shape, 0)


def column(row, size):
    shape = (size, size)
    on = rows_of(shape) == lanes_of(shape)
    return jnp.sum(jnp.where(on, jnp.broadcast_to(row, shape), 0.0), axis=1, keepdims=True)


def row(col, size):
    shape = (size, size)
    on = rows_of(shape) == lanes_of(shape)
    return jnp.sum(jnp.where(on, jnp.broadcast_to(col, shape), 0.0), axis=0, keepdims=True)


def pieces(value):
    high = value.astype(bf16).astype(f32)
    rest = value - high
    middle = rest.astype(bf16).astype(f32)
    low = (rest - middle).astype(bf16).astype(f32)
    return high, middle, low


def sigmoid(x):
    return 0.5 * jnp.tanh(0.5 * x) + 0.5


def pack_kernel(features, positions, lists, w_center, w_neighbor, message, proj, center, square, held):
    rounded = features[...].astype(bf16)
    own = nn(rounded, w_neighbor[...]).astype(bf16)
    proj[...] = own
    center[...] = nn(rounded, w_center[...]).astype(bf16)
    square[...] = jnp.zeros((128, 128), f32)
    square[0:3, 0:ATOMS] = positions[...]
    high, middle, low = pieces(square[0:8, :])
    parts = jnp.concatenate([high, middle, low, jnp.zeros((8, 128), f32)], axis=0).astype(bf16)
    held[0:ATOMS, :] = own
    held[ATOMS:128, :] = jnp.zeros((128 - ATOMS, WIDTH), bf16)
    square[0:27, 0:GHOST] = lists[...].astype(f32)
    by_entry = square[...].T
    wide = lanes_of((128, 128)).astype(f32)
    for i, cell in enumerate(CELLS):
        chosen = jnp.where(by_entry[:, cell : cell + 1] == wide, 1.0, 0.0).astype(bf16)
        message[i, 0:GHOST, :] = nn(chosen[0:GHOST], held[...]).astype(bf16)
        moved = nt(parts, chosen)
        message[i, GHOST:MESSAGE, :] = jnp.concatenate([moved[0:16], moved[16:32]], axis=1).astype(bf16)


def pack(features, positions, lists, w_center, w_neighbor):
    return pl.pallas_call(
        pack_kernel,
        out_shape=(
            jax.ShapeDtypeStruct((26, MESSAGE, WIDTH), bf16),
            jax.ShapeDtypeStruct((ATOMS, WIDTH), bf16),
            jax.ShapeDtypeStruct((ATOMS, WIDTH), bf16),
        ),
        in_specs=[pl.BlockSpec(memory_space=pltpu.VMEM)] * 5,
        out_specs=(pl.BlockSpec(memory_space=pltpu.VMEM),) * 3,
        scratch_shapes=[pltpu.VMEM((128, 128), f32), pltpu.VMEM((128, WIDTH), bf16)],
        name="pack",
    )(features, positions, lists, w_center, w_neighbor)


def exchange_kernel(sizes, sign, source, target, send_sem, recv_sem):
    axes = ("gx", "gy", "gz")
    here = [lax.axis_index(a) for a in axes]

    def place(direction):
        return tuple(
            lax.rem(h + (sign * t + n), n) for h, t, n in zip(here, direction, sizes)
        )

    barrier = pltpu.get_barrier_semaphore()
    for d in DIRECTIONS:
        pl.semaphore_signal(barrier, inc=1, device_id=place(d), device_id_type=pl.DeviceIdType.MESH)
    pl.semaphore_wait(barrier, 26)
    copies = []
    for i, d in enumerate(DIRECTIONS):
        copy = pltpu.make_async_remote_copy(
            src_ref=source.at[i],
            dst_ref=target.at[i],
            send_sem=send_sem.at[i],
            recv_sem=recv_sem.at[i],
            device_id=place(d),
            device_id_type=pl.DeviceIdType.MESH,
        )
        copy.start()
        copies.append(copy)
    for copy in copies:
        copy.wait()


def exchange(message, sizes, sign):
    return pl.pallas_call(
        functools.partial(exchange_kernel, sizes, sign),
        out_shape=jax.ShapeDtypeStruct(message.shape, message.dtype),
        in_specs=[pl.BlockSpec(memory_space=pl.ANY)],
        out_specs=pl.BlockSpec(memory_space=pl.ANY),
        scratch_shapes=[pltpu.SemaphoreType.DMA((26,)), pltpu.SemaphoreType.DMA((26,))],
        compiler_params=pltpu.CompilerParams(
            collective_id=0 if sign > 0 else 1, has_side_effects=True
        ),
        name="exchange_out" if sign > 0 else "exchange_back",
    )(message)


R_INDEX, R_ENV, R_SCALED, R_SCALE, R_SLOPE, R_U, R_INV, R_Y, R_BESS, R_BESS_D = 0, 1, 2, 3, 4, 5, 8, 9, 17, 25
R_COUNT = 33


def geometry(index, rx, ry, rz, live, scale):
    squared = rx * rx + ry * ry + rz * rz
    distance = jnp.sqrt(squared)
    inverse = 1.0 / distance
    ux, uy, uz = rx * inverse, ry * inverse, rz * inverse
    x = distance * (1.0 / CUT)
    x2 = x * x
    x5 = x2 * x2 * x
    x6 = x5 * x
    inside = jnp.where(x < 1.0, live, 0.0)
    env = inside * (1.0 + x6 * (-28.0 + x * (48.0 - 21.0 * x)))
    slope = inside * (x5 * (-168.0 + x * (336.0 - 168.0 * x))) * (1.0 / CUT)
    s3, s5, s15 = math.sqrt(3.0), math.sqrt(5.0), math.sqrt(15.0)
    ys = [
        s3 * ux,
        s3 * uy,
        s3 * uz,
        s15 * ux * uy,
        s15 * uy * uz,
        0.5 * s5 * (3.0 * uz * uz - 1.0),
        s15 * ux * uz,
        0.5 * s15 * (ux * ux - uy * uy),
    ]
    theta = distance * (math.pi / CUT)
    sin1, cos1 = jnp.sin(theta), jnp.cos(theta)
    sines, cosines = [jnp.zeros_like(sin1), sin1], [jnp.ones_like(cos1), cos1]
    for _ in range(BASIS - 1):
        sines.append(2.0 * cos1 * sines[-1] - sines[-2])
        cosines.append(2.0 * cos1 * cosines[-1] - cosines[-2])
    norm = math.sqrt(2.0 / CUT)
    bess, bess_d = [], []
    for n in range(1, BASIS + 1):
        value = norm * sines[n] * inverse
        bess.append(value)
        bess_d.append((norm * n * math.pi / CUT * cosines[n] - value) * inverse)
    return [index, env, env * scale, scale, slope, ux, uy, uz, inverse] + ys + bess + bess_d


def edge_blocks(
    per_atom,
    slots,
    table,
    onehot,
    head_proj,
    tail_proj,
    w_env,
    w_latent,
    w_out,
    w_basis,
    env_t,
    latent_t,
    out_t,
    final_col,
    acc,
    acc_tail,
    energy,
):
    width = GROUP * per_atom
    lane = lanes_of((GROUP, 128))

    def chunks_of(q):
        atoms = [slots[q, pl.ds(j, GROUP, stride=GROUP), :] for j in range(GROUP)]
        if per_atom == SLOTS:
            return atoms
        out = []
        for g in (0, 4):
            a0 = atoms[g]
            a1 = pltpu.roll(atoms[g + 1], 96, 1)
            a2 = pltpu.roll(atoms[g + 2], 64, 1)
            a3 = pltpu.roll(atoms[g + 3], 32, 1)
            out += [
                jnp.where(lane < 96, a0, a1),
                jnp.where(lane < 64, a1, a2),
                jnp.where(lane < 32, a2, a3),
            ]
        return out

    packed = [jnp.concatenate(chunks_of(q), axis=1) for q in range(6)]
    for q, value in enumerate(geometry(*packed)):
        for k in range(width // 128):
            table[k, q * GROUP : (q + 1) * GROUP, :] = value[:, 128 * k : 128 * k + 128]

    acc[...] = jnp.zeros(acc.shape, f32)

    wide = (GROUP, width)
    first_lane = rows_of(wide) * per_atom
    mask = (lanes_of(wide) >= first_lane) & (lanes_of(wide) < first_lane + per_atom)
    maskf = jnp.where(mask, 1.0, 0.0).astype(f32)

    deg = rows_of((3 * CHANNELS, 80)) // CHANNELS
    comp = lanes_of((3 * CHANNELS, 80)) // GROUP
    allowed = (
        ((deg == 0) & (comp == 0))
        | ((deg == 1) & (comp >= 1) & (comp <= 3))
        | ((deg == 2) & (comp >= 4) & (comp <= 8))
    )

    def block(b, carry):
        def value(q):
            parts = [table[k, pl.ds(q * GROUP + b, 1), :] for k in range(width // 128)]
            return jnp.concatenate(parts, axis=1)

        def eight(q):
            place = pl.ds(q * GROUP + b, GROUP, stride=GROUP)
            return jnp.concatenate([table[k, place, :] for k in range(width // 128)], axis=1)

        index = value(R_INDEX).astype(i32)
        env = value(R_ENV)
        bess = eight(R_BESS)
        tile = (16, width)
        apart = (jnp.broadcast_to(index, tile) - rows_of(tile)).astype(jnp.int16)
        for h in range(BASIS_AT // 16):
            onehot[16 * h : 16 * h + 16, 0:width] = jnp.where(
                apart == jnp.int16(16 * h), jnp.ones(tile, bf16), jnp.zeros(tile, bf16)
            )
        last = jnp.where(index == rows_of(wide) + (BASIS_AT - 8), 1.0, 0.0)
        onehot[BASIS_AT - 8 : BASIS_AT + 8, 0:width] = jnp.concatenate([last, bess], axis=0).astype(bf16)
        onehot[CENTER_AT:LIST, 0:width] = jnp.concatenate(
            [maskf, jnp.zeros(wide, f32)], axis=0
        ).astype(bf16)
        hot = onehot[:, 0:width]

        pre = nn(jnp.concatenate([head_proj[...], tail_proj[b]], axis=1), hot)
        sig = sigmoid(pre)
        act = pre * sig
        act_d = sig + act * (1.0 - sig)
        latent = env * act
        latent_h = latent.astype(bf16)
        weights = nn(env_t[...], latent_h)
        weights_h = weights.astype(bf16)
        ys = eight(R_Y)
        harm = jnp.concatenate(
            [maskf]
            + [maskf * ys[m : m + 1] for m in range(8)]
            + [jnp.zeros(wide, f32)],
            axis=0,
        ).astype(bf16)
        around = jnp.where(allowed, ENV_NORM * nt(weights_h, harm), 0.0)
        around_h = around.astype(bf16)
        tensor = nn(around_h, harm)
        scalars_h = (weights * tensor).astype(bf16)
        mixed = nn(latent_t[...], jnp.concatenate([latent_h, scalars_h], axis=0))
        sig = sigmoid(mixed)
        update = mixed * sig
        update_d = sig + update * (1.0 - sig)
        refined_h = (latent + env * update).astype(bf16)
        hidden = nn(out_t[...], refined_h)
        sig = sigmoid(hidden)
        hidden_act = hidden * sig
        final = final_col[:, 0:1]
        per_edge = jnp.sum(hidden_act * final, axis=0, keepdims=True)
        energy[pl.ds(pl.multiple_of(b * GROUP, GROUP), GROUP), :] = jnp.broadcast_to(
            jnp.sum(maskf * (env * per_edge), axis=1, keepdims=True), (GROUP, 128)
        )

        scaled = value(R_SCALED)
        d_hidden = ((sig + hidden_act * (1.0 - sig)) * final * scaled).astype(bf16)
        d_refined = nn(w_out[...], d_hidden)
        d_env = value(R_SCALE) * per_edge
        d_env += jnp.sum(d_refined * update, axis=0, keepdims=True)
        d_mixed = (env * d_refined * update_d).astype(bf16)
        d_both = nn(w_latent[...], d_mixed)
        d_scalars = d_both[WIDTH:]
        d_tensor_h = (d_scalars * weights).astype(bf16)
        d_around = jnp.where(allowed, ENV_NORM * nt(d_tensor_h, harm), 0.0)
        d_weights = d_scalars * tensor + nn(d_around.astype(bf16), harm)
        d_latent = d_refined + d_both[0:WIDTH] + nn(w_env[...], d_weights.astype(bf16))
        d_env += jnp.sum(d_latent * act, axis=0, keepdims=True)
        d_pre = (env * d_latent * act_d).astype(bf16)
        d_bess = nn(w_basis[...], d_pre)
        both = jnp.concatenate([around.T, d_around.T], axis=1).astype(bf16)
        d_harm = nn(both, jnp.concatenate([d_tensor_h, weights_h], axis=0))
        dy = [
            jnp.sum(maskf * d_harm[m * GROUP : (m + 1) * GROUP], axis=0, keepdims=True)
            for m in range(1, 9)
        ]

        ux, uy, uz, inverse = (value(q) for q in (R_U, R_U + 1, R_U + 2, R_INV))
        d_dist = d_env * value(R_SLOPE) + jnp.sum(d_bess * eight(R_BESS_D), axis=0, keepdims=True)
        s3, s5, s15 = math.sqrt(3.0), math.sqrt(5.0), math.sqrt(15.0)
        gx = s3 * dy[0] + s15 * (uy * dy[3] + uz * dy[6] + ux * dy[7])
        gy = s3 * dy[1] + s15 * (ux * dy[3] + uz * dy[4] - uy * dy[7])
        gz = s3 * dy[2] + s15 * (uy * dy[4] + ux * dy[6]) + 3.0 * s5 * uz * dy[5]
        along = d_dist - inverse * (gx * ux + gy * uy + gz * uz)
        d_rel = [inverse * g + along * u for g, u in ((gx, ux), (gy, uy), (gz, uz))]
        place = rows_of(wide)
        moved = jnp.where(place == 0, d_rel[0], 0.0)
        moved = jnp.where(place == 1, d_rel[1], moved)
        moved = jnp.where(place == 2, d_rel[2], moved)
        high = moved.astype(bf16).astype(f32)
        moved_h = jnp.concatenate([high, moved - high], axis=0).astype(bf16)
        spread = nt(jnp.concatenate([d_pre, moved_h], axis=0), hot)
        acc[...] += spread[:, 0:HEAD]
        acc_tail[b] = spread[:, HEAD:]
        return carry

    lax.fori_loop(0, ATOMS // GROUP, block, 0)


def edge_kernel(
    received,
    proj,
    center,
    positions,
    species,
    neighbor,
    live_in,
    kind_scale,
    kind_shift,
    w_basis,
    w_env,
    w_latent,
    w_out,
    w_final,
    energy_out,
    back,
    own_proj_grad,
    center_grad,
    own_pos_grad,
    rows,
    tail_rows,
    coords,
    head_proj,
    tail_proj,
    env_t,
    latent_t,
    out_t,
    final_col,
    slots,
    table,
    onehot,
    acc,
    acc_tail,
    energy,
):
    rows[0:ATOMS, :] = proj[...].astype(f32)
    for i in range(26):
        rows[STARTS[i] : STARTS[i] + SIZES[i], :] = received[i, 0:GHOST, :].astype(f32)[0 : SIZES[i]]
    rows[BASIS_AT:CENTER_AT, :] = w_basis[...].astype(f32)
    rows[CENTER_AT:LIST, :] = jnp.zeros((LIST - CENTER_AT, WIDTH), f32)
    for k in range(HEAD // 128):
        head_proj[:, 128 * k : 128 * k + 128] = rows[128 * k : 128 * k + 128, :].T.astype(bf16)
    for b in range(ATOMS // GROUP):
        rows[CENTER_AT : CENTER_AT + GROUP, :] = center[...].astype(f32)[GROUP * b : GROUP * b + GROUP]
        tail_proj[b] = rows[HEAD:LIST, :].T.astype(bf16)

    lane = lanes_of((8, 128))
    coords[...] = jnp.zeros(coords.shape, f32)
    coords[0:3, 0:ATOMS] = positions[...]
    filled = [coords[0:8, 128 * k : 128 * k + 128] for k in range(8)]
    which = rows_of((8, 128))
    for i, d in enumerate(DIRECTIONS):
        block = received[i, GHOST:MESSAGE, :].astype(f32)
        value = block[0:8, 0:128] + block[8:16, 0:128] + block[0:8, 128:256]
        step = [t * SIDE * SPACING for t in d]
        shift = jnp.where(which == 0, step[0], jnp.where(which == 1, step[1], step[2]))
        value = value - shift
        k, at = divmod(STARTS[i], 128)
        end = at + SIZES[i]
        value = pltpu.roll(value, at, 1) if at else value
        filled[k] = jnp.where((lane >= at) & (lane < end), value, filled[k])
        if end > 128:
            filled[k + 1] = jnp.where(lane < end - 128, value, filled[k + 1])

    env_t[...] = w_env[...].astype(f32).T.astype(bf16)
    latent_t[...] = w_latent[...].astype(f32).T.astype(bf16)
    out_t[...] = w_out[...].astype(f32).T.astype(bf16)
    final_col[...] = jnp.broadcast_to(column(w_final[...], OUT_WIDTH), (OUT_WIDTH, 128))

    kinds = species[...]
    scale_row = jnp.where(
        kinds == 0,
        kind_scale[0],
        jnp.where(kinds == 1, kind_scale[1], jnp.where(kinds == 2, kind_scale[2], kind_scale[3])),
    )
    shift_row = jnp.where(
        kinds == 0,
        kind_shift[0],
        jnp.where(kinds == 1, kind_shift[1], jnp.where(kinds == 2, kind_shift[2], kind_shift[3])),
    )

    full = (ATOMS, SLOTS)
    local = neighbor[...]
    ghost = local - ATOMS
    cell = jnp.where(ghost < 0, 13, (ghost * 1366) >> 16)
    jump = jnp.zeros((8, 128), i32)
    for i, c in enumerate(CELLS):
        jump = jnp.where(lane == c, STARTS[i] - ATOMS - GHOST * c, jump)
    jump = jnp.concatenate([jump] * 8, axis=0)
    index = local + jnp.take_along_axis(jump, cell, axis=1, mode="promise_in_bounds")
    low, page = index & 127, index >> 7
    rel = []
    for a in range(3):
        found = jnp.zeros(full, f32)
        for k in range(8):
            source = jnp.broadcast_to(filled[k][a : a + 1, :], full)
            taken = jnp.take_along_axis(source, low, axis=1, mode="promise_in_bounds")
            found = jnp.where(page == k, taken, found)
        rel.append(found - column(positions[a : a + 1, :], ATOMS))
    distance = jnp.sqrt(rel[0] * rel[0] + rel[1] * rel[1] + rel[2] * rel[2])
    live = jnp.where(distance * (1.0 / CUT) < 1.0, live_in[...], 0)

    before = jnp.where(rows_of((SLOTS, SLOTS)) < lanes_of((SLOTS, SLOTS)), 1.0, 0.0).astype(bf16)
    gap = nn((1 - live).astype(f32).astype(bf16), before).astype(i32)
    most = jnp.max(jnp.sum(live.astype(f32), axis=1, keepdims=True))
    values = [index] + rel
    for step in range(7):
        by = 1 << step
        moves = jnp.where((gap & by) != 0, live, 0)
        come = pltpu.roll(moves, SLOTS - by, 1) != 0
        values = [jnp.where(come, pltpu.roll(v, SLOTS - by, 1), v) for v in values]
        gap = jnp.where(come, pltpu.roll(gap, SLOTS - by, 1), gap)
        live = jnp.where(come, 1, live - moves)
    kept = live != 0
    slots[0] = jnp.where(kept, values[0], LIST - 1).astype(f32)
    slots[1] = jnp.where(kept, values[1], 0.5 * CUT)
    slots[2] = jnp.where(kept, values[2], 0.0)
    slots[3] = jnp.where(kept, values[3], 0.0)
    slots[4] = live.astype(f32)
    slots[5] = jnp.broadcast_to(column(scale_row, ATOMS), full)

    shared = (
        slots,
        table,
        onehot,
        head_proj,
        tail_proj,
        w_env,
        w_latent,
        w_out,
        w_basis,
        env_t,
        latent_t,
        out_t,
        final_col,
        acc,
        acc_tail,
        energy,
    )

    @pl.when(most <= 96.0)
    def _():
        edge_blocks(96, *shared)

    @pl.when(most > 96.0)
    def _():
        edge_blocks(SLOTS, *shared)

    energy_out[...] = scale_row * row(energy[:, 0:1], ATOMS) + shift_row

    tail = acc_tail[0]
    for b in range(1, ATOMS // GROUP):
        tail = tail + acc_tail[b]
    for k in range(HEAD // 128):
        rows[128 * k : 128 * k + 128, :] = acc[0:WIDTH, 128 * k : 128 * k + 128].T
    rows[HEAD:LIST, :] = tail[0:WIDTH].T
    place = CENTER_AT - HEAD
    pulled = jnp.zeros((8, 128), f32)
    for b in range(ATOMS // GROUP):
        tail_rows[...] = acc_tail[b][0:WIDTH].T
        center_grad[GROUP * b : GROUP * b + GROUP, :] = tail_rows[place : place + GROUP, :]
        value = acc_tail[b][WIDTH : WIDTH + 8] + acc_tail[b][WIDTH + 8 : WIDTH + 16]
        value = pltpu.roll(value, (GROUP * b - place) % 128, 1)
        pulled = jnp.where((lane >= GROUP * b) & (lane < GROUP * b + GROUP), value, pulled)
    coord_grad = [
        acc[WIDTH : WIDTH + 8, 128 * k : 128 * k + 128] + acc[WIDTH + 8 : WIDTH + 16, 128 * k : 128 * k + 128]
        for k in range(HEAD // 128)
    ]
    coord_grad.append(tail[WIDTH : WIDTH + 8] + tail[WIDTH + 8 : WIDTH + 16])
    own_proj_grad[...] = rows[0:ATOMS, :]
    own_pos_grad[...] = jnp.where(lane < ATOMS, coord_grad[0] - pulled, 0.0)
    entry = rows_of((GHOST, WIDTH))
    for i in range(26):
        value = rows[STARTS[i] : STARTS[i] + GHOST, :] if STARTS[i] + GHOST <= LIST else None
        if value is None:
            tail_rows[0:GHOST, :] = jnp.zeros((GHOST, WIDTH), f32)
            tail_rows[0 : SIZES[i], :] = rows[STARTS[i] : STARTS[i] + SIZES[i], :]
            value = tail_rows[0:GHOST, :]
        elif SIZES[i] < GHOST:
            value = jnp.where(entry < SIZES[i], value, 0.0)
        back[i, 0:GHOST, :] = value.astype(bf16)
        k, at = divmod(STARTS[i], 128)
        moved = coord_grad[k]
        if at:
            moved = pltpu.roll(moved, 128 - at, 1)
        if at + SIZES[i] > 128:
            moved = jnp.where(lane < 128 - at, moved, pltpu.roll(coord_grad[k + 1], 128 - at, 1))
        moved = jnp.where(lane < SIZES[i], moved, 0.0)
        high, middle, lowest = pieces(moved)
        back[i, GHOST:MESSAGE, :] = jnp.concatenate(
            [
                jnp.concatenate([high, middle], axis=0),
                jnp.concatenate([lowest, jnp.zeros((8, 128), f32)], axis=0),
            ],
            axis=1,
        ).astype(bf16)


def edges(received, proj, center, positions, species, neighbor, live, scale, shift, *weights):
    vmem = pl.BlockSpec(memory_space=pltpu.VMEM)
    smem = pl.BlockSpec(memory_space=pltpu.SMEM)
    return pl.pallas_call(
        edge_kernel,
        out_shape=(
            jax.ShapeDtypeStruct((1, ATOMS), f32),
            jax.ShapeDtypeStruct((26, MESSAGE, WIDTH), bf16),
            jax.ShapeDtypeStruct((ATOMS, WIDTH), f32),
            jax.ShapeDtypeStruct((ATOMS, WIDTH), f32),
            jax.ShapeDtypeStruct((8, 128), f32),
        ),
        in_specs=[vmem] * 7 + [smem] * 2 + [vmem] * 5,
        out_specs=(vmem,) * 5,
        scratch_shapes=[
            pltpu.VMEM((LIST, WIDTH), f32),
            pltpu.VMEM((128, WIDTH), f32),
            pltpu.VMEM((8, LIST), f32),
            pltpu.VMEM((WIDTH, HEAD), bf16),
            pltpu.VMEM((8, WIDTH, 128), bf16),
            pltpu.VMEM((3 * CHANNELS, WIDTH), bf16),
            pltpu.VMEM((WIDTH, WIDTH + 3 * CHANNELS), bf16),
            pltpu.VMEM((OUT_WIDTH, WIDTH), bf16),
            pltpu.VMEM((OUT_WIDTH, 128), f32),
            pltpu.VMEM((6, ATOMS, SLOTS), f32),
            pltpu.VMEM((8, R_COUNT * GROUP, 128), f32),
            pltpu.VMEM((LIST, GROUP * SLOTS), bf16),
            pltpu.VMEM((WIDTH + 16, HEAD), f32),
            pltpu.VMEM((8, WIDTH + 16, 128), f32),
            pltpu.VMEM((ATOMS, 128), f32),
        ],
        compiler_params=pltpu.CompilerParams(vmem_limit_bytes=56 * 1024 * 1024),
        name="edges",
    )(received, proj, center, positions, species, neighbor, live, scale, shift, *weights)


def unpack_kernel(
    returned, own_proj_grad, center_grad, own_pos_grad, lists, w_center, w_neighbor, forces, feature_grad, padded
):
    padded[...] = jnp.full((32, 128), -1, i32)
    padded[0:27, 0:GHOST] = lists[...]
    proj_grad = own_proj_grad[...]
    pos_grad = jnp.zeros((32, ATOMS), f32)
    atom = rows_of((ATOMS, GHOST))
    for i, cell in enumerate(CELLS):
        chosen = jnp.where(padded[cell : cell + 1, 0:GHOST] == atom, 1.0, 0.0).astype(bf16)
        proj_grad = proj_grad + nn(chosen, returned[i, 0:GHOST, :])
        block = returned[i, GHOST:MESSAGE, :]
        parts = jnp.concatenate([block[:, 0:GHOST], block[:, 128 : 128 + GHOST]], axis=0)
        pos_grad = pos_grad + nt(parts, chosen)
    feature_grad[...] = nt(proj_grad.astype(bf16), w_neighbor[...]) + nt(
        center_grad[...].astype(bf16), w_center[...]
    )
    total = own_pos_grad[:, 0:ATOMS] + pos_grad[0:8] + pos_grad[8:16] + pos_grad[16:24]
    forces[...] = -total[0:3]


def unpack(*args):
    vmem = pl.BlockSpec(memory_space=pltpu.VMEM)
    return pl.pallas_call(
        unpack_kernel,
        out_shape=(
            jax.ShapeDtypeStruct((3, ATOMS), f32),
            jax.ShapeDtypeStruct((ATOMS, WIDTH), f32),
        ),
        in_specs=[vmem] * 7,
        out_specs=(vmem,) * 2,
        scratch_shapes=[pltpu.VMEM((32, 128), i32)],
        name="unpack",
    )(*args)


def solution(mesh):
    sizes = tuple(mesh.shape[a] for a in ("gx", "gy", "gz"))

    def local(
        positions,
        atom_features,
        species,
        edge_neighbor,
        edge_live,
        send_list,
        species_scale,
        species_shift,
        w_center,
        w_neighbor,
        w_basis,
        w_env,
        w_latent,
        w_out,
        w_final,
    ):
        message, proj, center = pack(atom_features, positions, send_list, w_center, w_neighbor)
        received = exchange(message, sizes, 1)
        energy, back, own_proj_grad, center_grad, own_pos_grad = edges(
            received,
            proj,
            center,
            positions,
            species.reshape(1, ATOMS),
            edge_neighbor,
            edge_live,
            species_scale,
            species_shift,
            w_basis,
            w_env,
            w_latent,
            w_out,
            w_final.reshape(1, OUT_WIDTH),
        )
        returned = exchange(back, sizes, -1)
        forces, feature_grad = unpack(
            returned, own_proj_grad, center_grad, own_pos_grad, send_list, w_center, w_neighbor
        )
        return energy.reshape(ATOMS), forces, feature_grad

    split = ("gx", "gy", "gz")
    return jax.shard_map(
        local,
        mesh=mesh,
        in_specs=(P(None, split), P(split, None), P(split), P(split, None), P(split, None), P(split, None))
        + (P(),) * 9,
        out_specs=(P(split), P(None, split), P(split, None)),
        check_vma=False,
    )
```

```python
import functools
import math

import jax
import jax.numpy as jnp
from jax import lax
from jax.experimental import pallas as pl
from jax.experimental.pallas import tpu as pltpu
from jax.sharding import PartitionSpec as P

SIDE = 4
REACH = 3
SPACING = 2.15
CUT = 6.0
ENV_NORM = 0.125
ATOMS = 64
SLOTS = 128
GHOST = 48
WIDTH = 256
CHANNELS = 64
OUT_WIDTH = 128
BASIS = 8
LIST = 1024
HEAD = 896
BASIS_AT = 1000
CENTER_AT = 1008
GROUP = 8

f32 = jnp.float32
bf16 = jnp.bfloat16
i32 = jnp.int32

FACES = [(-1, 0, 0), (1, 0, 0), (0, -1, 0), (0, 1, 0), (0, 0, -1), (0, 0, 1)]
X_FACE, Y_FACE, Z_FACE = 0, 2, 4
Y_CELLS = [(0, -1, 0), (0, 1, 0)]
Z_CELLS = [(0, ty, tz) for tz in (-1, 1) for ty in (0, -1, 1)]
X_CELLS = [
    (tx,) + behind for tx in (-1, 1) for behind in [(0, 0)] + [c[1:] for c in Y_CELLS + Z_CELLS]
]
DIRECTIONS = Y_CELLS + Z_CELLS + X_CELLS
Z_AT, X_AT = (2, 5), (8, 17)
CELLS = [9 * (tx + 1) + 3 * (ty + 1) + tz + 1 for tx, ty, tz in DIRECTIONS]
SIZES = [math.prod(REACH if t else SIDE for t in d) for d in DIRECTIONS]
STARTS = [ATOMS + sum(SIZES[:i]) for i in range(26)]
assert STARTS[-1] + SIZES[-1] == BASIS_AT
FACE_CELLS = [9 * (tx + 1) + 3 * (ty + 1) + tz + 1 for tx, ty, tz in FACES]
LIST_ROW = 3
FACE_LIST = 4


def list_slot(direction):
    tx, ty, tz = direction
    return 3 * (tx + 1) + (tz + 1 if ty else 1)


def nn(a, b):
    return jnp.dot(a, b, preferred_element_type=f32)


def nt(a, b):
    return lax.dot_general(a, b, (((1,), (1,)), ((), ())), preferred_element_type=f32)


def lanes_of(shape):
    return lax.broadcasted_iota(i32, shape, len(shape) - 1)


def rows_of(shape):
    return lax.broadcasted_iota(i32, shape, 0)


def column(row, size):
    shape = (size, size)
    on = rows_of(shape) == lanes_of(shape)
    return jnp.sum(jnp.where(on, jnp.broadcast_to(row, shape), 0.0), axis=1, keepdims=True)


def row(col, size):
    shape = (size, size)
    on = rows_of(shape) == lanes_of(shape)
    return jnp.sum(jnp.where(on, jnp.broadcast_to(col, shape), 0.0), axis=0, keepdims=True)


def pieces(value):
    high = value.astype(bf16).astype(f32)
    rest = value - high
    middle = rest.astype(bf16).astype(f32)
    low = (rest - middle).astype(bf16).astype(f32)
    return high, middle, low


def sigmoid(x):
    return 0.5 * jnp.tanh(0.5 * x) + 0.5


def pack_kernel(
    features, positions, lists, w_center, w_neighbor, face_rows, face_small, proj, center, square, listed, held
):
    rounded = features[...].astype(bf16)
    own = nn(rounded, w_neighbor[...]).astype(bf16)
    proj[...] = own
    center[...] = nn(rounded, w_center[...]).astype(bf16)
    square[...] = jnp.zeros((128, 128), f32)
    square[0:3, 0:ATOMS] = positions[...]
    parts = jnp.concatenate(list(pieces(square[0:8, :])), axis=0)
    parts = jnp.concatenate([parts, jnp.zeros((8, 128), f32)], axis=0).astype(bf16)
    held[0:ATOMS, :] = own
    held[ATOMS:128, :] = jnp.zeros((128 - ATOMS, WIDTH), bf16)
    listed[...] = jnp.full((32, 128), -1.0, f32)
    listed[0:27, 0:GHOST] = lists[...].astype(f32)
    square[0:32, :] = listed[...]
    by_entry = square[...].T
    wide = lanes_of((128, 128)).astype(f32)
    which = rows_of((8, 128))
    for i, (face, cell) in enumerate(zip(FACES, FACE_CELLS)):
        chosen = jnp.where(by_entry[:, cell : cell + 1] == wide, 1.0, 0.0).astype(bf16)
        face_rows[i] = nn(chosen[0:GHOST], held[...]).astype(bf16)
        moved = nt(parts, chosen)
        small = moved[0:8] + moved[8:16] + moved[16:24]
        axis = [a for a in range(3) if face[a]][0]
        for d, c in zip(DIRECTIONS, CELLS):
            first = 1 if d[1] else 2 if d[2] else 0
            if first != axis or d[first] != face[first] or first == 0:
                continue
            r, half = divmod(list_slot(d), 2)
            entries = jnp.broadcast_to(listed[c : c + 1, :], (8, 128))
            if half:
                entries = pltpu.roll(entries, 64, 1)
            lane = lanes_of((8, 128))
            here = (which == LIST_ROW + r) & ((lane >= 64) if half else (lane < 64))
            small = jnp.where(here, entries, small)
        face_small[i] = small


def pack(features, positions, lists, w_center, w_neighbor):
    return pl.pallas_call(
        pack_kernel,
        out_shape=(
            jax.ShapeDtypeStruct((6, GHOST, WIDTH), bf16),
            jax.ShapeDtypeStruct((6, 8, 128), f32),
            jax.ShapeDtypeStruct((ATOMS, WIDTH), bf16),
            jax.ShapeDtypeStruct((ATOMS, WIDTH), bf16),
        ),
        in_specs=[pl.BlockSpec(memory_space=pltpu.VMEM)] * 5,
        out_specs=(pl.BlockSpec(memory_space=pltpu.VMEM),) * 4,
        scratch_shapes=[
            pltpu.VMEM((128, 128), f32),
            pltpu.VMEM((32, 128), f32),
            pltpu.VMEM((128, WIDTH), bf16),
        ],
        name="pack",
    )(features, positions, lists, w_center, w_neighbor)


STAGES = 14


def neighbours(sizes):
    axes = ("gx", "gy", "gz")
    here = [lax.axis_index(a) for a in axes]

    def place(axis, step):
        return tuple(
            lax.rem(h + (step + n), n) if a == axis else h
            for a, (h, n) in enumerate(zip(here, sizes))
        )

    barrier = pltpu.get_barrier_semaphore()
    for axis in range(3):
        for step in (-1, 1):
            pl.semaphore_signal(
                barrier, inc=1, device_id=place(axis, step), device_id_type=pl.DeviceIdType.MESH
            )
    pl.semaphore_wait(barrier, 6)
    return place


def sender(place, send_sem, recv_sem):
    count = [0]

    def send(pairs, axis, step):
        started = []
        for source, target in pairs:
            k = count[0]
            count[0] += 1
            copy = pltpu.make_async_remote_copy(
                src_ref=source,
                dst_ref=target,
                send_sem=send_sem.at[k],
                recv_sem=recv_sem.at[k],
                device_id=place(axis, step),
                device_id_type=pl.DeviceIdType.MESH,
            )
            copy.start()
            started.append(copy)
        return started

    return send


def arrived(*groups):
    for group in groups:
        for copy in group:
            copy.wait_recv()


def sent(*groups):
    for group in groups:
        for copy in group:
            copy.wait_send()


def out_kernel(sizes, face_rows, face_small, rows, small, send_sem, recv_sem):
    send = sender(neighbours(sizes), send_sem, recv_sem)
    own = [(face_rows, face_small), (rows, small)]

    def move(source, target, count, from_face, axis, step):
        origin = own[0] if from_face else own[1]
        return send(
            [(o.at[pl.ds(source, count)], g.at[pl.ds(target, count)]) for o, g in zip(origin, own[1])],
            axis,
            step,
        )

    steps = ((0, -1), (1, 1))
    y = [move(Y_FACE + k, k, 1, True, 1, t) for k, t in steps]
    z_own = [move(Z_FACE + k, Z_AT[k], 1, True, 2, t) for k, t in steps]
    x_own = [move(X_FACE + k, X_AT[k], 1, True, 0, t) for k, t in steps]
    arrived(*y)
    z_pair = [move(0, Z_AT[k] + 1, 2, False, 2, t) for k, t in steps]
    x_pair = [move(0, X_AT[k] + 1, 2, False, 0, t) for k, t in steps]
    x_rest = []
    for half in (0, 1):
        arrived(z_own[half], z_pair[half])
        x_rest += [
            move(Z_AT[half], X_AT[k] + Z_AT[half] + 1, 3, False, 0, t) for k, t in steps
        ]
    arrived(*x_own, *x_pair, *x_rest)
    sent(*y, *z_own, *x_own, *z_pair, *x_pair, *x_rest)


def back_kernel(
    sizes, rows, small, face_rows, face_small, from_x, from_x_small, from_z, from_z_small, total, total_small,
    send_sem, recv_sem
):
    send = sender(neighbours(sizes), send_sem, recv_sem)

    def move(source, target, axis, step):
        return send(list(zip(source, target)), axis, step)

    def at(refs, start, count):
        return [r.at[pl.ds(start, count)] for r in refs]

    given, faces = (rows, small), (face_rows, face_small)
    sums = (total, total_small)
    steps = ((0, -1), (1, 1))
    in_x = [(from_x.at[k], from_x_small.at[k]) for k in (0, 1)]
    in_z = [(from_z.at[k], from_z_small.at[k]) for k in (0, 1)]
    x_rest = [move(at(given, X_AT[k] + 3, 6), at(in_x[k], 2, 6), 0, -t) for k, t in steps]
    x_pair = [move(at(given, X_AT[k] + 1, 2), at(in_x[k], 0, 2), 0, -t) for k, t in steps]
    x_own = [move(at(given, X_AT[k], 1), at(faces, X_FACE + k, 1), 0, -t) for k, t in steps]
    arrived(*x_rest)
    for i in range(2, 8):
        total[i] = (
            rows[i].astype(f32) + from_x[0, i].astype(f32) + from_x[1, i].astype(f32)
        ).astype(bf16)
        total_small[i] = small[i] + from_x_small[0, i] + from_x_small[1, i]
    z_pair = [move(at(sums, Z_AT[k] + 1, 2), at(in_z[k], 0, 2), 2, -t) for k, t in steps]
    z_own = [move(at(sums, Z_AT[k], 1), at(faces, Z_FACE + k, 1), 2, -t) for k, t in steps]
    arrived(*x_pair, *z_pair)
    for i in range(2):
        total[i] = (
            rows[i].astype(f32)
            + from_x[0, i].astype(f32)
            + from_x[1, i].astype(f32)
            + from_z[0, i].astype(f32)
            + from_z[1, i].astype(f32)
        ).astype(bf16)
        total_small[i] = (
            small[i] + from_x_small[0, i] + from_x_small[1, i] + from_z_small[0, i] + from_z_small[1, i]
        )
    y = [move(at(sums, k, 1), at(faces, Y_FACE + k, 1), 1, -t) for k, t in steps]
    arrived(*x_own, *z_own, *y)
    sent(*x_rest, *x_pair, *x_own, *z_pair, *z_own, *y)


def exchange_out(face_rows, face_small, sizes):
    vmem = pl.BlockSpec(memory_space=pltpu.VMEM)
    return pl.pallas_call(
        functools.partial(out_kernel, sizes),
        out_shape=(
            jax.ShapeDtypeStruct((26, GHOST, WIDTH), bf16),
            jax.ShapeDtypeStruct((26, 8, 128), f32),
        ),
        in_specs=[vmem] * 2,
        out_specs=(vmem,) * 2,
        scratch_shapes=[pltpu.SemaphoreType.DMA((2 * STAGES,)), pltpu.SemaphoreType.DMA((2 * STAGES,))],
        compiler_params=pltpu.CompilerParams(collective_id=0, has_side_effects=True),
        name="exchange_out",
    )(face_rows, face_small)


def exchange_back(rows, small, sizes):
    vmem = pl.BlockSpec(memory_space=pltpu.VMEM)
    return pl.pallas_call(
        functools.partial(back_kernel, sizes),
        out_shape=(
            jax.ShapeDtypeStruct((6, GHOST, WIDTH), bf16),
            jax.ShapeDtypeStruct((6, 8, 128), f32),
        ),
        in_specs=[vmem] * 2,
        out_specs=(vmem,) * 2,
        scratch_shapes=[
            pltpu.VMEM((2, 8, GHOST, WIDTH), bf16),
            pltpu.VMEM((2, 8, 8, 128), f32),
            pltpu.VMEM((2, 2, GHOST, WIDTH), bf16),
            pltpu.VMEM((2, 2, 8, 128), f32),
            pltpu.VMEM((8, GHOST, WIDTH), bf16),
            pltpu.VMEM((8, 8, 128), f32),
            pltpu.SemaphoreType.DMA((2 * 12,)),
            pltpu.SemaphoreType.DMA((2 * 12,)),
        ],
        compiler_params=pltpu.CompilerParams(collective_id=1, has_side_effects=True),
        name="exchange_back",
    )(rows, small)


R_INDEX, R_ENV, R_SCALED, R_SCALE, R_SLOPE, R_U, R_INV, R_Y, R_BESS, R_BESS_D = 0, 1, 2, 3, 4, 5, 8, 9, 17, 25
R_COUNT = 33


def geometry(index, rx, ry, rz, live, scale):
    squared = rx * rx + ry * ry + rz * rz
    distance = jnp.sqrt(squared)
    inverse = 1.0 / distance
    ux, uy, uz = rx * inverse, ry * inverse, rz * inverse
    x = distance * (1.0 / CUT)
    x2 = x * x
    x5 = x2 * x2 * x
    x6 = x5 * x
    inside = jnp.where(x < 1.0, live, 0.0)
    env = inside * (1.0 + x6 * (-28.0 + x * (48.0 - 21.0 * x)))
    slope = inside * (x5 * (-168.0 + x * (336.0 - 168.0 * x))) * (1.0 / CUT)
    s3, s5, s15 = math.sqrt(3.0), math.sqrt(5.0), math.sqrt(15.0)
    ys = [
        s3 * ux,
        s3 * uy,
        s3 * uz,
        s15 * ux * uy,
        s15 * uy * uz,
        0.5 * s5 * (3.0 * uz * uz - 1.0),
        s15 * ux * uz,
        0.5 * s15 * (ux * ux - uy * uy),
    ]
    theta = distance * (math.pi / CUT)
    sin1, cos1 = jnp.sin(theta), jnp.cos(theta)
    sines, cosines = [jnp.zeros_like(sin1), sin1], [jnp.ones_like(cos1), cos1]
    for _ in range(BASIS - 1):
        sines.append(2.0 * cos1 * sines[-1] - sines[-2])
        cosines.append(2.0 * cos1 * cosines[-1] - cosines[-2])
    norm = math.sqrt(2.0 / CUT)
    bess, bess_d = [], []
    for n in range(1, BASIS + 1):
        value = norm * sines[n] * inverse
        bess.append(value)
        bess_d.append((norm * n * math.pi / CUT * cosines[n] - value) * inverse)
    return [index, env, env * scale, scale, slope, ux, uy, uz, inverse] + ys + bess + bess_d


def edge_blocks(
    per_atom,
    slots,
    table,
    onehot,
    head_proj,
    tail_proj,
    w_env,
    w_latent,
    w_out,
    w_basis,
    env_t,
    latent_t,
    out_t,
    final_col,
    acc,
    acc_tail,
    energy,
):
    width = GROUP * per_atom
    lane = lanes_of((GROUP, 128))

    def chunks_of(q):
        atoms = [slots[q, pl.ds(j, GROUP, stride=GROUP), :] for j in range(GROUP)]
        if per_atom == SLOTS:
            return atoms
        out = []
        for g in (0, 4):
            a0 = atoms[g]
            a1 = pltpu.roll(atoms[g + 1], 96, 1)
            a2 = pltpu.roll(atoms[g + 2], 64, 1)
            a3 = pltpu.roll(atoms[g + 3], 32, 1)
            out += [
                jnp.where(lane < 96, a0, a1),
                jnp.where(lane < 64, a1, a2),
                jnp.where(lane < 32, a2, a3),
            ]
        return out

    packed = [jnp.concatenate(chunks_of(q), axis=1) for q in range(6)]
    for q, value in enumerate(geometry(*packed)):
        for k in range(width // 128):
            table[k, q * GROUP : (q + 1) * GROUP, :] = value[:, 128 * k : 128 * k + 128]

    acc[...] = jnp.zeros(acc.shape, f32)

    wide = (GROUP, width)
    first_lane = rows_of(wide) * per_atom
    mask = (lanes_of(wide) >= first_lane) & (lanes_of(wide) < first_lane + per_atom)
    maskf = jnp.where(mask, 1.0, 0.0).astype(f32)

    deg = rows_of((3 * CHANNELS, 80)) // CHANNELS
    comp = lanes_of((3 * CHANNELS, 80)) // GROUP
    allowed = (
        ((deg == 0) & (comp == 0))
        | ((deg == 1) & (comp >= 1) & (comp <= 3))
        | ((deg == 2) & (comp >= 4) & (comp <= 8))
    )

    def block(b, carry):
        def value(q):
            parts = [table[k, pl.ds(q * GROUP + b, 1), :] for k in range(width // 128)]
            return jnp.concatenate(parts, axis=1)

        def eight(q):
            place = pl.ds(q * GROUP + b, GROUP, stride=GROUP)
            return jnp.concatenate([table[k, place, :] for k in range(width // 128)], axis=1)

        index = value(R_INDEX).astype(i32)
        env = value(R_ENV)
        bess = eight(R_BESS)
        tile = (16, width)
        apart = (jnp.broadcast_to(index, tile) - rows_of(tile)).astype(jnp.int16)
        for h in range(BASIS_AT // 16):
            onehot[16 * h : 16 * h + 16, 0:width] = jnp.where(
                apart == jnp.int16(16 * h), jnp.ones(tile, bf16), jnp.zeros(tile, bf16)
            )
        last = jnp.where(index == rows_of(wide) + (BASIS_AT - 8), 1.0, 0.0)
        onehot[BASIS_AT - 8 : BASIS_AT + 8, 0:width] = jnp.concatenate([last, bess], axis=0).astype(bf16)
        onehot[CENTER_AT:LIST, 0:width] = jnp.concatenate(
            [maskf, jnp.zeros(wide, f32)], axis=0
        ).astype(bf16)
        hot = onehot[:, 0:width]

        pre = nn(jnp.concatenate([head_proj[...], tail_proj[b]], axis=1), hot)
        sig = sigmoid(pre)
        act = pre * sig
        act_d = sig + act * (1.0 - sig)
        latent = env * act
        latent_h = latent.astype(bf16)
        weights = nn(env_t[...], latent_h)
        weights_h = weights.astype(bf16)
        ys = eight(R_Y)
        harm = jnp.concatenate(
            [maskf]
            + [maskf * ys[m : m + 1] for m in range(8)]
            + [jnp.zeros(wide, f32)],
            axis=0,
        ).astype(bf16)
        around = jnp.where(allowed, ENV_NORM * nt(weights_h, harm), 0.0)
        around_h = around.astype(bf16)
        tensor = nn(around_h, harm)
        scalars_h = (weights * tensor).astype(bf16)
        mixed = nn(latent_t[...], jnp.concatenate([latent_h, scalars_h], axis=0))
        sig = sigmoid(mixed)
        update = mixed * sig
        update_d = sig + update * (1.0 - sig)
        refined_h = (latent + env * update).astype(bf16)
        hidden = nn(out_t[...], refined_h)
        sig = sigmoid(hidden)
        hidden_act = hidden * sig
        final = final_col[:, 0:1]
        per_edge = jnp.sum(hidden_act * final, axis=0, keepdims=True)
        energy[pl.ds(pl.multiple_of(b * GROUP, GROUP), GROUP), :] = jnp.broadcast_to(
            jnp.sum(maskf * (env * per_edge), axis=1, keepdims=True), (GROUP, 128)
        )

        scaled = value(R_SCALED)
        d_hidden = ((sig + hidden_act * (1.0 - sig)) * final * scaled).astype(bf16)
        d_refined = nn(w_out[...], d_hidden)
        d_env = value(R_SCALE) * per_edge
        d_env += jnp.sum(d_refined * update, axis=0, keepdims=True)
        d_mixed = (env * d_refined * update_d).astype(bf16)
        d_both = nn(w_latent[...], d_mixed)
        d_scalars = d_both[WIDTH:]
        d_tensor_h = (d_scalars * weights).astype(bf16)
        d_around = jnp.where(allowed, ENV_NORM * nt(d_tensor_h, harm), 0.0)
        d_weights = d_scalars * tensor + nn(d_around.astype(bf16), harm)
        d_latent = d_refined + d_both[0:WIDTH] + nn(w_env[...], d_weights.astype(bf16))
        d_env += jnp.sum(d_latent * act, axis=0, keepdims=True)
        d_pre = (env * d_latent * act_d).astype(bf16)
        d_bess = nn(w_basis[...], d_pre)
        both = jnp.concatenate([around.T, d_around.T], axis=1).astype(bf16)
        d_harm = nn(both, jnp.concatenate([d_tensor_h, weights_h], axis=0))
        dy = [
            jnp.sum(maskf * d_harm[m * GROUP : (m + 1) * GROUP], axis=0, keepdims=True)
            for m in range(1, 9)
        ]

        ux, uy, uz, inverse = (value(q) for q in (R_U, R_U + 1, R_U + 2, R_INV))
        d_dist = d_env * value(R_SLOPE) + jnp.sum(d_bess * eight(R_BESS_D), axis=0, keepdims=True)
        s3, s5, s15 = math.sqrt(3.0), math.sqrt(5.0), math.sqrt(15.0)
        gx = s3 * dy[0] + s15 * (uy * dy[3] + uz * dy[6] + ux * dy[7])
        gy = s3 * dy[1] + s15 * (ux * dy[3] + uz * dy[4] - uy * dy[7])
        gz = s3 * dy[2] + s15 * (uy * dy[4] + ux * dy[6]) + 3.0 * s5 * uz * dy[5]
        along = d_dist - inverse * (gx * ux + gy * uy + gz * uz)
        d_rel = [inverse * g + along * u for g, u in ((gx, ux), (gy, uy), (gz, uz))]
        place = rows_of(wide)
        moved = jnp.where(place == 0, d_rel[0], 0.0)
        moved = jnp.where(place == 1, d_rel[1], moved)
        moved = jnp.where(place == 2, d_rel[2], moved)
        high = moved.astype(bf16).astype(f32)
        moved_h = jnp.concatenate([high, moved - high], axis=0).astype(bf16)
        spread = nt(jnp.concatenate([d_pre, moved_h], axis=0), hot)
        acc[...] += spread[:, 0:HEAD]
        acc_tail[b] = spread[:, HEAD:]
        return carry

    lax.fori_loop(0, ATOMS // GROUP, block, 0)


def edge_kernel(
    received,
    received_small,
    proj,
    center,
    positions,
    species,
    neighbor,
    live_in,
    kind_scale,
    kind_shift,
    w_basis,
    w_env,
    w_latent,
    w_out,
    w_final,
    energy_out,
    back,
    back_small,
    own_proj_grad,
    center_grad,
    own_pos_grad,
    rows,
    tail_rows,
    lists,
    faces,
    coords,
    head_proj,
    tail_proj,
    env_t,
    latent_t,
    out_t,
    final_col,
    slots,
    table,
    onehot,
    acc,
    acc_tail,
    energy,
):
    rows[0:ATOMS, :] = proj[...].astype(f32)
    lane = lanes_of((8, 128))
    lists[...] = jnp.full((128, 128), -1.0, f32)
    faces[...] = jnp.full((128, 128), -2.0, f32)
    corner = [i for i in range(26) if DIRECTIONS[i] not in FACES]
    for i in corner:
        r, half = divmod(list_slot(DIRECTIONS[i]), 2)
        entries = received_small[i, LIST_ROW + r : LIST_ROW + r + 1, :]
        lists[i : i + 1, :] = pltpu.roll(entries, 64, 1) if half else entries
        r = LIST_ROW + FACE_LIST // 2
        faces[i : i + 1, :] = jnp.where(lane[0:1] < GHOST, received_small[i, r : r + 1, :], -2.0)
    entry_col = lists[...].T
    face_col = faces[...].T
    chosen = {
        i: jnp.where(entry_col[:, i : i + 1] == faces[i : i + 1, :], 1.0, 0.0).astype(bf16) for i in corner
    }
    for i in range(26):
        if i in chosen:
            value = nn(chosen[i][0:GHOST, 0:GHOST], received[i])
        else:
            value = received[i].astype(f32)
        rows[STARTS[i] : STARTS[i] + SIZES[i], :] = value[0 : SIZES[i]]
    rows[BASIS_AT:CENTER_AT, :] = w_basis[...].astype(f32)
    rows[CENTER_AT:LIST, :] = jnp.zeros((LIST - CENTER_AT, WIDTH), f32)
    for k in range(HEAD // 128):
        head_proj[:, 128 * k : 128 * k + 128] = rows[128 * k : 128 * k + 128, :].T.astype(bf16)
    for b in range(ATOMS // GROUP):
        rows[CENTER_AT : CENTER_AT + GROUP, :] = center[...].astype(f32)[GROUP * b : GROUP * b + GROUP]
        tail_proj[b] = rows[HEAD:LIST, :].T.astype(bf16)

    coords[...] = jnp.zeros(coords.shape, f32)
    coords[0:3, 0:ATOMS] = positions[...]
    filled = [coords[0:8, 128 * k : 128 * k + 128] for k in range(8)]
    which = rows_of((8, 128))
    for i, d in enumerate(DIRECTIONS):
        value = received_small[i]
        if i in chosen:
            parts = jnp.concatenate(list(pieces(value)) + [jnp.zeros((8, 128), f32)], axis=0)
            parts = nt(parts.astype(bf16), chosen[i])
            value = parts[0:8] + parts[8:16] + parts[16:24]
        step = [t * SIDE * SPACING for t in d]
        shift = jnp.where(which == 0, step[0], jnp.where(which == 1, step[1], step[2]))
        value = value - shift
        k, at = divmod(STARTS[i], 128)
        end = at + SIZES[i]
        value = pltpu.roll(value, at, 1) if at else value
        filled[k] = jnp.where((lane >= at) & (lane < end), value, filled[k])
        if end > 128:
            filled[k + 1] = jnp.where(lane < end - 128, value, filled[k + 1])

    env_t[...] = w_env[...].astype(f32).T.astype(bf16)
    latent_t[...] = w_latent[...].astype(f32).T.astype(bf16)
    out_t[...] = w_out[...].astype(f32).T.astype(bf16)
    final_col[...] = jnp.broadcast_to(column(w_final[...], OUT_WIDTH), (OUT_WIDTH, 128))

    kinds = species[...]
    scale_row = jnp.where(
        kinds == 0,
        kind_scale[0],
        jnp.where(kinds == 1, kind_scale[1], jnp.where(kinds == 2, kind_scale[2], kind_scale[3])),
    )
    shift_row = jnp.where(
        kinds == 0,
        kind_shift[0],
        jnp.where(kinds == 1, kind_shift[1], jnp.where(kinds == 2, kind_shift[2], kind_shift[3])),
    )

    full = (ATOMS, SLOTS)
    local = neighbor[...]
    ghost = local - ATOMS
    cell = jnp.where(ghost < 0, 13, (ghost * 1366) >> 16)
    jump = jnp.zeros((8, 128), i32)
    for i, c in enumerate(CELLS):
        jump = jnp.where(lane == c, STARTS[i] - ATOMS - GHOST * c, jump)
    jump = jnp.concatenate([jump] * 8, axis=0)
    index = local + jnp.take_along_axis(jump, cell, axis=1, mode="promise_in_bounds")
    low, page = index & 127, index >> 7
    rel = []
    for a in range(3):
        found = jnp.zeros(full, f32)
        for k in range(8):
            source = jnp.broadcast_to(filled[k][a : a + 1, :], full)
            taken = jnp.take_along_axis(source, low, axis=1, mode="promise_in_bounds")
            found = jnp.where(page == k, taken, found)
        rel.append(found - column(positions[a : a + 1, :], ATOMS))
    distance = jnp.sqrt(rel[0] * rel[0] + rel[1] * rel[1] + rel[2] * rel[2])
    live = jnp.where(distance * (1.0 / CUT) < 1.0, live_in[...], 0)

    before = jnp.where(rows_of((SLOTS, SLOTS)) < lanes_of((SLOTS, SLOTS)), 1.0, 0.0).astype(bf16)
    gap = nn((1 - live).astype(f32).astype(bf16), before).astype(i32)
    most = jnp.max(jnp.sum(live.astype(f32), axis=1, keepdims=True))
    values = [index] + rel
    for step in range(7):
        by = 1 << step
        moves = jnp.where((gap & by) != 0, live, 0)
        come = pltpu.roll(moves, SLOTS - by, 1) != 0
        values = [jnp.where(come, pltpu.roll(v, SLOTS - by, 1), v) for v in values]
        gap = jnp.where(come, pltpu.roll(gap, SLOTS - by, 1), gap)
        live = jnp.where(come, 1, live - moves)
    kept = live != 0
    slots[0] = jnp.where(kept, values[0], LIST - 1).astype(f32)
    slots[1] = jnp.where(kept, values[1], 0.5 * CUT)
    slots[2] = jnp.where(kept, values[2], 0.0)
    slots[3] = jnp.where(kept, values[3], 0.0)
    slots[4] = live.astype(f32)
    slots[5] = jnp.broadcast_to(column(scale_row, ATOMS), full)

    shared = (
        slots,
        table,
        onehot,
        head_proj,
        tail_proj,
        w_env,
        w_latent,
        w_out,
        w_basis,
        env_t,
        latent_t,
        out_t,
        final_col,
        acc,
        acc_tail,
        energy,
    )

    @pl.when(most <= 96.0)
    def _():
        edge_blocks(96, *shared)

    @pl.when(most > 96.0)
    def _():
        edge_blocks(SLOTS, *shared)

    energy_out[...] = scale_row * row(energy[:, 0:1], ATOMS) + shift_row

    tail = acc_tail[0]
    for b in range(1, ATOMS // GROUP):
        tail = tail + acc_tail[b]
    for k in range(HEAD // 128):
        rows[128 * k : 128 * k + 128, :] = acc[0:WIDTH, 128 * k : 128 * k + 128].T
    rows[HEAD:LIST, :] = tail[0:WIDTH].T
    place = CENTER_AT - HEAD
    pulled = jnp.zeros((8, 128), f32)
    for b in range(ATOMS // GROUP):
        tail_rows[...] = acc_tail[b][0:WIDTH].T
        center_grad[GROUP * b : GROUP * b + GROUP, :] = tail_rows[place : place + GROUP, :]
        value = acc_tail[b][WIDTH : WIDTH + 8] + acc_tail[b][WIDTH + 8 : WIDTH + 16]
        value = pltpu.roll(value, (GROUP * b - place) % 128, 1)
        pulled = jnp.where((lane >= GROUP * b) & (lane < GROUP * b + GROUP), value, pulled)
    coord_grad = [
        acc[WIDTH : WIDTH + 8, 128 * k : 128 * k + 128] + acc[WIDTH + 8 : WIDTH + 16, 128 * k : 128 * k + 128]
        for k in range(HEAD // 128)
    ]
    coord_grad.append(tail[WIDTH : WIDTH + 8] + tail[WIDTH + 8 : WIDTH + 16])
    own_proj_grad[...] = rows[0:ATOMS, :]
    own_pos_grad[...] = jnp.where(lane < ATOMS, coord_grad[0] - pulled, 0.0)
    entry = rows_of((GHOST, WIDTH))
    for i in range(26):
        value = rows[STARTS[i] : STARTS[i] + GHOST, :] if STARTS[i] + GHOST <= LIST else None
        if value is None:
            tail_rows[0:GHOST, :] = jnp.zeros((GHOST, WIDTH), f32)
            tail_rows[0 : SIZES[i], :] = rows[STARTS[i] : STARTS[i] + SIZES[i], :]
            value = tail_rows[0:GHOST, :]
        elif SIZES[i] < GHOST:
            value = jnp.where(entry < SIZES[i], value, 0.0)
        value = value.astype(bf16)
        if i in chosen:
            back_chosen = jnp.where(
                face_col[:, i : i + 1] == jnp.where(lane[0:1] < SIZES[i], lists[i : i + 1, :], -1.0), 1.0, 0.0
            ).astype(bf16)
            value = nn(back_chosen[0:GHOST, 0:GHOST], value).astype(bf16)
        back[i] = value
        k, at = divmod(STARTS[i], 128)
        moved = coord_grad[k]
        if at:
            moved = pltpu.roll(moved, 128 - at, 1)
        if at + SIZES[i] > 128:
            moved = jnp.where(lane < 128 - at, moved, pltpu.roll(coord_grad[k + 1], 128 - at, 1))
        moved = jnp.where(lane < SIZES[i], moved, 0.0)
        if i in chosen:
            parts = jnp.concatenate(list(pieces(moved)) + [jnp.zeros((8, 128), f32)], axis=0)
            parts = nt(parts.astype(bf16), back_chosen)
            moved = parts[0:8] + parts[8:16] + parts[16:24]
        back_small[i] = moved


def edges(received, received_small, proj, center, positions, species, neighbor, live, scale, shift, *weights):
    vmem = pl.BlockSpec(memory_space=pltpu.VMEM)
    smem = pl.BlockSpec(memory_space=pltpu.SMEM)
    return pl.pallas_call(
        edge_kernel,
        out_shape=(
            jax.ShapeDtypeStruct((1, ATOMS), f32),
            jax.ShapeDtypeStruct((26, GHOST, WIDTH), bf16),
            jax.ShapeDtypeStruct((26, 8, 128), f32),
            jax.ShapeDtypeStruct((ATOMS, WIDTH), f32),
            jax.ShapeDtypeStruct((ATOMS, WIDTH), f32),
            jax.ShapeDtypeStruct((8, 128), f32),
        ),
        in_specs=[vmem] * 8 + [smem] * 2 + [vmem] * 5,
        out_specs=(vmem,) * 6,
        scratch_shapes=[
            pltpu.VMEM((LIST, WIDTH), f32),
            pltpu.VMEM((128, WIDTH), f32),
            pltpu.VMEM((128, 128), f32),
            pltpu.VMEM((128, 128), f32),
            pltpu.VMEM((8, LIST), f32),
            pltpu.VMEM((WIDTH, HEAD), bf16),
            pltpu.VMEM((8, WIDTH, 128), bf16),
            pltpu.VMEM((3 * CHANNELS, WIDTH), bf16),
            pltpu.VMEM((WIDTH, WIDTH + 3 * CHANNELS), bf16),
            pltpu.VMEM((OUT_WIDTH, WIDTH), bf16),
            pltpu.VMEM((OUT_WIDTH, 128), f32),
            pltpu.VMEM((6, ATOMS, SLOTS), f32),
            pltpu.VMEM((8, R_COUNT * GROUP, 128), f32),
            pltpu.VMEM((LIST, GROUP * SLOTS), bf16),
            pltpu.VMEM((WIDTH + 16, HEAD), f32),
            pltpu.VMEM((8, WIDTH + 16, 128), f32),
            pltpu.VMEM((ATOMS, 128), f32),
        ],
        compiler_params=pltpu.CompilerParams(vmem_limit_bytes=56 * 1024 * 1024),
        name="edges",
    )(
        received, received_small, proj, center, positions, species, neighbor, live, scale, shift, *weights
    )


def unpack_kernel(
    face_rows, face_small, own_proj_grad, center_grad, own_pos_grad, lists, w_center, w_neighbor, forces,
    feature_grad, padded
):
    padded[...] = jnp.full((32, 128), -1, i32)
    padded[0:27, 0:GHOST] = lists[...]
    proj_grad = own_proj_grad[...]
    pos_grad = jnp.zeros((32, ATOMS), f32)
    atom = rows_of((ATOMS, 128))
    for i, cell in enumerate(FACE_CELLS):
        chosen = jnp.where(padded[cell : cell + 1, :] == atom, 1.0, 0.0).astype(bf16)
        proj_grad = proj_grad + nn(chosen[:, 0:GHOST], face_rows[i])
        parts = jnp.concatenate(list(pieces(face_small[i])) + [jnp.zeros((8, 128), f32)], axis=0)
        pos_grad = pos_grad + nt(parts.astype(bf16), chosen)
    feature_grad[...] = nt(proj_grad.astype(bf16), w_neighbor[...]) + nt(
        center_grad[...].astype(bf16), w_center[...]
    )
    total = own_pos_grad[:, 0:ATOMS] + pos_grad[0:8] + pos_grad[8:16] + pos_grad[16:24]
    forces[...] = -total[0:3]


def unpack(*args):
    vmem = pl.BlockSpec(memory_space=pltpu.VMEM)
    return pl.pallas_call(
        unpack_kernel,
        out_shape=(
            jax.ShapeDtypeStruct((3, ATOMS), f32),
            jax.ShapeDtypeStruct((ATOMS, WIDTH), f32),
        ),
        in_specs=[vmem] * 8,
        out_specs=(vmem,) * 2,
        scratch_shapes=[pltpu.VMEM((32, 128), i32)],
        name="unpack",
    )(*args)


def solution(mesh):
    sizes = tuple(mesh.shape[a] for a in ("gx", "gy", "gz"))

    def local(
        positions,
        atom_features,
        species,
        edge_neighbor,
        edge_live,
        send_list,
        species_scale,
        species_shift,
        w_center,
        w_neighbor,
        w_basis,
        w_env,
        w_latent,
        w_out,
        w_final,
    ):
        face_rows, face_small, proj, center = pack(
            atom_features, positions, send_list, w_center, w_neighbor
        )
        received, received_small = exchange_out(face_rows, face_small, sizes)
        energy, back, back_small, own_proj_grad, center_grad, own_pos_grad = edges(
            received,
            received_small,
            proj,
            center,
            positions,
            species.reshape(1, ATOMS),
            edge_neighbor,
            edge_live,
            species_scale,
            species_shift,
            w_basis,
            w_env,
            w_latent,
            w_out,
            w_final.reshape(1, OUT_WIDTH),
        )
        face_rows, face_small = exchange_back(back, back_small, sizes)
        forces, feature_grad = unpack(
            face_rows, face_small, own_proj_grad, center_grad, own_pos_grad, send_list, w_center, w_neighbor
        )
        return energy.reshape(ATOMS), forces, feature_grad

    split = ("gx", "gy", "gz")
    return jax.shard_map(
        local,
        mesh=mesh,
        in_specs=(P(None, split), P(split, None), P(split), P(split, None), P(split, None), P(split, None))
        + (P(),) * 9,
        out_specs=(P(split), P(None, split), P(split, None)),
        check_vma=False,
    )
```

```python
import functools
import math

import jax
import jax.numpy as jnp
from jax import lax
from jax.experimental import pallas as pl
from jax.experimental.pallas import tpu as pltpu
from jax.sharding import PartitionSpec as P

SIDE = 4
REACH = 3
SPACING = 2.15
CUT = 6.0
ENV_NORM = 0.125
ATOMS = 64
SLOTS = 128
GHOST = 48
WIDTH = 256
CHANNELS = 64
OUT_WIDTH = 128
BASIS = 8
LIST = 1024
HEAD = 896
BASIS_AT = 1000
CENTER_AT = 1008
GROUP = 8
ABREAST = 4

f32 = jnp.float32
bf16 = jnp.bfloat16
i32 = jnp.int32

FACES = [(-1, 0, 0), (1, 0, 0), (0, -1, 0), (0, 1, 0), (0, 0, -1), (0, 0, 1)]
X_FACE, Y_FACE, Z_FACE = 0, 2, 4
Y_CELLS = [(0, -1, 0), (0, 1, 0)]
Z_CELLS = [(0, ty, tz) for tz in (-1, 1) for ty in (0, -1, 1)]
X_CELLS = [
    (tx,) + behind for tx in (-1, 1) for behind in [(0, 0)] + [c[1:] for c in Y_CELLS + Z_CELLS]
]
DIRECTIONS = Y_CELLS + Z_CELLS + X_CELLS
Z_AT, X_AT = (2, 5), (8, 17)
CELLS = [9 * (tx + 1) + 3 * (ty + 1) + tz + 1 for tx, ty, tz in DIRECTIONS]
SIZES = [math.prod(REACH if t else SIDE for t in d) for d in DIRECTIONS]
STARTS = [ATOMS + sum(SIZES[:i]) for i in range(26)]
assert STARTS[-1] + SIZES[-1] == BASIS_AT
FACE_CELLS = [9 * (tx + 1) + 3 * (ty + 1) + tz + 1 for tx, ty, tz in FACES]
LIST_ROW = 3
FACE_LIST = 4


def list_slot(direction):
    tx, ty, tz = direction
    return 3 * (tx + 1) + (tz + 1 if ty else 1)


def nn(a, b):
    return jnp.dot(a, b, preferred_element_type=f32)


def nt(a, b):
    return lax.dot_general(a, b, (((1,), (1,)), ((), ())), preferred_element_type=f32)


def lanes_of(shape):
    return lax.broadcasted_iota(i32, shape, len(shape) - 1)


def rows_of(shape):
    return lax.broadcasted_iota(i32, shape, 0)


def column(row, size):
    shape = (size, size)
    on = rows_of(shape) == lanes_of(shape)
    return jnp.sum(jnp.where(on, jnp.broadcast_to(row, shape), 0.0), axis=1, keepdims=True)


def row(col, size):
    shape = (size, size)
    on = rows_of(shape) == lanes_of(shape)
    return jnp.sum(jnp.where(on, jnp.broadcast_to(col, shape), 0.0), axis=0, keepdims=True)


def pieces(value):
    high = value.astype(bf16).astype(f32)
    rest = value - high
    middle = rest.astype(bf16).astype(f32)
    low = (rest - middle).astype(bf16).astype(f32)
    return high, middle, low


def sigmoid(x):
    return 0.5 * jnp.tanh(0.5 * x) + 0.5


PARTNERS = Y_CELLS + Z_CELLS + FACES[0:2]


def greet(sizes):
    here = [lax.axis_index(a) for a in ("gx", "gy", "gz")]

    def place(direction):
        return tuple(lax.rem(h + (t + n), n) if t else h for h, t, n in zip(here, direction, sizes))

    barrier = pltpu.get_barrier_semaphore()
    for d in PARTNERS:
        pl.semaphore_signal(barrier, inc=1, device_id=place(d), device_id_type=pl.DeviceIdType.MESH)
    return place, barrier


def sender(place, send_sem, recv_sem):
    count = [0]

    def send(sources, targets, direction):
        started = []
        for source, target in zip(sources, targets):
            k = count[0]
            count[0] += 1
            copy = pltpu.make_async_remote_copy(
                src_ref=source,
                dst_ref=target,
                send_sem=send_sem.at[k],
                recv_sem=recv_sem.at[k],
                device_id=place(direction),
                device_id_type=pl.DeviceIdType.MESH,
            )
            copy.start()
            started.append(copy)
        return started

    return send


def arrived(*groups):
    for group in groups:
        for copy in group:
            copy.wait_recv()


def sent(*groups):
    for group in groups:
        for copy in group:
            copy.wait_send()


def at(refs, start, count):
    return [r.at[pl.ds(start, count)] for r in refs]


def first_face(direction):
    tx, ty, tz = direction
    return Y_FACE + (ty + 1) // 2 if ty else Z_FACE + (tz + 1) // 2 if tz else X_FACE + (tx + 1) // 2


def out_kernel(
    sizes, features, positions, lists, w_center, w_neighbor, rows, small, proj, center, square, listed, held,
    face_rows, face_small, send_sem, recv_sem
):
    place, barrier = greet(sizes)
    rounded = features[...].astype(bf16)
    own = nn(rounded, w_neighbor[...]).astype(bf16)
    proj[...] = own
    center[...] = nn(rounded, w_center[...]).astype(bf16)
    square[...] = jnp.zeros((128, 128), f32)
    square[0:3, 0:ATOMS] = positions[...]
    parts = jnp.concatenate(list(pieces(square[0:8, :])), axis=0)
    parts = jnp.concatenate([parts, jnp.zeros((8, 128), f32)], axis=0).astype(bf16)
    held[0:ATOMS, :] = own
    held[ATOMS:128, :] = jnp.zeros((128 - ATOMS, WIDTH), bf16)
    listed[...] = jnp.full((32, 128), -1.0, f32)
    listed[0:27, 0:GHOST] = lists[...].astype(f32)
    square[0:32, :] = listed[...]
    by_entry = square[...].T
    wide = lanes_of((128, 128)).astype(f32)
    which = rows_of((8, 128))
    for i, (face, cell) in enumerate(zip(FACES, FACE_CELLS)):
        chosen = jnp.where(by_entry[:, cell : cell + 1] == wide, 1.0, 0.0).astype(bf16)
        face_rows[i] = nn(chosen[0:GHOST], held[...]).astype(bf16)
        moved = nt(parts, chosen)
        packed = moved[0:8] + moved[8:16] + moved[16:24]
        axis = [a for a in range(3) if face[a]][0]
        for d, c in zip(DIRECTIONS, CELLS):
            first = 1 if d[1] else 2 if d[2] else 0
            if first != axis or d[first] != face[first] or first == 0:
                continue
            r, half = divmod(list_slot(d), 2)
            entries = jnp.broadcast_to(listed[c : c + 1, :], (8, 128))
            if half:
                entries = pltpu.roll(entries, 64, 1)
            lane = lanes_of((8, 128))
            here = (which == LIST_ROW + r) & ((lane >= 64) if half else (lane < 64))
            packed = jnp.where(here, entries, packed)
        face_small[i] = packed
    pl.semaphore_wait(barrier, len(PARTNERS))
    send = sender(place, send_sem, recv_sem)
    own, cells = (face_rows, face_small), (rows, small)
    direct = {}
    for i in sorted(range(8), key=lambda i: (i < 2, i)):
        d = DIRECTIONS[i]
        direct[i] = send(at(own, first_face(d), 1), at(cells, i, 1), d)
    steps = ((0, FACES[0]), (1, FACES[1]))
    x_own = [send(at(own, X_FACE + k, 1), at(cells, X_AT[k], 1), d) for k, d in steps]
    onward = []
    for start, count in ((0, 2), (2, 3), (5, 3)):
        arrived(*[direct[i] for i in range(start, start + count)])
        onward += [
            send(at(cells, start, count), at(cells, X_AT[k] + 1 + start, count), d) for k, d in steps
        ]
    arrived(*x_own, *onward)
    sent(*direct.values(), *x_own, *onward)


def send_out(features, positions, lists, w_center, w_neighbor, sizes):
    vmem = pl.BlockSpec(memory_space=pltpu.VMEM)
    return pl.pallas_call(
        functools.partial(out_kernel, sizes),
        out_shape=(
            jax.ShapeDtypeStruct((26, GHOST, WIDTH), bf16),
            jax.ShapeDtypeStruct((26, 8, 128), f32),
            jax.ShapeDtypeStruct((ATOMS, WIDTH), bf16),
            jax.ShapeDtypeStruct((ATOMS, WIDTH), bf16),
        ),
        in_specs=[vmem] * 5,
        out_specs=(vmem,) * 4,
        scratch_shapes=[
            pltpu.VMEM((128, 128), f32),
            pltpu.VMEM((32, 128), f32),
            pltpu.VMEM((128, WIDTH), bf16),
            pltpu.VMEM((6, GHOST, WIDTH), bf16),
            pltpu.VMEM((6, 8, 128), f32),
            pltpu.SemaphoreType.DMA((32,)),
            pltpu.SemaphoreType.DMA((32,)),
        ],
        compiler_params=pltpu.CompilerParams(collective_id=0, has_side_effects=True),
        name="send_out",
    )(features, positions, lists, w_center, w_neighbor)


def back_kernel(
    sizes, rows, small, owner_rows, owner_small, from_x, from_x_small, total, total_small, send_sem, recv_sem
):
    place, barrier = greet(sizes)
    pl.semaphore_wait(barrier, len(PARTNERS))
    send = sender(place, send_sem, recv_sem)
    given, sums, owners = (rows, small), (total, total_small), (owner_rows, owner_small)
    steps = ((0, FACES[1]), (1, FACES[0]))
    in_x = [(from_x.at[k], from_x_small.at[k]) for k in (0, 1)]
    x_rest = [send(at(given, X_AT[k] + 3, 6), at(in_x[k], 2, 6), d) for k, d in steps]
    x_pair = [send(at(given, X_AT[k] + 1, 2), at(in_x[k], 0, 2), d) for k, d in steps]
    x_own = [send(at(given, X_AT[k], 1), at(owners, 8 + k, 1), d) for k, d in steps]
    direct = []
    for group, cells in ((x_rest, range(2, 8)), (x_pair, range(2))):
        arrived(*group)
        for i in cells:
            total[i] = (
                rows[i].astype(f32) + from_x[0, i].astype(f32) + from_x[1, i].astype(f32)
            ).astype(bf16)
            total_small[i] = small[i] + from_x_small[0, i] + from_x_small[1, i]
            d = tuple(-t for t in DIRECTIONS[i])
            direct.append(send(at(sums, i, 1), at(owners, i, 1), d))
    arrived(*x_own, *direct)
    sent(*x_rest, *x_pair, *x_own, *direct)


def send_back(rows, small, sizes):
    vmem = pl.BlockSpec(memory_space=pltpu.VMEM)
    return pl.pallas_call(
        functools.partial(back_kernel, sizes),
        out_shape=(
            jax.ShapeDtypeStruct((10, GHOST, WIDTH), bf16),
            jax.ShapeDtypeStruct((10, 8, 128), f32),
        ),
        in_specs=[vmem] * 2,
        out_specs=(vmem,) * 2,
        scratch_shapes=[
            pltpu.VMEM((2, 8, GHOST, WIDTH), bf16),
            pltpu.VMEM((2, 8, 8, 128), f32),
            pltpu.VMEM((8, GHOST, WIDTH), bf16),
            pltpu.VMEM((8, 8, 128), f32),
            pltpu.SemaphoreType.DMA((28,)),
            pltpu.SemaphoreType.DMA((28,)),
        ],
        compiler_params=pltpu.CompilerParams(collective_id=1, has_side_effects=True),
        name="send_back",
    )(rows, small)


R_INDEX, R_ENV, R_SCALED, R_SCALE, R_SLOPE, R_U, R_INV, R_Y, R_BESS, R_BESS_D = 0, 1, 2, 3, 4, 5, 8, 9, 17, 25
R_COUNT = 33


def geometry(index, rx, ry, rz, live, scale):
    squared = rx * rx + ry * ry + rz * rz
    distance = jnp.sqrt(squared)
    inverse = 1.0 / distance
    ux, uy, uz = rx * inverse, ry * inverse, rz * inverse
    x = distance * (1.0 / CUT)
    x2 = x * x
    x5 = x2 * x2 * x
    x6 = x5 * x
    inside = jnp.where(x < 1.0, live, 0.0)
    env = inside * (1.0 + x6 * (-28.0 + x * (48.0 - 21.0 * x)))
    slope = inside * (x5 * (-168.0 + x * (336.0 - 168.0 * x))) * (1.0 / CUT)
    s3, s5, s15 = math.sqrt(3.0), math.sqrt(5.0), math.sqrt(15.0)
    ys = [
        s3 * ux,
        s3 * uy,
        s3 * uz,
        s15 * ux * uy,
        s15 * uy * uz,
        0.5 * s5 * (3.0 * uz * uz - 1.0),
        s15 * ux * uz,
        0.5 * s15 * (ux * ux - uy * uy),
    ]
    theta = distance * (math.pi / CUT)
    sin1, cos1 = jnp.sin(theta), jnp.cos(theta)
    sines, cosines = [jnp.zeros_like(sin1), sin1], [jnp.ones_like(cos1), cos1]
    for _ in range(BASIS - 1):
        sines.append(2.0 * cos1 * sines[-1] - sines[-2])
        cosines.append(2.0 * cos1 * cosines[-1] - cosines[-2])
    norm = math.sqrt(2.0 / CUT)
    bess, bess_d = [], []
    for n in range(1, BASIS + 1):
        value = norm * sines[n] * inverse
        bess.append(value)
        bess_d.append((norm * n * math.pi / CUT * cosines[n] - value) * inverse)
    return [index, env, env * scale, scale, slope, ux, uy, uz, inverse] + ys + bess + bess_d


def edge_blocks(
    per_atom,
    slots,
    table,
    onehot,
    head_proj,
    tail_proj,
    w_env,
    w_latent,
    w_out,
    w_basis,
    env_t,
    latent_t,
    out_t,
    final_col,
    acc,
    acc_tail,
    energy,
):
    width = GROUP * per_atom
    abreast = 1 if per_atom == SLOTS else ABREAST
    lane = lanes_of((GROUP, 128))

    def chunks_of(q):
        atoms = [slots[q, pl.ds(j, GROUP, stride=GROUP), :] for j in range(GROUP)]
        if per_atom == SLOTS:
            return atoms
        out = []
        for g in (0, 4):
            a0 = atoms[g]
            a1 = pltpu.roll(atoms[g + 1], 96, 1)
            a2 = pltpu.roll(atoms[g + 2], 64, 1)
            a3 = pltpu.roll(atoms[g + 3], 32, 1)
            out += [
                jnp.where(lane < 96, a0, a1),
                jnp.where(lane < 64, a1, a2),
                jnp.where(lane < 32, a2, a3),
            ]
        return out

    packed = [jnp.concatenate(chunks_of(q), axis=1) for q in range(6)]
    for q, value in enumerate(geometry(*packed)):
        for k in range(width // 128):
            table[k, q * GROUP : (q + 1) * GROUP, :] = value[:, 128 * k : 128 * k + 128]

    acc[...] = jnp.zeros(acc.shape, f32)

    wide = (GROUP, width)
    first_lane = rows_of(wide) * per_atom
    mask = (lanes_of(wide) >= first_lane) & (lanes_of(wide) < first_lane + per_atom)
    maskf = jnp.where(mask, 1.0, 0.0).astype(f32)

    deg = rows_of((3 * CHANNELS, 80)) // CHANNELS
    comp = lanes_of((3 * CHANNELS, 80)) // GROUP
    allowed = (
        ((deg == 0) & (comp == 0))
        | ((deg == 1) & (comp >= 1) & (comp <= 3))
        | ((deg == 2) & (comp >= 4) & (comp <= 8))
    )

    def block(b, onehot):
        def value(q):
            parts = [table[k, pl.ds(q * GROUP + b, 1), :] for k in range(width // 128)]
            return jnp.concatenate(parts, axis=1)

        def eight(q):
            place = pl.ds(q * GROUP + b, GROUP, stride=GROUP)
            return jnp.concatenate([table[k, place, :] for k in range(width // 128)], axis=1)

        index = value(R_INDEX).astype(i32)
        env = value(R_ENV)
        bess = eight(R_BESS)
        tile = (16, width)
        apart = (jnp.broadcast_to(index, tile) - rows_of(tile)).astype(jnp.int16)
        for h in range(BASIS_AT // 16):
            onehot[16 * h : 16 * h + 16, 0:width] = jnp.where(
                apart == jnp.int16(16 * h), jnp.ones(tile, bf16), jnp.zeros(tile, bf16)
            )
        last = jnp.where(index == rows_of(wide) + (BASIS_AT - 8), 1.0, 0.0)
        onehot[BASIS_AT - 8 : BASIS_AT + 8, 0:width] = jnp.concatenate([last, bess], axis=0).astype(bf16)
        onehot[CENTER_AT:LIST, 0:width] = jnp.concatenate(
            [maskf, jnp.zeros(wide, f32)], axis=0
        ).astype(bf16)
        hot = onehot[:, 0:width]

        yield
        pre = nn(jnp.concatenate([head_proj[...], tail_proj[b]], axis=1), hot)
        sig = sigmoid(pre)
        act = pre * sig
        act_d = sig + act * (1.0 - sig)
        latent = env * act
        latent_h = latent.astype(bf16)
        yield
        weights = nn(env_t[...], latent_h)
        weights_h = weights.astype(bf16)
        ys = eight(R_Y)
        harm = jnp.concatenate(
            [maskf]
            + [maskf * ys[m : m + 1] for m in range(8)]
            + [jnp.zeros(wide, f32)],
            axis=0,
        ).astype(bf16)
        yield
        around = jnp.where(allowed, ENV_NORM * nt(weights_h, harm), 0.0)
        around_h = around.astype(bf16)
        yield
        tensor = nn(around_h, harm)
        scalars_h = (weights * tensor).astype(bf16)
        yield
        mixed = nn(latent_t[...], jnp.concatenate([latent_h, scalars_h], axis=0))
        sig = sigmoid(mixed)
        update = mixed * sig
        update_d = sig + update * (1.0 - sig)
        refined_h = (latent + env * update).astype(bf16)
        yield
        hidden = nn(out_t[...], refined_h)
        sig = sigmoid(hidden)
        hidden_act = hidden * sig
        final = final_col[:, 0:1]
        per_edge = jnp.sum(hidden_act * final, axis=0, keepdims=True)
        energy[pl.ds(pl.multiple_of(b * GROUP, GROUP), GROUP), :] = jnp.broadcast_to(
            jnp.sum(maskf * (env * per_edge), axis=1, keepdims=True), (GROUP, 128)
        )

        scaled = value(R_SCALED)
        d_hidden = ((sig + hidden_act * (1.0 - sig)) * final * scaled).astype(bf16)
        yield
        d_refined = nn(w_out[...], d_hidden)
        d_env = value(R_SCALE) * per_edge
        d_env += jnp.sum(d_refined * update, axis=0, keepdims=True)
        d_mixed = (env * d_refined * update_d).astype(bf16)
        yield
        d_both = nn(w_latent[...], d_mixed)
        d_scalars = d_both[WIDTH:]
        d_tensor_h = (d_scalars * weights).astype(bf16)
        yield
        d_around = jnp.where(allowed, ENV_NORM * nt(d_tensor_h, harm), 0.0)
        yield
        d_weights = d_scalars * tensor + nn(d_around.astype(bf16), harm)
        yield
        d_latent = d_refined + d_both[0:WIDTH] + nn(w_env[...], d_weights.astype(bf16))
        d_env += jnp.sum(d_latent * act, axis=0, keepdims=True)
        d_pre = (env * d_latent * act_d).astype(bf16)
        yield
        d_bess = nn(w_basis[...], d_pre)
        both = jnp.concatenate([around.T, d_around.T], axis=1).astype(bf16)
        d_harm = nn(both, jnp.concatenate([d_tensor_h, weights_h], axis=0))
        dy = [
            jnp.sum(maskf * d_harm[m * GROUP : (m + 1) * GROUP], axis=0, keepdims=True)
            for m in range(1, 9)
        ]

        ux, uy, uz, inverse = (value(q) for q in (R_U, R_U + 1, R_U + 2, R_INV))
        d_dist = d_env * value(R_SLOPE) + jnp.sum(d_bess * eight(R_BESS_D), axis=0, keepdims=True)
        s3, s5, s15 = math.sqrt(3.0), math.sqrt(5.0), math.sqrt(15.0)
        gx = s3 * dy[0] + s15 * (uy * dy[3] + uz * dy[6] + ux * dy[7])
        gy = s3 * dy[1] + s15 * (ux * dy[3] + uz * dy[4] - uy * dy[7])
        gz = s3 * dy[2] + s15 * (uy * dy[4] + ux * dy[6]) + 3.0 * s5 * uz * dy[5]
        along = d_dist - inverse * (gx * ux + gy * uy + gz * uz)
        d_rel = [inverse * g + along * u for g, u in ((gx, ux), (gy, uy), (gz, uz))]
        place = rows_of(wide)
        moved = jnp.where(place == 0, d_rel[0], 0.0)
        moved = jnp.where(place == 1, d_rel[1], moved)
        moved = jnp.where(place == 2, d_rel[2], moved)
        high = moved.astype(bf16).astype(f32)
        moved_h = jnp.concatenate([high, moved - high], axis=0).astype(bf16)
        yield
        spread = nt(jnp.concatenate([d_pre, moved_h], axis=0), hot)
        acc[...] += spread[:, 0:HEAD]
        acc_tail[b] = spread[:, HEAD:]

    def several(i, carry):
        running = [block(abreast * i + k, onehot.at[k]) for k in range(abreast)]
        while running:
            running = [r for r in running if next(r, 0) is None]
        return carry

    lax.fori_loop(0, ATOMS // GROUP // abreast, several, 0)


def edge_kernel(
    received,
    received_small,
    proj,
    center,
    positions,
    species,
    neighbor,
    live_in,
    kind_scale,
    kind_shift,
    w_basis,
    env_t,
    w_latent,
    w_out,
    w_final,
    energy_out,
    back,
    back_small,
    own_proj_grad,
    center_grad,
    own_pos_grad,
    rows,
    tail_rows,
    lists,
    faces,
    coords,
    head_proj,
    tail_proj,
    env_back,
    latent_t,
    out_t,
    final_col,
    slots,
    table,
    onehot,
    acc,
    acc_tail,
    energy,
):
    rows[0:ATOMS, :] = proj[...].astype(f32)
    lane = lanes_of((8, 128))
    lists[...] = jnp.full((128, 128), -1.0, f32)
    faces[...] = jnp.full((128, 128), -2.0, f32)
    corner = [i for i in range(26) if DIRECTIONS[i] not in FACES]
    for i in corner:
        r, half = divmod(list_slot(DIRECTIONS[i]), 2)
        entries = received_small[i, LIST_ROW + r : LIST_ROW + r + 1, :]
        lists[i : i + 1, :] = pltpu.roll(entries, 64, 1) if half else entries
        r = LIST_ROW + FACE_LIST // 2
        faces[i : i + 1, :] = jnp.where(lane[0:1] < GHOST, received_small[i, r : r + 1, :], -2.0)
    entry_col = lists[...].T
    face_col = faces[...].T
    chosen = {
        i: jnp.where(entry_col[:, i : i + 1] == faces[i : i + 1, :], 1.0, 0.0).astype(bf16) for i in corner
    }
    for i in range(26):
        if i in chosen:
            value = nn(chosen[i][0:GHOST, 0:GHOST], received[i])
        else:
            value = received[i].astype(f32)
        rows[STARTS[i] : STARTS[i] + SIZES[i], :] = value[0 : SIZES[i]]
    rows[BASIS_AT:CENTER_AT, :] = w_basis[...].astype(f32)
    rows[CENTER_AT:LIST, :] = jnp.zeros((LIST - CENTER_AT, WIDTH), f32)
    for k in range(HEAD // 128):
        head_proj[:, 128 * k : 128 * k + 128] = rows[128 * k : 128 * k + 128, :].T.astype(bf16)
    for b in range(ATOMS // GROUP):
        rows[CENTER_AT : CENTER_AT + GROUP, :] = center[...].astype(f32)[GROUP * b : GROUP * b + GROUP]
        tail_proj[b] = rows[HEAD:LIST, :].T.astype(bf16)

    coords[...] = jnp.zeros(coords.shape, f32)
    coords[0:3, 0:ATOMS] = positions[...]
    filled = [coords[0:8, 128 * k : 128 * k + 128] for k in range(8)]
    which = rows_of((8, 128))
    for i, d in enumerate(DIRECTIONS):
        value = received_small[i]
        if i in chosen:
            parts = jnp.concatenate(list(pieces(value)) + [jnp.zeros((8, 128), f32)], axis=0)
            parts = nt(parts.astype(bf16), chosen[i])
            value = parts[0:8] + parts[8:16] + parts[16:24]
        step = [t * SIDE * SPACING for t in d]
        shift = jnp.where(which == 0, step[0], jnp.where(which == 1, step[1], step[2]))
        value = value - shift
        k, at = divmod(STARTS[i], 128)
        end = at + SIZES[i]
        value = pltpu.roll(value, at, 1) if at else value
        filled[k] = jnp.where((lane >= at) & (lane < end), value, filled[k])
        if end > 128:
            filled[k + 1] = jnp.where(lane < end - 128, value, filled[k + 1])

    env_back[...] = env_t[...].astype(f32).T.astype(bf16)
    latent_t[...] = w_latent[...].astype(f32).T.astype(bf16)
    out_t[...] = w_out[...].astype(f32).T.astype(bf16)
    final_col[...] = jnp.broadcast_to(column(w_final[...], OUT_WIDTH), (OUT_WIDTH, 128))

    kinds = species[...]
    scale_row = jnp.where(
        kinds == 0,
        kind_scale[0],
        jnp.where(kinds == 1, kind_scale[1], jnp.where(kinds == 2, kind_scale[2], kind_scale[3])),
    )
    shift_row = jnp.where(
        kinds == 0,
        kind_shift[0],
        jnp.where(kinds == 1, kind_shift[1], jnp.where(kinds == 2, kind_shift[2], kind_shift[3])),
    )

    full = (ATOMS, SLOTS)
    local = neighbor[...]
    ghost = local - ATOMS
    cell = jnp.where(ghost < 0, 13, (ghost * 1366) >> 16)
    jump = jnp.zeros((8, 128), i32)
    for i, c in enumerate(CELLS):
        jump = jnp.where(lane == c, STARTS[i] - ATOMS - GHOST * c, jump)
    jump = jnp.concatenate([jump] * 8, axis=0)
    index = local + jnp.take_along_axis(jump, cell, axis=1, mode="promise_in_bounds")
    low, page = index & 127, index >> 7
    rel = []
    for a in range(3):
        found = jnp.zeros(full, f32)
        for k in range(8):
            source = jnp.broadcast_to(filled[k][a : a + 1, :], full)
            taken = jnp.take_along_axis(source, low, axis=1, mode="promise_in_bounds")
            found = jnp.where(page == k, taken, found)
        rel.append(found - column(positions[a : a + 1, :], ATOMS))
    distance = jnp.sqrt(rel[0] * rel[0] + rel[1] * rel[1] + rel[2] * rel[2])
    live = jnp.where(distance * (1.0 / CUT) < 1.0, live_in[...], 0)

    before = jnp.where(rows_of((SLOTS, SLOTS)) < lanes_of((SLOTS, SLOTS)), 1.0, 0.0).astype(bf16)
    gap = nn((1 - live).astype(f32).astype(bf16), before).astype(i32)
    most = jnp.max(jnp.sum(live.astype(f32), axis=1, keepdims=True))
    values = [index] + rel
    for step in range(7):
        by = 1 << step
        moves = jnp.where((gap & by) != 0, live, 0)
        come = pltpu.roll(moves, SLOTS - by, 1) != 0
        values = [jnp.where(come, pltpu.roll(v, SLOTS - by, 1), v) for v in values]
        gap = jnp.where(come, pltpu.roll(gap, SLOTS - by, 1), gap)
        live = jnp.where(come, 1, live - moves)
    kept = live != 0
    slots[0] = jnp.where(kept, values[0], LIST - 1).astype(f32)
    slots[1] = jnp.where(kept, values[1], 0.5 * CUT)
    slots[2] = jnp.where(kept, values[2], 0.0)
    slots[3] = jnp.where(kept, values[3], 0.0)
    slots[4] = live.astype(f32)
    slots[5] = jnp.broadcast_to(column(scale_row, ATOMS), full)

    shared = (
        slots,
        table,
        onehot,
        head_proj,
        tail_proj,
        env_back,
        w_latent,
        w_out,
        w_basis,
        env_t,
        latent_t,
        out_t,
        final_col,
        acc,
        acc_tail,
        energy,
    )

    @pl.when(most <= 96.0)
    def _():
        edge_blocks(96, *shared)

    @pl.when(most > 96.0)
    def _():
        edge_blocks(SLOTS, *shared)

    energy_out[...] = scale_row * row(energy[:, 0:1], ATOMS) + shift_row

    tail = acc_tail[0]
    for b in range(1, ATOMS // GROUP):
        tail = tail + acc_tail[b]
    for k in range(HEAD // 128):
        rows[128 * k : 128 * k + 128, :] = acc[0:WIDTH, 128 * k : 128 * k + 128].T
    rows[HEAD:LIST, :] = tail[0:WIDTH].T
    place = CENTER_AT - HEAD
    pulled = jnp.zeros((8, 128), f32)
    for b in range(ATOMS // GROUP):
        tail_rows[...] = acc_tail[b][0:WIDTH].T
        center_grad[GROUP * b : GROUP * b + GROUP, :] = tail_rows[place : place + GROUP, :]
        value = acc_tail[b][WIDTH : WIDTH + 8] + acc_tail[b][WIDTH + 8 : WIDTH + 16]
        value = pltpu.roll(value, (GROUP * b - place) % 128, 1)
        pulled = jnp.where((lane >= GROUP * b) & (lane < GROUP * b + GROUP), value, pulled)
    coord_grad = [
        acc[WIDTH : WIDTH + 8, 128 * k : 128 * k + 128] + acc[WIDTH + 8 : WIDTH + 16, 128 * k : 128 * k + 128]
        for k in range(HEAD // 128)
    ]
    coord_grad.append(tail[WIDTH : WIDTH + 8] + tail[WIDTH + 8 : WIDTH + 16])
    own_proj_grad[...] = rows[0:ATOMS, :]
    own_pos_grad[...] = jnp.where(lane < ATOMS, coord_grad[0] - pulled, 0.0)
    entry = rows_of((GHOST, WIDTH))
    for i in range(26):
        value = rows[STARTS[i] : STARTS[i] + GHOST, :] if STARTS[i] + GHOST <= LIST else None
        if value is None:
            tail_rows[0:GHOST, :] = jnp.zeros((GHOST, WIDTH), f32)
            tail_rows[0 : SIZES[i], :] = rows[STARTS[i] : STARTS[i] + SIZES[i], :]
            value = tail_rows[0:GHOST, :]
        elif SIZES[i] < GHOST:
            value = jnp.where(entry < SIZES[i], value, 0.0)
        value = value.astype(bf16)
        if i in chosen:
            back_chosen = jnp.where(
                face_col[:, i : i + 1] == jnp.where(lane[0:1] < SIZES[i], lists[i : i + 1, :], -1.0), 1.0, 0.0
            ).astype(bf16)
            value = nn(back_chosen[0:GHOST, 0:GHOST], value).astype(bf16)
        back[i] = value
        k, at = divmod(STARTS[i], 128)
        moved = coord_grad[k]
        if at:
            moved = pltpu.roll(moved, 128 - at, 1)
        if at + SIZES[i] > 128:
            moved = jnp.where(lane < 128 - at, moved, pltpu.roll(coord_grad[k + 1], 128 - at, 1))
        moved = jnp.where(lane < SIZES[i], moved, 0.0)
        if i in chosen:
            parts = jnp.concatenate(list(pieces(moved)) + [jnp.zeros((8, 128), f32)], axis=0)
            parts = nt(parts.astype(bf16), back_chosen)
            moved = parts[0:8] + parts[8:16] + parts[16:24]
        back_small[i] = moved


def edges(received, received_small, proj, center, positions, species, neighbor, live, scale, shift, *weights):
    vmem = pl.BlockSpec(memory_space=pltpu.VMEM)
    smem = pl.BlockSpec(memory_space=pltpu.SMEM)
    return pl.pallas_call(
        edge_kernel,
        out_shape=(
            jax.ShapeDtypeStruct((1, ATOMS), f32),
            jax.ShapeDtypeStruct((26, GHOST, WIDTH), bf16),
            jax.ShapeDtypeStruct((26, 8, 128), f32),
            jax.ShapeDtypeStruct((ATOMS, WIDTH), f32),
            jax.ShapeDtypeStruct((ATOMS, WIDTH), f32),
            jax.ShapeDtypeStruct((8, 128), f32),
        ),
        in_specs=[vmem] * 8 + [smem] * 2 + [vmem] * 5,
        out_specs=(vmem,) * 6,
        scratch_shapes=[
            pltpu.VMEM((LIST, WIDTH), f32),
            pltpu.VMEM((128, WIDTH), f32),
            pltpu.VMEM((128, 128), f32),
            pltpu.VMEM((128, 128), f32),
            pltpu.VMEM((8, LIST), f32),
            pltpu.VMEM((WIDTH, HEAD), bf16),
            pltpu.VMEM((8, WIDTH, 128), bf16),
            pltpu.VMEM((WIDTH, 3 * CHANNELS), bf16),
            pltpu.VMEM((WIDTH, WIDTH + 3 * CHANNELS), bf16),
            pltpu.VMEM((OUT_WIDTH, WIDTH), bf16),
            pltpu.VMEM((OUT_WIDTH, 128), f32),
            pltpu.VMEM((6, ATOMS, SLOTS), f32),
            pltpu.VMEM((8, R_COUNT * GROUP, 128), f32),
            pltpu.VMEM((ABREAST, LIST, GROUP * SLOTS), bf16),
            pltpu.VMEM((WIDTH + 16, HEAD), f32),
            pltpu.VMEM((8, WIDTH + 16, 128), f32),
            pltpu.VMEM((ATOMS, 128), f32),
        ],
        compiler_params=pltpu.CompilerParams(vmem_limit_bytes=56 * 1024 * 1024),
        name="edges",
    )(
        received, received_small, proj, center, positions, species, neighbor, live, scale, shift, *weights
    )


def unpack_kernel(
    face_rows, face_small, own_proj_grad, center_grad, own_pos_grad, lists, w_center, w_neighbor, forces,
    feature_grad, padded
):
    padded[...] = jnp.full((32, 128), -1, i32)
    padded[0:27, 0:GHOST] = lists[...]
    proj_grad = own_proj_grad[...]
    pos_grad = jnp.zeros((32, ATOMS), f32)
    atom = rows_of((ATOMS, 128))
    for i, d in enumerate(DIRECTIONS[0:8] + FACES[0:2]):
        cell = FACE_CELLS[first_face(d)]
        chosen = jnp.where(padded[cell : cell + 1, :] == atom, 1.0, 0.0).astype(bf16)
        proj_grad = proj_grad + nn(chosen[:, 0:GHOST], face_rows[i])
        parts = jnp.concatenate(list(pieces(face_small[i])) + [jnp.zeros((8, 128), f32)], axis=0)
        pos_grad = pos_grad + nt(parts.astype(bf16), chosen)
    feature_grad[...] = nt(proj_grad.astype(bf16), w_neighbor[...]) + nt(
        center_grad[...].astype(bf16), w_center[...]
    )
    total = own_pos_grad[:, 0:ATOMS] + pos_grad[0:8] + pos_grad[8:16] + pos_grad[16:24]
    forces[...] = -total[0:3]


def unpack(*args):
    vmem = pl.BlockSpec(memory_space=pltpu.VMEM)
    return pl.pallas_call(
        unpack_kernel,
        out_shape=(
            jax.ShapeDtypeStruct((3, ATOMS), f32),
            jax.ShapeDtypeStruct((ATOMS, WIDTH), f32),
        ),
        in_specs=[vmem] * 8,
        out_specs=(vmem,) * 2,
        scratch_shapes=[pltpu.VMEM((32, 128), i32)],
        name="unpack",
    )(*args)


def solution(mesh):
    sizes = tuple(mesh.shape[a] for a in ("gx", "gy", "gz"))

    def local(
        positions,
        atom_features,
        species,
        edge_neighbor,
        edge_live,
        send_list,
        species_scale,
        species_shift,
        w_center,
        w_neighbor,
        w_basis,
        w_env,
        w_latent,
        w_out,
        w_final,
    ):
        received, received_small, proj, center = send_out(
            atom_features, positions, send_list, w_center, w_neighbor, sizes
        )
        energy, back, back_small, own_proj_grad, center_grad, own_pos_grad = edges(
            received,
            received_small,
            proj,
            center,
            positions,
            species.reshape(1, ATOMS),
            edge_neighbor,
            edge_live,
            species_scale,
            species_shift,
            w_basis,
            w_env.T,
            w_latent,
            w_out,
            w_final.reshape(1, OUT_WIDTH),
        )
        owner_rows, owner_small = send_back(back, back_small, sizes)
        forces, feature_grad = unpack(
            owner_rows, owner_small, own_proj_grad, center_grad, own_pos_grad, send_list, w_center, w_neighbor
        )
        return energy.reshape(ATOMS), forces, feature_grad

    split = ("gx", "gy", "gz")
    return jax.shard_map(
        local,
        mesh=mesh,
        in_specs=(P(None, split), P(split, None), P(split), P(split, None), P(split, None), P(split, None))
        + (P(),) * 9,
        out_specs=(P(split), P(None, split), P(split, None)),
        check_vma=False,
    )
```

```python
import functools
import math

import jax
import jax.numpy as jnp
from jax import lax
from jax.experimental import pallas as pl
from jax.experimental.pallas import tpu as pltpu
from jax.sharding import PartitionSpec as P

SIDE = 4
REACH = 3
SPACING = 2.15
CUT = 6.0
ENV_NORM = 0.125
ATOMS = 64
SLOTS = 128
GHOST = 48
WIDTH = 256
CHANNELS = 64
OUT_WIDTH = 128
BASIS = 8
LIST = 1024
HEAD = 896
BASIS_AT = 1000
CENTER_AT = 1008
GROUP = 8
ABREAST = 4
SKEW = 1

f32 = jnp.float32
bf16 = jnp.bfloat16
i32 = jnp.int32

FACES = [(-1, 0, 0), (1, 0, 0), (0, -1, 0), (0, 1, 0), (0, 0, -1), (0, 0, 1)]
X_FACE, Y_FACE, Z_FACE = 0, 2, 4
Y_CELLS = [(0, -1, 0), (0, 1, 0)]
Z_CELLS = [(0, ty, tz) for tz in (-1, 1) for ty in (0, -1, 1)]
X_CELLS = [
    (tx,) + behind for tx in (-1, 1) for behind in [(0, 0)] + [c[1:] for c in Y_CELLS + Z_CELLS]
]
DIRECTIONS = Y_CELLS + Z_CELLS + X_CELLS
Z_AT, X_AT = (2, 5), (8, 17)
CELLS = [9 * (tx + 1) + 3 * (ty + 1) + tz + 1 for tx, ty, tz in DIRECTIONS]
SIZES = [math.prod(REACH if t else SIDE for t in d) for d in DIRECTIONS]
STARTS = [ATOMS + sum(SIZES[:i]) for i in range(26)]
assert STARTS[-1] + SIZES[-1] == BASIS_AT
FACE_CELLS = [9 * (tx + 1) + 3 * (ty + 1) + tz + 1 for tx, ty, tz in FACES]
LIST_ROW = 3
FACE_LIST = 4


def list_slot(direction):
    tx, ty, tz = direction
    return 3 * (tx + 1) + (tz + 1 if ty else 1)


def nn(a, b):
    return jnp.dot(a, b, preferred_element_type=f32)


def nt(a, b):
    return lax.dot_general(a, b, (((1,), (1,)), ((), ())), preferred_element_type=f32)


def lanes_of(shape):
    return lax.broadcasted_iota(i32, shape, len(shape) - 1)


def rows_of(shape):
    return lax.broadcasted_iota(i32, shape, 0)


def column(row, size):
    shape = (size, size)
    on = rows_of(shape) == lanes_of(shape)
    return jnp.sum(jnp.where(on, jnp.broadcast_to(row, shape), 0.0), axis=1, keepdims=True)


def row(col, size):
    shape = (size, size)
    on = rows_of(shape) == lanes_of(shape)
    return jnp.sum(jnp.where(on, jnp.broadcast_to(col, shape), 0.0), axis=0, keepdims=True)


def pieces(value):
    high = value.astype(bf16).astype(f32)
    rest = value - high
    middle = rest.astype(bf16).astype(f32)
    low = (rest - middle).astype(bf16).astype(f32)
    return high, middle, low


def sigmoid(x):
    return 0.5 * jnp.tanh(0.5 * x) + 0.5


PARTNERS = Y_CELLS + Z_CELLS + FACES[0:2]


def greet(sizes):
    here = [lax.axis_index(a) for a in ("gx", "gy", "gz")]

    def place(direction):
        return tuple(lax.rem(h + (t + n), n) if t else h for h, t, n in zip(here, direction, sizes))

    barrier = pltpu.get_barrier_semaphore()
    for d in PARTNERS:
        pl.semaphore_signal(barrier, inc=1, device_id=place(d), device_id_type=pl.DeviceIdType.MESH)
    return place, barrier


def sender(place, send_sem, recv_sem):
    count = [0]

    def send(sources, targets, direction):
        started = []
        for source, target in zip(sources, targets):
            k = count[0]
            count[0] += 1
            copy = pltpu.make_async_remote_copy(
                src_ref=source,
                dst_ref=target,
                send_sem=send_sem.at[k],
                recv_sem=recv_sem.at[k],
                device_id=place(direction),
                device_id_type=pl.DeviceIdType.MESH,
            )
            copy.start()
            started.append(copy)
        return started

    return send


def arrived(*groups):
    for group in groups:
        for copy in group:
            copy.wait_recv()


def sent(*groups):
    for group in groups:
        for copy in group:
            copy.wait_send()


def at(refs, start, count):
    return [r.at[pl.ds(start, count)] for r in refs]


def first_face(direction):
    tx, ty, tz = direction
    return Y_FACE + (ty + 1) // 2 if ty else Z_FACE + (tz + 1) // 2 if tz else X_FACE + (tx + 1) // 2


def out_kernel(
    sizes, features, positions, lists, w_center, w_neighbor, rows, small, proj, center, square, listed, held,
    face_rows, face_small, send_sem, recv_sem
):
    place, barrier = greet(sizes)
    rounded = features[...].astype(bf16)
    own = nn(rounded, w_neighbor[...]).astype(bf16)
    proj[...] = own
    center[...] = nn(rounded, w_center[...]).astype(bf16)
    square[...] = jnp.zeros((128, 128), f32)
    square[0:3, 0:ATOMS] = positions[...]
    parts = jnp.concatenate(list(pieces(square[0:8, :])), axis=0)
    parts = jnp.concatenate([parts, jnp.zeros((8, 128), f32)], axis=0).astype(bf16)
    held[0:ATOMS, :] = own
    held[ATOMS:128, :] = jnp.zeros((128 - ATOMS, WIDTH), bf16)
    listed[...] = jnp.full((32, 128), -1.0, f32)
    listed[0:27, 0:GHOST] = lists[...].astype(f32)
    square[0:32, :] = listed[...]
    by_entry = square[...].T
    wide = lanes_of((128, 128)).astype(f32)
    which = rows_of((8, 128))
    for i, (face, cell) in enumerate(zip(FACES, FACE_CELLS)):
        chosen = jnp.where(by_entry[:, cell : cell + 1] == wide, 1.0, 0.0).astype(bf16)
        face_rows[i] = nn(chosen[0:GHOST], held[...]).astype(bf16)
        moved = nt(parts, chosen)
        packed = moved[0:8] + moved[8:16] + moved[16:24]
        axis = [a for a in range(3) if face[a]][0]
        for d, c in zip(DIRECTIONS, CELLS):
            first = 1 if d[1] else 2 if d[2] else 0
            if first != axis or d[first] != face[first] or first == 0:
                continue
            r, half = divmod(list_slot(d), 2)
            entries = jnp.broadcast_to(listed[c : c + 1, :], (8, 128))
            if half:
                entries = pltpu.roll(entries, 64, 1)
            lane = lanes_of((8, 128))
            here = (which == LIST_ROW + r) & ((lane >= 64) if half else (lane < 64))
            packed = jnp.where(here, entries, packed)
        face_small[i] = packed
    pl.semaphore_wait(barrier, len(PARTNERS))
    send = sender(place, send_sem, recv_sem)
    own, cells = (face_rows, face_small), (rows, small)
    direct = {}
    for i in sorted(range(8), key=lambda i: (i < 2, i)):
        d = DIRECTIONS[i]
        direct[i] = send(at(own, first_face(d), 1), at(cells, i, 1), d)
    steps = ((0, FACES[0]), (1, FACES[1]))
    x_own = [send(at(own, X_FACE + k, 1), at(cells, X_AT[k], 1), d) for k, d in steps]
    onward = []
    for start, count in ((0, 2), (2, 3), (5, 3)):
        arrived(*[direct[i] for i in range(start, start + count)])
        onward += [
            send(at(cells, start, count), at(cells, X_AT[k] + 1 + start, count), d) for k, d in steps
        ]
    arrived(*x_own, *onward)
    sent(*direct.values(), *x_own, *onward)


def send_out(features, positions, lists, w_center, w_neighbor, sizes):
    vmem = pl.BlockSpec(memory_space=pltpu.VMEM)
    return pl.pallas_call(
        functools.partial(out_kernel, sizes),
        out_shape=(
            jax.ShapeDtypeStruct((26, GHOST, WIDTH), bf16),
            jax.ShapeDtypeStruct((26, 8, 128), f32),
            jax.ShapeDtypeStruct((ATOMS, WIDTH), bf16),
            jax.ShapeDtypeStruct((ATOMS, WIDTH), bf16),
        ),
        in_specs=[vmem] * 5,
        out_specs=(vmem,) * 4,
        scratch_shapes=[
            pltpu.VMEM((128, 128), f32),
            pltpu.VMEM((32, 128), f32),
            pltpu.VMEM((128, WIDTH), bf16),
            pltpu.VMEM((6, GHOST, WIDTH), bf16),
            pltpu.VMEM((6, 8, 128), f32),
            pltpu.SemaphoreType.DMA((32,)),
            pltpu.SemaphoreType.DMA((32,)),
        ],
        compiler_params=pltpu.CompilerParams(collective_id=0, has_side_effects=True),
        name="send_out",
    )(features, positions, lists, w_center, w_neighbor)


def back_kernel(
    sizes, grad_t, coord_grad, lists, faces, owner_rows, owner_small, grads, rows, small, from_x, from_x_small,
    total, total_small, send_sem, recv_sem
):
    place, barrier = greet(sizes)
    for k in range(LIST // 128):
        grads[128 * k : 128 * k + 128, :] = grad_t[:, 128 * k : 128 * k + 128].astype(f32).T
    face_col = faces[...].T
    entry, lane = rows_of((GHOST, WIDTH)), lanes_of((8, 128))

    def fill(i):
        start, count = STARTS[i], SIZES[i]
        first = min(start, LIST - GHOST)
        value = grads[first : first + GHOST, :]
        if first < start:
            value = jnp.concatenate(
                [value[start - first : start - first + count], jnp.zeros((GHOST - count, WIDTH), f32)], axis=0
            )
        elif count < GHOST:
            value = jnp.where(entry < count, value, 0.0)
        value = value.astype(bf16)
        k, offset = divmod(start, 128)
        moved = coord_grad[:, 128 * k : 128 * k + 128]
        if offset:
            moved = pltpu.roll(moved, 128 - offset, 1)
        if offset + count > 128:
            after = pltpu.roll(coord_grad[:, 128 * k + 128 : 128 * k + 256], 128 - offset, 1)
            moved = jnp.where(lane < 128 - offset, moved, after)
        moved = jnp.where(lane < count, moved, 0.0)
        if DIRECTIONS[i] not in FACES:
            listed = jnp.where(lane[0:1] < count, lists[i : i + 1, :], -1.0)
            chosen = jnp.where(face_col[:, i : i + 1] == listed, 1.0, 0.0).astype(bf16)
            value = nn(chosen[0:GHOST, 0:GHOST], value).astype(bf16)
            parts = jnp.concatenate(list(pieces(moved)) + [jnp.zeros((8, 128), f32)], axis=0)
            parts = nt(parts.astype(bf16), chosen)
            moved = parts[0:8] + parts[8:16] + parts[16:24]
        rows[i] = value
        small[i] = moved

    for i in range(8, 26):
        fill(i)
    pl.semaphore_wait(barrier, len(PARTNERS))
    send = sender(place, send_sem, recv_sem)
    given, sums, owners = (rows, small), (total, total_small), (owner_rows, owner_small)
    steps = ((0, FACES[1]), (1, FACES[0]))
    in_x = [(from_x.at[k], from_x_small.at[k]) for k in (0, 1)]
    x_rest = [send(at(given, X_AT[k] + 3, 6), at(in_x[k], 2, 6), d) for k, d in steps]
    x_pair = [send(at(given, X_AT[k] + 1, 2), at(in_x[k], 0, 2), d) for k, d in steps]
    x_own = [send(at(given, X_AT[k], 1), at(owners, 8 + k, 1), d) for k, d in steps]
    for i in range(8):
        fill(i)
    direct = []
    for group, cells in ((x_rest, range(2, 8)), (x_pair, range(2))):
        arrived(*group)
        for i in cells:
            total[i] = (
                rows[i].astype(f32) + from_x[0, i].astype(f32) + from_x[1, i].astype(f32)
            ).astype(bf16)
            total_small[i] = small[i] + from_x_small[0, i] + from_x_small[1, i]
            d = tuple(-t for t in DIRECTIONS[i])
            direct.append(send(at(sums, i, 1), at(owners, i, 1), d))
    arrived(*x_own, *direct)
    sent(*x_rest, *x_pair, *x_own, *direct)


def send_back(grad_t, coord_grad, lists, faces, sizes):
    vmem = pl.BlockSpec(memory_space=pltpu.VMEM)
    return pl.pallas_call(
        functools.partial(back_kernel, sizes),
        out_shape=(
            jax.ShapeDtypeStruct((10, GHOST, WIDTH), bf16),
            jax.ShapeDtypeStruct((10, 8, 128), f32),
        ),
        in_specs=[vmem] * 4,
        out_specs=(vmem,) * 2,
        scratch_shapes=[
            pltpu.VMEM((LIST, WIDTH), f32),
            pltpu.VMEM((26, GHOST, WIDTH), bf16),
            pltpu.VMEM((26, 8, 128), f32),
            pltpu.VMEM((2, 8, GHOST, WIDTH), bf16),
            pltpu.VMEM((2, 8, 8, 128), f32),
            pltpu.VMEM((8, GHOST, WIDTH), bf16),
            pltpu.VMEM((8, 8, 128), f32),
            pltpu.SemaphoreType.DMA((28,)),
            pltpu.SemaphoreType.DMA((28,)),
        ],
        compiler_params=pltpu.CompilerParams(collective_id=1, has_side_effects=True),
        name="send_back",
    )(grad_t, coord_grad, lists, faces)


R_INDEX, R_ENV, R_SCALED, R_SCALE, R_SLOPE, R_U, R_INV, R_Y, R_BESS, R_BESS_D = 0, 1, 2, 3, 4, 5, 8, 9, 17, 25
R_COUNT = 33


def geometry(index, rx, ry, rz, live, scale):
    squared = rx * rx + ry * ry + rz * rz
    distance = jnp.sqrt(squared)
    inverse = 1.0 / distance
    ux, uy, uz = rx * inverse, ry * inverse, rz * inverse
    x = distance * (1.0 / CUT)
    x2 = x * x
    x5 = x2 * x2 * x
    x6 = x5 * x
    inside = jnp.where(x < 1.0, live, 0.0)
    env = inside * (1.0 + x6 * (-28.0 + x * (48.0 - 21.0 * x)))
    slope = inside * (x5 * (-168.0 + x * (336.0 - 168.0 * x))) * (1.0 / CUT)
    s3, s5, s15 = math.sqrt(3.0), math.sqrt(5.0), math.sqrt(15.0)
    ys = [
        s3 * ux,
        s3 * uy,
        s3 * uz,
        s15 * ux * uy,
        s15 * uy * uz,
        0.5 * s5 * (3.0 * uz * uz - 1.0),
        s15 * ux * uz,
        0.5 * s15 * (ux * ux - uy * uy),
    ]
    theta = distance * (math.pi / CUT)
    sin1, cos1 = jnp.sin(theta), jnp.cos(theta)
    sines, cosines = [jnp.zeros_like(sin1), sin1], [jnp.ones_like(cos1), cos1]
    for _ in range(BASIS - 1):
        sines.append(2.0 * cos1 * sines[-1] - sines[-2])
        cosines.append(2.0 * cos1 * cosines[-1] - cosines[-2])
    norm = math.sqrt(2.0 / CUT)
    bess, bess_d = [], []
    for n in range(1, BASIS + 1):
        value = norm * sines[n] * inverse
        bess.append(value)
        bess_d.append((norm * n * math.pi / CUT * cosines[n] - value) * inverse)
    return [index, env, env * scale, scale, slope, ux, uy, uz, inverse] + ys + bess + bess_d


def edge_blocks(
    per_atom,
    slots,
    table,
    onehot,
    head_proj,
    tail_proj,
    w_env,
    w_latent,
    w_out,
    w_basis,
    env_t,
    latent_t,
    out_t,
    final_col,
    acc,
    acc_tail,
    energy,
):
    width = GROUP * per_atom
    abreast = 1 if per_atom == SLOTS else ABREAST
    lane = lanes_of((GROUP, 128))

    def chunks_of(q):
        atoms = [slots[q, pl.ds(j, GROUP, stride=GROUP), :] for j in range(GROUP)]
        if per_atom == SLOTS:
            return atoms
        out = []
        for g in (0, 4):
            a0 = atoms[g]
            a1 = pltpu.roll(atoms[g + 1], 96, 1)
            a2 = pltpu.roll(atoms[g + 2], 64, 1)
            a3 = pltpu.roll(atoms[g + 3], 32, 1)
            out += [
                jnp.where(lane < 96, a0, a1),
                jnp.where(lane < 64, a1, a2),
                jnp.where(lane < 32, a2, a3),
            ]
        return out

    packed = [jnp.concatenate(chunks_of(q), axis=1) for q in range(6)]
    for q, value in enumerate(geometry(*packed)):
        for k in range(width // 128):
            table[k, q * GROUP : (q + 1) * GROUP, :] = value[:, 128 * k : 128 * k + 128]

    acc[...] = jnp.zeros(acc.shape, f32)

    wide = (GROUP, width)
    first_lane = rows_of(wide) * per_atom
    mask = (lanes_of(wide) >= first_lane) & (lanes_of(wide) < first_lane + per_atom)
    maskf = jnp.where(mask, 1.0, 0.0).astype(f32)

    deg = rows_of((3 * CHANNELS, 80)) // CHANNELS
    comp = lanes_of((3 * CHANNELS, 80)) // GROUP
    allowed = (
        ((deg == 0) & (comp == 0))
        | ((deg == 1) & (comp >= 1) & (comp <= 3))
        | ((deg == 2) & (comp >= 4) & (comp <= 8))
    )

    def block(b, onehot):
        def value(q):
            parts = [table[k, pl.ds(q * GROUP + b, 1), :] for k in range(width // 128)]
            return jnp.concatenate(parts, axis=1)

        def eight(q):
            place = pl.ds(q * GROUP + b, GROUP, stride=GROUP)
            return jnp.concatenate([table[k, place, :] for k in range(width // 128)], axis=1)

        index = value(R_INDEX).astype(i32)
        env = value(R_ENV)
        bess = eight(R_BESS)
        tile = (16, width)
        apart = (jnp.broadcast_to(index, tile) - rows_of(tile)).astype(jnp.int16)
        for h in range(BASIS_AT // 16):
            onehot[16 * h : 16 * h + 16, 0:width] = jnp.where(
                apart == jnp.int16(16 * h), jnp.ones(tile, bf16), jnp.zeros(tile, bf16)
            )
        last = jnp.where(index == rows_of(wide) + (BASIS_AT - 8), 1.0, 0.0)
        onehot[BASIS_AT - 8 : BASIS_AT + 8, 0:width] = jnp.concatenate([last, bess], axis=0).astype(bf16)
        onehot[CENTER_AT:LIST, 0:width] = jnp.concatenate(
            [maskf, jnp.zeros(wide, f32)], axis=0
        ).astype(bf16)
        hot = onehot[:, 0:width]

        yield
        pre = nn(jnp.concatenate([head_proj[...], tail_proj[b]], axis=1), hot)
        sig = sigmoid(pre)
        act = pre * sig
        act_d = sig + act * (1.0 - sig)
        latent = env * act
        latent_h = latent.astype(bf16)
        yield
        weights = nn(env_t[...], latent_h)
        weights_h = weights.astype(bf16)
        ys = eight(R_Y)
        harm = jnp.concatenate(
            [maskf]
            + [maskf * ys[m : m + 1] for m in range(8)]
            + [jnp.zeros(wide, f32)],
            axis=0,
        ).astype(bf16)
        yield
        around = jnp.where(allowed, ENV_NORM * nt(weights_h, harm), 0.0)
        around_h = around.astype(bf16)
        yield
        tensor = nn(around_h, harm)
        scalars_h = (weights * tensor).astype(bf16)
        yield
        mixed = nn(latent_t[...], jnp.concatenate([latent_h, scalars_h], axis=0))
        sig = sigmoid(mixed)
        update = mixed * sig
        update_d = sig + update * (1.0 - sig)
        refined_h = (latent + env * update).astype(bf16)
        yield
        hidden = nn(out_t[...], refined_h)
        sig = sigmoid(hidden)
        hidden_act = hidden * sig
        final = final_col[:, 0:1]
        per_edge = jnp.sum(hidden_act * final, axis=0, keepdims=True)
        energy[pl.ds(pl.multiple_of(b * GROUP, GROUP), GROUP), :] = jnp.broadcast_to(
            jnp.sum(maskf * (env * per_edge), axis=1, keepdims=True), (GROUP, 128)
        )

        scaled = value(R_SCALED)
        d_hidden = ((sig + hidden_act * (1.0 - sig)) * final * scaled).astype(bf16)
        yield
        d_refined = nn(w_out[...], d_hidden)
        d_env = value(R_SCALE) * per_edge
        d_env += jnp.sum(d_refined * update, axis=0, keepdims=True)
        d_mixed = (env * d_refined * update_d).astype(bf16)
        yield
        d_both = nn(w_latent[...], d_mixed)
        d_scalars = d_both[WIDTH:]
        d_tensor_h = (d_scalars * weights).astype(bf16)
        yield
        d_around = jnp.where(allowed, ENV_NORM * nt(d_tensor_h, harm), 0.0)
        yield
        d_weights = d_scalars * tensor + nn(d_around.astype(bf16), harm)
        yield
        d_latent = d_refined + d_both[0:WIDTH] + nn(w_env[...], d_weights.astype(bf16))
        d_env += jnp.sum(d_latent * act, axis=0, keepdims=True)
        d_pre = (env * d_latent * act_d).astype(bf16)
        yield
        d_bess = nn(w_basis[...], d_pre)
        both = jnp.concatenate([around.T, d_around.T], axis=1).astype(bf16)
        d_harm = nn(both, jnp.concatenate([d_tensor_h, weights_h], axis=0))
        dy = [
            jnp.sum(maskf * d_harm[m * GROUP : (m + 1) * GROUP], axis=0, keepdims=True)
            for m in range(1, 9)
        ]

        ux, uy, uz, inverse = (value(q) for q in (R_U, R_U + 1, R_U + 2, R_INV))
        d_dist = d_env * value(R_SLOPE) + jnp.sum(d_bess * eight(R_BESS_D), axis=0, keepdims=True)
        s3, s5, s15 = math.sqrt(3.0), math.sqrt(5.0), math.sqrt(15.0)
        gx = s3 * dy[0] + s15 * (uy * dy[3] + uz * dy[6] + ux * dy[7])
        gy = s3 * dy[1] + s15 * (ux * dy[3] + uz * dy[4] - uy * dy[7])
        gz = s3 * dy[2] + s15 * (uy * dy[4] + ux * dy[6]) + 3.0 * s5 * uz * dy[5]
        along = d_dist - inverse * (gx * ux + gy * uy + gz * uz)
        d_rel = [inverse * g + along * u for g, u in ((gx, ux), (gy, uy), (gz, uz))]
        place = rows_of(wide)
        moved = jnp.where(place == 0, d_rel[0], 0.0)
        moved = jnp.where(place == 1, d_rel[1], moved)
        moved = jnp.where(place == 2, d_rel[2], moved)
        high = moved.astype(bf16).astype(f32)
        moved_h = jnp.concatenate([high, moved - high], axis=0).astype(bf16)
        yield
        spread = nt(jnp.concatenate([d_pre, moved_h], axis=0), hot)
        acc[...] += spread[:, 0:HEAD]
        acc_tail[b] = spread[:, HEAD:]

    def several(i, carry):
        running = [(k, block(abreast * i + k, onehot.at[k])) for k in range(abreast)]
        tick = 0
        while running:
            running = [
                r for r in running if tick < SKEW * r[0] or next(r[1], 0) is None
            ]
            tick += 1
        return carry

    lax.fori_loop(0, ATOMS // GROUP // abreast, several, 0)


def edge_kernel(
    received,
    received_small,
    proj,
    center,
    positions,
    species,
    neighbor,
    live_in,
    kind_scale,
    kind_shift,
    w_basis,
    env_t,
    w_latent,
    w_out,
    w_final,
    energy_out,
    grad_t,
    coord_grad,
    lists,
    faces,
    own_proj_grad,
    center_grad,
    own_pos_grad,
    rows,
    coords,
    head_proj,
    tail_proj,
    env_back,
    latent_t,
    out_t,
    final_col,
    slots,
    table,
    onehot,
    acc,
    acc_tail,
    energy,
):
    rows[0:ATOMS, :] = proj[...].astype(f32)
    lane = lanes_of((8, 128))
    lists[...] = jnp.full((128, 128), -1.0, f32)
    faces[...] = jnp.full((128, 128), -2.0, f32)
    corner = [i for i in range(26) if DIRECTIONS[i] not in FACES]
    for i in corner:
        r, half = divmod(list_slot(DIRECTIONS[i]), 2)
        entries = received_small[i, LIST_ROW + r : LIST_ROW + r + 1, :]
        lists[i : i + 1, :] = pltpu.roll(entries, 64, 1) if half else entries
        r = LIST_ROW + FACE_LIST // 2
        faces[i : i + 1, :] = jnp.where(lane[0:1] < GHOST, received_small[i, r : r + 1, :], -2.0)
    entry_col = lists[...].T
    chosen = {
        i: jnp.where(entry_col[:, i : i + 1] == faces[i : i + 1, :], 1.0, 0.0).astype(bf16) for i in corner
    }
    for i in range(26):
        if i in chosen:
            value = nn(chosen[i][0:GHOST, 0:GHOST], received[i])
        else:
            value = received[i].astype(f32)
        rows[STARTS[i] : STARTS[i] + SIZES[i], :] = value[0 : SIZES[i]]
    rows[BASIS_AT:CENTER_AT, :] = w_basis[...].astype(f32)
    rows[CENTER_AT:LIST, :] = jnp.zeros((LIST - CENTER_AT, WIDTH), f32)
    for k in range(HEAD // 128):
        head_proj[:, 128 * k : 128 * k + 128] = rows[128 * k : 128 * k + 128, :].T.astype(bf16)
    for b in range(ATOMS // GROUP):
        rows[CENTER_AT : CENTER_AT + GROUP, :] = center[...].astype(f32)[GROUP * b : GROUP * b + GROUP]
        tail_proj[b] = rows[HEAD:LIST, :].T.astype(bf16)

    coords[...] = jnp.zeros(coords.shape, f32)
    coords[0:3, 0:ATOMS] = positions[...]
    filled = [coords[0:8, 128 * k : 128 * k + 128] for k in range(8)]
    which = rows_of((8, 128))
    for i, d in enumerate(DIRECTIONS):
        value = received_small[i]
        if i in chosen:
            parts = jnp.concatenate(list(pieces(value)) + [jnp.zeros((8, 128), f32)], axis=0)
            parts = nt(parts.astype(bf16), chosen[i])
            value = parts[0:8] + parts[8:16] + parts[16:24]
        step = [t * SIDE * SPACING for t in d]
        shift = jnp.where(which == 0, step[0], jnp.where(which == 1, step[1], step[2]))
        value = value - shift
        k, at = divmod(STARTS[i], 128)
        end = at + SIZES[i]
        value = pltpu.roll(value, at, 1) if at else value
        filled[k] = jnp.where((lane >= at) & (lane < end), value, filled[k])
        if end > 128:
            filled[k + 1] = jnp.where(lane < end - 128, value, filled[k + 1])

    env_back[...] = env_t[...].astype(f32).T.astype(bf16)
    latent_t[...] = w_latent[...].astype(f32).T.astype(bf16)
    out_t[...] = w_out[...].astype(f32).T.astype(bf16)
    final_col[...] = jnp.broadcast_to(column(w_final[...], OUT_WIDTH), (OUT_WIDTH, 128))

    kinds = species[...]
    scale_row = jnp.where(
        kinds == 0,
        kind_scale[0],
        jnp.where(kinds == 1, kind_scale[1], jnp.where(kinds == 2, kind_scale[2], kind_scale[3])),
    )
    shift_row = jnp.where(
        kinds == 0,
        kind_shift[0],
        jnp.where(kinds == 1, kind_shift[1], jnp.where(kinds == 2, kind_shift[2], kind_shift[3])),
    )

    full = (ATOMS, SLOTS)
    local = neighbor[...]
    ghost = local - ATOMS
    cell = jnp.where(ghost < 0, 13, (ghost * 1366) >> 16)
    jump = jnp.zeros((8, 128), i32)
    for i, c in enumerate(CELLS):
        jump = jnp.where(lane == c, STARTS[i] - ATOMS - GHOST * c, jump)
    jump = jnp.concatenate([jump] * 8, axis=0)
    index = local + jnp.take_along_axis(jump, cell, axis=1, mode="promise_in_bounds")
    low, page = index & 127, index >> 7
    rel = []
    for a in range(3):
        found = jnp.zeros(full, f32)
        for k in range(8):
            source = jnp.broadcast_to(filled[k][a : a + 1, :], full)
            taken = jnp.take_along_axis(source, low, axis=1, mode="promise_in_bounds")
            found = jnp.where(page == k, taken, found)
        rel.append(found - column(positions[a : a + 1, :], ATOMS))
    distance = jnp.sqrt(rel[0] * rel[0] + rel[1] * rel[1] + rel[2] * rel[2])
    live = jnp.where(distance * (1.0 / CUT) < 1.0, live_in[...], 0)

    before = jnp.where(rows_of((SLOTS, SLOTS)) < lanes_of((SLOTS, SLOTS)), 1.0, 0.0).astype(bf16)
    gap = nn((1 - live).astype(f32).astype(bf16), before).astype(i32)
    most = jnp.max(jnp.sum(live.astype(f32), axis=1, keepdims=True))
    values = [index] + rel
    for step in range(7):
        by = 1 << step
        moves = jnp.where((gap & by) != 0, live, 0)
        come = pltpu.roll(moves, SLOTS - by, 1) != 0
        values = [jnp.where(come, pltpu.roll(v, SLOTS - by, 1), v) for v in values]
        gap = jnp.where(come, pltpu.roll(gap, SLOTS - by, 1), gap)
        live = jnp.where(come, 1, live - moves)
    kept = live != 0
    slots[0] = jnp.where(kept, values[0], LIST - 1).astype(f32)
    slots[1] = jnp.where(kept, values[1], 0.5 * CUT)
    slots[2] = jnp.where(kept, values[2], 0.0)
    slots[3] = jnp.where(kept, values[3], 0.0)
    slots[4] = live.astype(f32)
    slots[5] = jnp.broadcast_to(column(scale_row, ATOMS), full)

    shared = (
        slots,
        table,
        onehot,
        head_proj,
        tail_proj,
        env_back,
        w_latent,
        w_out,
        w_basis,
        env_t,
        latent_t,
        out_t,
        final_col,
        acc,
        acc_tail,
        energy,
    )

    @pl.when(most <= 96.0)
    def _():
        edge_blocks(96, *shared)

    @pl.when(most > 96.0)
    def _():
        edge_blocks(SLOTS, *shared)

    energy_out[...] = scale_row * row(energy[:, 0:1], ATOMS) + shift_row

    tail = acc_tail[0]
    for b in range(1, ATOMS // GROUP):
        tail = tail + acc_tail[b]
    grad_t[:, 0:HEAD] = acc[0:WIDTH, :].astype(bf16)
    grad_t[:, HEAD:LIST] = tail[0:WIDTH].astype(bf16)
    high, rest = slice(WIDTH, WIDTH + 8), slice(WIDTH + 8, WIDTH + 16)
    coord_grad[:, 0:HEAD] = acc[high, :] + acc[rest, :]
    coord_grad[:, HEAD:LIST] = tail[high] + tail[rest]
    wide = lanes_of((WIDTH + 16, 128))
    pulled = jnp.zeros((WIDTH + 16, 128), f32)
    for b in range(ATOMS // GROUP):
        value = pltpu.roll(acc_tail[b], (GROUP * b - (CENTER_AT - HEAD)) % 128, 1)
        pulled = jnp.where((wide >= GROUP * b) & (wide < GROUP * b + GROUP), value, pulled)
    center_grad[...] = pulled[0:WIDTH].T[0:ATOMS]
    own_proj_grad[...] = acc[0:WIDTH, 0:128].T[0:ATOMS]
    own_pos_grad[...] = jnp.where(lane < ATOMS, coord_grad[:, 0:128] - pulled[high] - pulled[rest], 0.0)


def edges(received, received_small, proj, center, positions, species, neighbor, live, scale, shift, *weights):
    vmem = pl.BlockSpec(memory_space=pltpu.VMEM)
    smem = pl.BlockSpec(memory_space=pltpu.SMEM)
    return pl.pallas_call(
        edge_kernel,
        out_shape=(
            jax.ShapeDtypeStruct((1, ATOMS), f32),
            jax.ShapeDtypeStruct((WIDTH, LIST), bf16),
            jax.ShapeDtypeStruct((8, LIST), f32),
            jax.ShapeDtypeStruct((128, 128), f32),
            jax.ShapeDtypeStruct((128, 128), f32),
            jax.ShapeDtypeStruct((ATOMS, WIDTH), f32),
            jax.ShapeDtypeStruct((ATOMS, WIDTH), f32),
            jax.ShapeDtypeStruct((8, 128), f32),
        ),
        in_specs=[vmem] * 8 + [smem] * 2 + [vmem] * 5,
        out_specs=(vmem,) * 8,
        scratch_shapes=[
            pltpu.VMEM((LIST, WIDTH), f32),
            pltpu.VMEM((8, LIST), f32),
            pltpu.VMEM((WIDTH, HEAD), bf16),
            pltpu.VMEM((8, WIDTH, 128), bf16),
            pltpu.VMEM((WIDTH, 3 * CHANNELS), bf16),
            pltpu.VMEM((WIDTH, WIDTH + 3 * CHANNELS), bf16),
            pltpu.VMEM((OUT_WIDTH, WIDTH), bf16),
            pltpu.VMEM((OUT_WIDTH, 128), f32),
            pltpu.VMEM((6, ATOMS, SLOTS), f32),
            pltpu.VMEM((8, R_COUNT * GROUP, 128), f32),
            pltpu.VMEM((ABREAST, LIST, GROUP * SLOTS), bf16),
            pltpu.VMEM((WIDTH + 16, HEAD), f32),
            pltpu.VMEM((8, WIDTH + 16, 128), f32),
            pltpu.VMEM((ATOMS, 128), f32),
        ],
        compiler_params=pltpu.CompilerParams(vmem_limit_bytes=56 * 1024 * 1024),
        name="edges",
    )(
        received, received_small, proj, center, positions, species, neighbor, live, scale, shift, *weights
    )


def unpack_kernel(
    face_rows, face_small, own_proj_grad, center_grad, own_pos_grad, lists, w_center, w_neighbor, forces,
    feature_grad, padded
):
    padded[...] = jnp.full((32, 128), -1, i32)
    padded[0:27, 0:GHOST] = lists[...]
    proj_grad = own_proj_grad[...]
    pos_grad = jnp.zeros((32, ATOMS), f32)
    atom = rows_of((ATOMS, 128))
    for i, d in enumerate(DIRECTIONS[0:8] + FACES[0:2]):
        cell = FACE_CELLS[first_face(d)]
        chosen = jnp.where(padded[cell : cell + 1, :] == atom, 1.0, 0.0).astype(bf16)
        proj_grad = proj_grad + nn(chosen[:, 0:GHOST], face_rows[i])
        parts = jnp.concatenate(list(pieces(face_small[i])) + [jnp.zeros((8, 128), f32)], axis=0)
        pos_grad = pos_grad + nt(parts.astype(bf16), chosen)
    feature_grad[...] = nt(proj_grad.astype(bf16), w_neighbor[...]) + nt(
        center_grad[...].astype(bf16), w_center[...]
    )
    total = own_pos_grad[:, 0:ATOMS] + pos_grad[0:8] + pos_grad[8:16] + pos_grad[16:24]
    forces[...] = -total[0:3]


def unpack(*args):
    vmem = pl.BlockSpec(memory_space=pltpu.VMEM)
    return pl.pallas_call(
        unpack_kernel,
        out_shape=(
            jax.ShapeDtypeStruct((3, ATOMS), f32),
            jax.ShapeDtypeStruct((ATOMS, WIDTH), f32),
        ),
        in_specs=[vmem] * 8,
        out_specs=(vmem,) * 2,
        scratch_shapes=[pltpu.VMEM((32, 128), i32)],
        name="unpack",
    )(*args)


def solution(mesh):
    sizes = tuple(mesh.shape[a] for a in ("gx", "gy", "gz"))

    def local(
        positions,
        atom_features,
        species,
        edge_neighbor,
        edge_live,
        send_list,
        species_scale,
        species_shift,
        w_center,
        w_neighbor,
        w_basis,
        w_env,
        w_latent,
        w_out,
        w_final,
    ):
        received, received_small, proj, center = send_out(
            atom_features, positions, send_list, w_center, w_neighbor, sizes
        )
        energy, grad_t, coord_grad, lists, faces, own_proj_grad, center_grad, own_pos_grad = edges(
            received,
            received_small,
            proj,
            center,
            positions,
            species.reshape(1, ATOMS),
            edge_neighbor,
            edge_live,
            species_scale,
            species_shift,
            w_basis,
            w_env.T,
            w_latent,
            w_out,
            w_final.reshape(1, OUT_WIDTH),
        )
        owner_rows, owner_small = send_back(grad_t, coord_grad, lists, faces, sizes)
        forces, feature_grad = unpack(
            owner_rows, owner_small, own_proj_grad, center_grad, own_pos_grad, send_list, w_center, w_neighbor
        )
        return energy.reshape(ATOMS), forces, feature_grad

    split = ("gx", "gy", "gz")
    return jax.shard_map(
        local,
        mesh=mesh,
        in_specs=(P(None, split), P(split, None), P(split), P(split, None), P(split, None), P(split, None))
        + (P(),) * 9,
        out_specs=(P(split), P(None, split), P(split, None)),
        check_vma=False,
    )
```

```python
import functools
import math

import jax
import jax.numpy as jnp
from jax import lax
from jax.experimental import pallas as pl
from jax.experimental.pallas import tpu as pltpu
from jax.sharding import PartitionSpec as P

SIDE = 4
REACH = 3
SPACING = 2.15
CUT = 6.0
ENV_NORM = 0.125
ATOMS = 64
SLOTS = 128
GHOST = 48
WIDTH = 256
CHANNELS = 64
OUT_WIDTH = 128
BASIS = 8
LIST = 1024
HEAD = 896
BASIS_AT = 1000
CENTER_AT = 1008
GROUP = 8
ROWS = 16
ABREAST = 4
SKEW = 1

f32 = jnp.float32
bf16 = jnp.bfloat16
i32 = jnp.int32

FACES = [(-1, 0, 0), (1, 0, 0), (0, -1, 0), (0, 1, 0), (0, 0, -1), (0, 0, 1)]
X_FACE, Y_FACE, Z_FACE = 0, 2, 4
Y_CELLS = [(0, -1, 0), (0, 1, 0)]
Z_CELLS = [(0, ty, tz) for tz in (-1, 1) for ty in (0, -1, 1)]
X_CELLS = [
    (tx,) + behind for tx in (-1, 1) for behind in [(0, 0)] + [c[1:] for c in Y_CELLS + Z_CELLS]
]
DIRECTIONS = Y_CELLS + Z_CELLS + X_CELLS
Z_AT, X_AT = (2, 5), (8, 17)
CELLS = [9 * (tx + 1) + 3 * (ty + 1) + tz + 1 for tx, ty, tz in DIRECTIONS]
SIZES = [math.prod(REACH if t else SIDE for t in d) for d in DIRECTIONS]
STARTS = [ATOMS + sum(SIZES[:i]) for i in range(26)]
assert STARTS[-1] + SIZES[-1] == BASIS_AT
FACE_CELLS = [9 * (tx + 1) + 3 * (ty + 1) + tz + 1 for tx, ty, tz in FACES]
LIST_ROW = 3
FACE_LIST = 4


def list_slot(direction):
    tx, ty, tz = direction
    return 3 * (tx + 1) + (tz + 1 if ty else 1)


def nn(a, b):
    return jnp.dot(a, b, preferred_element_type=f32)


def nt(a, b):
    return lax.dot_general(a, b, (((1,), (1,)), ((), ())), preferred_element_type=f32)


def lanes_of(shape):
    return lax.broadcasted_iota(i32, shape, len(shape) - 1)


def rows_of(shape):
    return lax.broadcasted_iota(i32, shape, 0)


def column(row, size):
    shape = (size, size)
    on = rows_of(shape) == lanes_of(shape)
    return jnp.sum(jnp.where(on, jnp.broadcast_to(row, shape), 0.0), axis=1, keepdims=True)


def row(col, size):
    shape = (size, size)
    on = rows_of(shape) == lanes_of(shape)
    return jnp.sum(jnp.where(on, jnp.broadcast_to(col, shape), 0.0), axis=0, keepdims=True)


def pieces(value):
    high = value.astype(bf16).astype(f32)
    rest = value - high
    middle = rest.astype(bf16).astype(f32)
    low = (rest - middle).astype(bf16).astype(f32)
    return high, middle, low


def sigmoid(x):
    return 0.5 * jnp.tanh(0.5 * x) + 0.5


PARTNERS = Y_CELLS + Z_CELLS + FACES[0:2]


def greet(sizes):
    here = [lax.axis_index(a) for a in ("gx", "gy", "gz")]

    def place(direction):
        return tuple(lax.rem(h + (t + n), n) if t else h for h, t, n in zip(here, direction, sizes))

    barrier = pltpu.get_barrier_semaphore()
    for d in PARTNERS:
        pl.semaphore_signal(barrier, inc=1, device_id=place(d), device_id_type=pl.DeviceIdType.MESH)
    return place, barrier


def sender(place, send_sem, recv_sem):
    count = [0]

    def send(sources, targets, direction):
        started = []
        for source, target in zip(sources, targets):
            k = count[0]
            count[0] += 1
            copy = pltpu.make_async_remote_copy(
                src_ref=source,
                dst_ref=target,
                send_sem=send_sem.at[k],
                recv_sem=recv_sem.at[k],
                device_id=place(direction),
                device_id_type=pl.DeviceIdType.MESH,
            )
            copy.start()
            started.append(copy)
        return started

    return send


def arrived(*groups):
    for group in groups:
        for copy in group:
            copy.wait_recv()


def sent(*groups):
    for group in groups:
        for copy in group:
            copy.wait_send()


def at(refs, start, count):
    return [r.at[pl.ds(start, count)] for r in refs]


def first_face(direction):
    tx, ty, tz = direction
    return Y_FACE + (ty + 1) // 2 if ty else Z_FACE + (tz + 1) // 2 if tz else X_FACE + (tx + 1) // 2


def out_kernel(
    sizes, features, positions, lists, w_center, w_neighbor, rows, small, proj, center, square, listed, held,
    face_rows, face_small, send_sem, recv_sem
):
    place, barrier = greet(sizes)
    rounded = features[...].astype(bf16)
    own = nn(rounded, w_neighbor[...]).astype(bf16)
    proj[...] = own
    center[...] = nn(rounded, w_center[...]).astype(bf16)
    square[...] = jnp.zeros((128, 128), f32)
    square[0:3, 0:ATOMS] = positions[...]
    parts = jnp.concatenate(list(pieces(square[0:8, :])), axis=0)
    parts = jnp.concatenate([parts, jnp.zeros((8, 128), f32)], axis=0).astype(bf16)
    held[0:ATOMS, :] = own
    held[ATOMS:128, :] = jnp.zeros((128 - ATOMS, WIDTH), bf16)
    listed[...] = jnp.full((32, 128), -1.0, f32)
    listed[0:27, 0:GHOST] = lists[...].astype(f32)
    square[0:32, :] = listed[...]
    by_entry = square[...].T
    wide = lanes_of((128, 128)).astype(f32)
    which = rows_of((8, 128))
    for i, (face, cell) in enumerate(zip(FACES, FACE_CELLS)):
        chosen = jnp.where(by_entry[:, cell : cell + 1] == wide, 1.0, 0.0).astype(bf16)
        face_rows[i] = nn(chosen[0:GHOST], held[...]).astype(bf16)
        moved = nt(parts, chosen)
        packed = moved[0:8] + moved[8:16] + moved[16:24]
        axis = [a for a in range(3) if face[a]][0]
        for d, c in zip(DIRECTIONS, CELLS):
            first = 1 if d[1] else 2 if d[2] else 0
            if first != axis or d[first] != face[first] or first == 0:
                continue
            r, half = divmod(list_slot(d), 2)
            entries = jnp.broadcast_to(listed[c : c + 1, :], (8, 128))
            if half:
                entries = pltpu.roll(entries, 64, 1)
            lane = lanes_of((8, 128))
            here = (which == LIST_ROW + r) & ((lane >= 64) if half else (lane < 64))
            packed = jnp.where(here, entries, packed)
        face_small[i] = packed
    pl.semaphore_wait(barrier, len(PARTNERS))
    send = sender(place, send_sem, recv_sem)
    own, cells = (face_rows, face_small), (rows, small)
    direct = {}
    for i in sorted(range(8), key=lambda i: (i < 2, i)):
        d = DIRECTIONS[i]
        direct[i] = send(at(own, first_face(d), 1), at(cells, i, 1), d)
    steps = ((0, FACES[0]), (1, FACES[1]))
    x_own = [send(at(own, X_FACE + k, 1), at(cells, X_AT[k], 1), d) for k, d in steps]
    onward = []
    for i in (0, 1, 2, 5, 3, 4, 6, 7):
        arrived(direct[i])
        onward += [send(at(cells, i, 1), at(cells, X_AT[k] + 1 + i, 1), d) for k, d in steps]
    arrived(*x_own, *onward)
    sent(*direct.values(), *x_own, *onward)


def send_out(features, positions, lists, w_center, w_neighbor, sizes):
    vmem = pl.BlockSpec(memory_space=pltpu.VMEM)
    return pl.pallas_call(
        functools.partial(out_kernel, sizes),
        out_shape=(
            jax.ShapeDtypeStruct((26, GHOST, WIDTH), bf16),
            jax.ShapeDtypeStruct((26, 8, 128), f32),
            jax.ShapeDtypeStruct((ATOMS, WIDTH), bf16),
            jax.ShapeDtypeStruct((ATOMS, WIDTH), bf16),
        ),
        in_specs=[vmem] * 5,
        out_specs=(vmem,) * 4,
        scratch_shapes=[
            pltpu.VMEM((128, 128), f32),
            pltpu.VMEM((32, 128), f32),
            pltpu.VMEM((128, WIDTH), bf16),
            pltpu.VMEM((6, GHOST, WIDTH), bf16),
            pltpu.VMEM((6, 8, 128), f32),
            pltpu.SemaphoreType.DMA((52,)),
            pltpu.SemaphoreType.DMA((52,)),
        ],
        compiler_params=pltpu.CompilerParams(collective_id=0, has_side_effects=True),
        name="send_out",
    )(features, positions, lists, w_center, w_neighbor)


def back_kernel(
    sizes, grad_t, coord_grad, lists, faces, owner_rows, owner_small, grads, rows, small, from_x, from_x_small,
    total, total_small, send_sem, recv_sem
):
    place, barrier = greet(sizes)
    for k in range(LIST // 128):
        grads[128 * k : 128 * k + 128, :] = grad_t[:, 128 * k : 128 * k + 128].astype(f32).T
    face_col = faces[...].T
    entry, lane = rows_of((GHOST, WIDTH)), lanes_of((8, 128))

    def fill(i):
        start, count = STARTS[i], SIZES[i]
        first = min(start, LIST - GHOST)
        value = grads[first : first + GHOST, :]
        if first < start:
            value = jnp.concatenate(
                [value[start - first : start - first + count], jnp.zeros((GHOST - count, WIDTH), f32)], axis=0
            )
        elif count < GHOST:
            value = jnp.where(entry < count, value, 0.0)
        value = value.astype(bf16)
        k, offset = divmod(start, 128)
        moved = coord_grad[:, 128 * k : 128 * k + 128]
        if offset:
            moved = pltpu.roll(moved, 128 - offset, 1)
        if offset + count > 128:
            after = pltpu.roll(coord_grad[:, 128 * k + 128 : 128 * k + 256], 128 - offset, 1)
            moved = jnp.where(lane < 128 - offset, moved, after)
        moved = jnp.where(lane < count, moved, 0.0)
        if DIRECTIONS[i] not in FACES:
            listed = jnp.where(lane[0:1] < count, lists[i : i + 1, :], -1.0)
            chosen = jnp.where(face_col[:, i : i + 1] == listed, 1.0, 0.0).astype(bf16)
            value = nn(chosen[0:GHOST, 0:GHOST], value).astype(bf16)
            parts = jnp.concatenate(list(pieces(moved)) + [jnp.zeros((8, 128), f32)], axis=0)
            parts = nt(parts.astype(bf16), chosen)
            moved = parts[0:8] + parts[8:16] + parts[16:24]
        rows[i] = value
        small[i] = moved

    for i in range(8, 26):
        fill(i)
    pl.semaphore_wait(barrier, len(PARTNERS))
    send = sender(place, send_sem, recv_sem)
    given, sums, owners = (rows, small), (total, total_small), (owner_rows, owner_small)
    steps = ((0, FACES[1]), (1, FACES[0]))
    order = (3, 4, 6, 7, 2, 5, 0, 1)
    x_small = [send([small.at[pl.ds(X_AT[k] + 1, 8)]], [from_x_small.at[k]], d) for k, d in steps]
    x_cells = {
        i: [send([rows.at[X_AT[k] + 1 + i]], [from_x.at[k, i]], d) for k, d in steps] for i in order
    }
    x_own = [send(at(given, X_AT[k], 1), at(owners, 8 + k, 1), d) for k, d in steps]
    for i in range(8):
        fill(i)
    arrived(*x_small)
    for i in range(8):
        total_small[i] = small[i] + from_x_small[0, i] + from_x_small[1, i]
    direct = []
    for i in order:
        arrived(*x_cells[i])
        total[i] = (
            rows[i].astype(f32) + from_x[0, i].astype(f32) + from_x[1, i].astype(f32)
        ).astype(bf16)
        d = tuple(-t for t in DIRECTIONS[i])
        direct.append(send(at(sums, i, 1), at(owners, i, 1), d))
    arrived(*x_own, *direct)
    sent(*x_small, *[c for i in order for c in x_cells[i]], *x_own, *direct)


def send_back(grad_t, coord_grad, lists, faces, sizes):
    vmem = pl.BlockSpec(memory_space=pltpu.VMEM)
    return pl.pallas_call(
        functools.partial(back_kernel, sizes),
        out_shape=(
            jax.ShapeDtypeStruct((10, GHOST, WIDTH), bf16),
            jax.ShapeDtypeStruct((10, 8, 128), f32),
        ),
        in_specs=[vmem] * 4,
        out_specs=(vmem,) * 2,
        scratch_shapes=[
            pltpu.VMEM((LIST, WIDTH), f32),
            pltpu.VMEM((26, GHOST, WIDTH), bf16),
            pltpu.VMEM((26, 8, 128), f32),
            pltpu.VMEM((2, 8, GHOST, WIDTH), bf16),
            pltpu.VMEM((2, 8, 8, 128), f32),
            pltpu.VMEM((8, GHOST, WIDTH), bf16),
            pltpu.VMEM((8, 8, 128), f32),
            pltpu.SemaphoreType.DMA((38,)),
            pltpu.SemaphoreType.DMA((38,)),
        ],
        compiler_params=pltpu.CompilerParams(collective_id=1, has_side_effects=True),
        name="send_back",
    )(grad_t, coord_grad, lists, faces)


R_INDEX, R_ENV, R_SCALED, R_SCALE, R_SLOPE, R_U, R_INV, R_Y, R_BESS, R_BESS_D = 0, 1, 2, 3, 4, 5, 8, 9, 17, 25
R_COUNT = 33


def geometry(index, rx, ry, rz, live, scale):
    squared = rx * rx + ry * ry + rz * rz
    distance = jnp.sqrt(squared)
    inverse = 1.0 / distance
    ux, uy, uz = rx * inverse, ry * inverse, rz * inverse
    x = distance * (1.0 / CUT)
    x2 = x * x
    x5 = x2 * x2 * x
    x6 = x5 * x
    inside = jnp.where(x < 1.0, live, 0.0)
    env = inside * (1.0 + x6 * (-28.0 + x * (48.0 - 21.0 * x)))
    slope = inside * (x5 * (-168.0 + x * (336.0 - 168.0 * x))) * (1.0 / CUT)
    s3, s5, s15 = math.sqrt(3.0), math.sqrt(5.0), math.sqrt(15.0)
    ys = [
        s3 * ux,
        s3 * uy,
        s3 * uz,
        s15 * ux * uy,
        s15 * uy * uz,
        0.5 * s5 * (3.0 * uz * uz - 1.0),
        s15 * ux * uz,
        0.5 * s15 * (ux * ux - uy * uy),
    ]
    theta = distance * (math.pi / CUT)
    sin1, cos1 = jnp.sin(theta), jnp.cos(theta)
    sines, cosines = [jnp.zeros_like(sin1), sin1], [jnp.ones_like(cos1), cos1]
    for _ in range(BASIS - 1):
        sines.append(2.0 * cos1 * sines[-1] - sines[-2])
        cosines.append(2.0 * cos1 * cosines[-1] - cosines[-2])
    norm = math.sqrt(2.0 / CUT)
    bess, bess_d = [], []
    for n in range(1, BASIS + 1):
        value = norm * sines[n] * inverse
        bess.append(value)
        bess_d.append((norm * n * math.pi / CUT * cosines[n] - value) * inverse)
    return [index, env, env * scale, scale, slope, ux, uy, uz, inverse] + ys + bess + bess_d


def by_rows(count, step):
    parts = [step(slice(r, r + ROWS)) for r in range(0, count, ROWS)]
    return tuple(jnp.concatenate(p, axis=0) for p in zip(*parts))


def edge_blocks(
    per_atom,
    slots,
    table,
    onehot,
    head_proj,
    tail_proj,
    w_env,
    w_latent,
    w_out,
    w_basis,
    env_t,
    latent_t,
    out_t,
    final_col,
    acc,
    acc_tail,
    energy,
):
    width = GROUP * per_atom
    abreast = 1 if per_atom == SLOTS else ABREAST
    lane = lanes_of((GROUP, 128))

    def chunks_of(q):
        atoms = [slots[q, pl.ds(j, GROUP, stride=GROUP), :] for j in range(GROUP)]
        if per_atom == SLOTS:
            return atoms
        out = []
        for g in (0, 4):
            a0 = atoms[g]
            a1 = pltpu.roll(atoms[g + 1], 96, 1)
            a2 = pltpu.roll(atoms[g + 2], 64, 1)
            a3 = pltpu.roll(atoms[g + 3], 32, 1)
            out += [
                jnp.where(lane < 96, a0, a1),
                jnp.where(lane < 64, a1, a2),
                jnp.where(lane < 32, a2, a3),
            ]
        return out

    packed = [jnp.concatenate(chunks_of(q), axis=1) for q in range(6)]
    for q, value in enumerate(geometry(*packed)):
        for k in range(width // 128):
            table[k, q * GROUP : (q + 1) * GROUP, :] = value[:, 128 * k : 128 * k + 128]

    acc[...] = jnp.zeros(acc.shape, f32)

    wide = (GROUP, width)
    first_lane = rows_of(wide) * per_atom
    mask = (lanes_of(wide) >= first_lane) & (lanes_of(wide) < first_lane + per_atom)
    maskf = jnp.where(mask, 1.0, 0.0).astype(f32)

    deg = rows_of((3 * CHANNELS, 80)) // CHANNELS
    comp = lanes_of((3 * CHANNELS, 80)) // GROUP
    allowed = (
        ((deg == 0) & (comp == 0))
        | ((deg == 1) & (comp >= 1) & (comp <= 3))
        | ((deg == 2) & (comp >= 4) & (comp <= 8))
    )

    def block(b, onehot):
        def value(q):
            parts = [table[k, pl.ds(q * GROUP + b, 1), :] for k in range(width // 128)]
            return jnp.concatenate(parts, axis=1)

        def eight(q):
            place = pl.ds(q * GROUP + b, GROUP, stride=GROUP)
            return jnp.concatenate([table[k, place, :] for k in range(width // 128)], axis=1)

        index = value(R_INDEX).astype(i32)
        env = value(R_ENV)
        bess = eight(R_BESS)
        tile = (16, width)
        apart = (jnp.broadcast_to(index, tile) - rows_of(tile)).astype(jnp.int16)
        for h in range(BASIS_AT // 16):
            onehot[16 * h : 16 * h + 16, 0:width] = jnp.where(
                apart == jnp.int16(16 * h), jnp.ones(tile, bf16), jnp.zeros(tile, bf16)
            )
        last = jnp.where(index == rows_of(wide) + (BASIS_AT - 8), 1.0, 0.0)
        onehot[BASIS_AT - 8 : BASIS_AT + 8, 0:width] = jnp.concatenate([last, bess], axis=0).astype(bf16)
        onehot[CENTER_AT:LIST, 0:width] = jnp.concatenate(
            [maskf, jnp.zeros(wide, f32)], axis=0
        ).astype(bf16)
        hot = onehot[:, 0:width]

        yield
        pre = nn(jnp.concatenate([head_proj[...], tail_proj[b]], axis=1), hot)

        def first(r):
            sig = sigmoid(pre[r])
            act = pre[r] * sig
            return act, sig + act * (1.0 - sig), (env * act).astype(bf16)

        act, act_d, latent_h = by_rows(WIDTH, first)
        yield
        weights = nn(env_t[...], latent_h)
        (weights_h,) = by_rows(3 * CHANNELS, lambda r: (weights[r].astype(bf16),))
        ys = eight(R_Y)
        harm = jnp.concatenate(
            [maskf]
            + [maskf * ys[m : m + 1] for m in range(8)]
            + [jnp.zeros(wide, f32)],
            axis=0,
        ).astype(bf16)
        yield
        around = jnp.where(allowed, ENV_NORM * nt(weights_h, harm), 0.0)
        around_h = around.astype(bf16)
        yield
        tensor = nn(around_h, harm)
        (scalars_h,) = by_rows(3 * CHANNELS, lambda r: ((weights[r] * tensor[r]).astype(bf16),))
        yield
        mixed = nn(latent_t[...], jnp.concatenate([latent_h, scalars_h], axis=0))

        def second(r):
            sig = sigmoid(mixed[r])
            update = mixed[r] * sig
            return update, sig + update * (1.0 - sig), (env * (act[r] + update)).astype(bf16)

        update, update_d, refined_h = by_rows(WIDTH, second)
        yield
        hidden = nn(out_t[...], refined_h)
        scaled = value(R_SCALED)
        sums = [jnp.zeros((ROWS, width), f32) for _ in range(3)]

        def third(r):
            sig = sigmoid(hidden[r])
            hidden_act = hidden[r] * sig
            final = final_col[r, 0:1]
            sums[0] = sums[0] + hidden_act * final
            return (((sig + hidden_act * (1.0 - sig)) * final * scaled).astype(bf16),)

        (d_hidden,) = by_rows(OUT_WIDTH, third)
        per_edge = jnp.sum(sums[0], axis=0, keepdims=True)
        energy[pl.ds(pl.multiple_of(b * GROUP, GROUP), GROUP), :] = jnp.broadcast_to(
            jnp.sum(maskf * (env * per_edge), axis=1, keepdims=True), (GROUP, 128)
        )

        yield
        d_refined = nn(w_out[...], d_hidden)

        def fourth(r):
            sums[1] = sums[1] + d_refined[r] * update[r]
            return ((env * d_refined[r] * update_d[r]).astype(bf16),)

        (d_mixed,) = by_rows(WIDTH, fourth)
        yield
        d_both = nn(w_latent[...], d_mixed)
        d_scalars = d_both[WIDTH:]
        (d_tensor_h,) = by_rows(3 * CHANNELS, lambda r: ((d_scalars[r] * weights[r]).astype(bf16),))
        yield
        d_around = jnp.where(allowed, ENV_NORM * nt(d_tensor_h, harm), 0.0)
        yield
        around_grad = nn(d_around.astype(bf16), harm)
        (d_weights,) = by_rows(
            3 * CHANNELS, lambda r: ((d_scalars[r] * tensor[r] + around_grad[r]).astype(bf16),)
        )
        yield
        from_weights = nn(w_env[...], d_weights)

        def fifth(r):
            d_latent = d_refined[r] + d_both[r] + from_weights[r]
            sums[2] = sums[2] + d_latent * act[r]
            return ((env * d_latent * act_d[r]).astype(bf16),)

        (d_pre,) = by_rows(WIDTH, fifth)
        d_env = value(R_SCALE) * per_edge + jnp.sum(sums[1] + sums[2], axis=0, keepdims=True)
        yield
        d_bess = nn(w_basis[...], d_pre)
        both = jnp.concatenate([around.T, d_around.T], axis=1).astype(bf16)
        d_harm = nn(both, jnp.concatenate([d_tensor_h, weights_h], axis=0))
        dy = [
            jnp.sum(maskf * d_harm[m * GROUP : (m + 1) * GROUP], axis=0, keepdims=True)
            for m in range(1, 9)
        ]

        ux, uy, uz, inverse = (value(q) for q in (R_U, R_U + 1, R_U + 2, R_INV))
        d_dist = d_env * value(R_SLOPE) + jnp.sum(d_bess * eight(R_BESS_D), axis=0, keepdims=True)
        s3, s5, s15 = math.sqrt(3.0), math.sqrt(5.0), math.sqrt(15.0)
        gx = s3 * dy[0] + s15 * (uy * dy[3] + uz * dy[6] + ux * dy[7])
        gy = s3 * dy[1] + s15 * (ux * dy[3] + uz * dy[4] - uy * dy[7])
        gz = s3 * dy[2] + s15 * (uy * dy[4] + ux * dy[6]) + 3.0 * s5 * uz * dy[5]
        along = d_dist - inverse * (gx * ux + gy * uy + gz * uz)
        d_rel = [inverse * g + along * u for g, u in ((gx, ux), (gy, uy), (gz, uz))]
        place = rows_of(wide)
        moved = jnp.where(place == 0, d_rel[0], 0.0)
        moved = jnp.where(place == 1, d_rel[1], moved)
        moved = jnp.where(place == 2, d_rel[2], moved)
        high = moved.astype(bf16).astype(f32)
        moved_h = jnp.concatenate([high, moved - high], axis=0).astype(bf16)
        yield
        spread = nt(jnp.concatenate([d_pre, moved_h], axis=0), hot)
        acc[...] += spread[:, 0:HEAD]
        acc_tail[b] = spread[:, HEAD:]

    def several(i, carry):
        running = [(k, block(abreast * i + k, onehot.at[k])) for k in range(abreast)]
        tick = 0
        while running:
            running = [
                r for r in running if tick < SKEW * r[0] or next(r[1], 0) is None
            ]
            tick += 1
        return carry

    lax.fori_loop(0, ATOMS // GROUP // abreast, several, 0)


def edge_kernel(
    received,
    received_small,
    proj,
    center,
    positions,
    species,
    neighbor,
    live_in,
    kind_scale,
    kind_shift,
    w_basis,
    env_t,
    w_latent,
    w_out,
    w_final,
    energy_out,
    grad_t,
    coord_grad,
    lists,
    faces,
    own_proj_grad,
    center_grad,
    own_pos_grad,
    rows,
    coords,
    head_proj,
    tail_proj,
    env_back,
    latent_t,
    out_t,
    final_col,
    slots,
    table,
    onehot,
    acc,
    acc_tail,
    energy,
):
    rows[0:ATOMS, :] = proj[...].astype(f32)
    lane = lanes_of((8, 128))
    lists[...] = jnp.full((128, 128), -1.0, f32)
    faces[...] = jnp.full((128, 128), -2.0, f32)
    corner = [i for i in range(26) if DIRECTIONS[i] not in FACES]
    for i in corner:
        r, half = divmod(list_slot(DIRECTIONS[i]), 2)
        entries = received_small[i, LIST_ROW + r : LIST_ROW + r + 1, :]
        lists[i : i + 1, :] = pltpu.roll(entries, 64, 1) if half else entries
        r = LIST_ROW + FACE_LIST // 2
        faces[i : i + 1, :] = jnp.where(lane[0:1] < GHOST, received_small[i, r : r + 1, :], -2.0)
    entry_col = lists[...].T
    chosen = {
        i: jnp.where(entry_col[:, i : i + 1] == faces[i : i + 1, :], 1.0, 0.0).astype(bf16) for i in corner
    }
    for i in range(26):
        if i in chosen:
            value = nn(chosen[i][0:GHOST, 0:GHOST], received[i])
        else:
            value = received[i].astype(f32)
        rows[STARTS[i] : STARTS[i] + SIZES[i], :] = value[0 : SIZES[i]]
    rows[BASIS_AT:CENTER_AT, :] = w_basis[...].astype(f32)
    rows[CENTER_AT:LIST, :] = jnp.zeros((LIST - CENTER_AT, WIDTH), f32)
    for k in range(HEAD // 128):
        head_proj[:, 128 * k : 128 * k + 128] = rows[128 * k : 128 * k + 128, :].T.astype(bf16)
    for b in range(ATOMS // GROUP):
        rows[CENTER_AT : CENTER_AT + GROUP, :] = center[...].astype(f32)[GROUP * b : GROUP * b + GROUP]
        tail_proj[b] = rows[HEAD:LIST, :].T.astype(bf16)

    coords[...] = jnp.zeros(coords.shape, f32)
    coords[0:3, 0:ATOMS] = positions[...]
    filled = [coords[0:8, 128 * k : 128 * k + 128] for k in range(8)]
    which = rows_of((8, 128))
    for i, d in enumerate(DIRECTIONS):
        value = received_small[i]
        if i in chosen:
            parts = jnp.concatenate(list(pieces(value)) + [jnp.zeros((8, 128), f32)], axis=0)
            parts = nt(parts.astype(bf16), chosen[i])
            value = parts[0:8] + parts[8:16] + parts[16:24]
        step = [t * SIDE * SPACING for t in d]
        shift = jnp.where(which == 0, step[0], jnp.where(which == 1, step[1], step[2]))
        value = value - shift
        k, at = divmod(STARTS[i], 128)
        end = at + SIZES[i]
        value = pltpu.roll(value, at, 1) if at else value
        filled[k] = jnp.where((lane >= at) & (lane < end), value, filled[k])
        if end > 128:
            filled[k + 1] = jnp.where(lane < end - 128, value, filled[k + 1])

    env_back[...] = env_t[...].astype(f32).T.astype(bf16)
    latent_t[...] = w_latent[...].astype(f32).T.astype(bf16)
    out_t[...] = w_out[...].astype(f32).T.astype(bf16)
    final_col[...] = jnp.broadcast_to(column(w_final[...], OUT_WIDTH), (OUT_WIDTH, 128))

    kinds = species[...]
    scale_row = jnp.where(
        kinds == 0,
        kind_scale[0],
        jnp.where(kinds == 1, kind_scale[1], jnp.where(kinds == 2, kind_scale[2], kind_scale[3])),
    )
    shift_row = jnp.where(
        kinds == 0,
        kind_shift[0],
        jnp.where(kinds == 1, kind_shift[1], jnp.where(kinds == 2, kind_shift[2], kind_shift[3])),
    )

    full = (ATOMS, SLOTS)
    local = neighbor[...]
    ghost = local - ATOMS
    cell = jnp.where(ghost < 0, 13, (ghost * 1366) >> 16)
    jump = jnp.zeros((8, 128), i32)
    for i, c in enumerate(CELLS):
        jump = jnp.where(lane == c, STARTS[i] - ATOMS - GHOST * c, jump)
    jump = jnp.concatenate([jump] * 8, axis=0)
    index = local + jnp.take_along_axis(jump, cell, axis=1, mode="promise_in_bounds")
    low, page = index & 127, index >> 7
    rel = []
    for a in range(3):
        found = jnp.zeros(full, f32)
        for k in range(8):
            source = jnp.broadcast_to(filled[k][a : a + 1, :], full)
            taken = jnp.take_along_axis(source, low, axis=1, mode="promise_in_bounds")
            found = jnp.where(page == k, taken, found)
        rel.append(found - column(positions[a : a + 1, :], ATOMS))
    distance = jnp.sqrt(rel[0] * rel[0] + rel[1] * rel[1] + rel[2] * rel[2])
    live = jnp.where(distance * (1.0 / CUT) < 1.0, live_in[...], 0)

    before = jnp.where(rows_of((SLOTS, SLOTS)) < lanes_of((SLOTS, SLOTS)), 1.0, 0.0).astype(bf16)
    gap = nn((1 - live).astype(f32).astype(bf16), before).astype(i32)
    most = jnp.max(jnp.sum(live.astype(f32), axis=1, keepdims=True))
    values = [index] + rel
    for step in range(7):
        by = 1 << step
        moves = jnp.where((gap & by) != 0, live, 0)
        come = pltpu.roll(moves, SLOTS - by, 1) != 0
        values = [jnp.where(come, pltpu.roll(v, SLOTS - by, 1), v) for v in values]
        gap = jnp.where(come, pltpu.roll(gap, SLOTS - by, 1), gap)
        live = jnp.where(come, 1, live - moves)
    kept = live != 0
    slots[0] = jnp.where(kept, values[0], LIST - 1).astype(f32)
    slots[1] = jnp.where(kept, values[1], 0.5 * CUT)
    slots[2] = jnp.where(kept, values[2], 0.0)
    slots[3] = jnp.where(kept, values[3], 0.0)
    slots[4] = live.astype(f32)
    slots[5] = jnp.broadcast_to(column(scale_row, ATOMS), full)

    shared = (
        slots,
        table,
        onehot,
        head_proj,
        tail_proj,
        env_back,
        w_latent,
        w_out,
        w_basis,
        env_t,
        latent_t,
        out_t,
        final_col,
        acc,
        acc_tail,
        energy,
    )

    @pl.when(most <= 96.0)
    def _():
        edge_blocks(96, *shared)

    @pl.when(most > 96.0)
    def _():
        edge_blocks(SLOTS, *shared)

    energy_out[...] = scale_row * row(energy[:, 0:1], ATOMS) + shift_row

    tail = acc_tail[0]
    for b in range(1, ATOMS // GROUP):
        tail = tail + acc_tail[b]
    grad_t[:, 0:HEAD] = acc[0:WIDTH, :].astype(bf16)
    grad_t[:, HEAD:LIST] = tail[0:WIDTH].astype(bf16)
    high, rest = slice(WIDTH, WIDTH + 8), slice(WIDTH + 8, WIDTH + 16)
    coord_grad[:, 0:HEAD] = acc[high, :] + acc[rest, :]
    coord_grad[:, HEAD:LIST] = tail[high] + tail[rest]
    wide = lanes_of((WIDTH + 16, 128))
    pulled = jnp.zeros((WIDTH + 16, 128), f32)
    for b in range(ATOMS // GROUP):
        value = pltpu.roll(acc_tail[b], (GROUP * b - (CENTER_AT - HEAD)) % 128, 1)
        pulled = jnp.where((wide >= GROUP * b) & (wide < GROUP * b + GROUP), value, pulled)
    center_grad[...] = pulled[0:WIDTH].T[0:ATOMS]
    own_proj_grad[...] = acc[0:WIDTH, 0:128].T[0:ATOMS]
    own_pos_grad[...] = jnp.where(lane < ATOMS, coord_grad[:, 0:128] - pulled[high] - pulled[rest], 0.0)


def edges(received, received_small, proj, center, positions, species, neighbor, live, scale, shift, *weights):
    vmem = pl.BlockSpec(memory_space=pltpu.VMEM)
    smem = pl.BlockSpec(memory_space=pltpu.SMEM)
    return pl.pallas_call(
        edge_kernel,
        out_shape=(
            jax.ShapeDtypeStruct((1, ATOMS), f32),
            jax.ShapeDtypeStruct((WIDTH, LIST), bf16),
            jax.ShapeDtypeStruct((8, LIST), f32),
            jax.ShapeDtypeStruct((128, 128), f32),
            jax.ShapeDtypeStruct((128, 128), f32),
            jax.ShapeDtypeStruct((ATOMS, WIDTH), f32),
            jax.ShapeDtypeStruct((ATOMS, WIDTH), f32),
            jax.ShapeDtypeStruct((8, 128), f32),
        ),
        in_specs=[vmem] * 8 + [smem] * 2 + [vmem] * 5,
        out_specs=(vmem,) * 8,
        scratch_shapes=[
            pltpu.VMEM((LIST, WIDTH), f32),
            pltpu.VMEM((8, LIST), f32),
            pltpu.VMEM((WIDTH, HEAD), bf16),
            pltpu.VMEM((8, WIDTH, 128), bf16),
            pltpu.VMEM((WIDTH, 3 * CHANNELS), bf16),
            pltpu.VMEM((WIDTH, WIDTH + 3 * CHANNELS), bf16),
            pltpu.VMEM((OUT_WIDTH, WIDTH), bf16),
            pltpu.VMEM((OUT_WIDTH, 128), f32),
            pltpu.VMEM((6, ATOMS, SLOTS), f32),
            pltpu.VMEM((8, R_COUNT * GROUP, 128), f32),
            pltpu.VMEM((ABREAST, LIST, GROUP * SLOTS), bf16),
            pltpu.VMEM((WIDTH + 16, HEAD), f32),
            pltpu.VMEM((8, WIDTH + 16, 128), f32),
            pltpu.VMEM((ATOMS, 128), f32),
        ],
        compiler_params=pltpu.CompilerParams(vmem_limit_bytes=56 * 1024 * 1024),
        name="edges",
    )(
        received, received_small, proj, center, positions, species, neighbor, live, scale, shift, *weights
    )


def unpack_kernel(
    face_rows, face_small, own_proj_grad, center_grad, own_pos_grad, lists, w_center, w_neighbor, forces,
    feature_grad, padded
):
    padded[...] = jnp.full((32, 128), -1, i32)
    padded[0:27, 0:GHOST] = lists[...]
    proj_grad = own_proj_grad[...]
    pos_grad = jnp.zeros((32, ATOMS), f32)
    atom = rows_of((ATOMS, 128))
    for i, d in enumerate(DIRECTIONS[0:8] + FACES[0:2]):
        cell = FACE_CELLS[first_face(d)]
        chosen = jnp.where(padded[cell : cell + 1, :] == atom, 1.0, 0.0).astype(bf16)
        proj_grad = proj_grad + nn(chosen[:, 0:GHOST], face_rows[i])
        parts = jnp.concatenate(list(pieces(face_small[i])) + [jnp.zeros((8, 128), f32)], axis=0)
        pos_grad = pos_grad + nt(parts.astype(bf16), chosen)
    feature_grad[...] = nt(proj_grad.astype(bf16), w_neighbor[...]) + nt(
        center_grad[...].astype(bf16), w_center[...]
    )
    total = own_pos_grad[:, 0:ATOMS] + pos_grad[0:8] + pos_grad[8:16] + pos_grad[16:24]
    forces[...] = -total[0:3]


def unpack(*args):
    vmem = pl.BlockSpec(memory_space=pltpu.VMEM)
    return pl.pallas_call(
        unpack_kernel,
        out_shape=(
            jax.ShapeDtypeStruct((3, ATOMS), f32),
            jax.ShapeDtypeStruct((ATOMS, WIDTH), f32),
        ),
        in_specs=[vmem] * 8,
        out_specs=(vmem,) * 2,
        scratch_shapes=[pltpu.VMEM((32, 128), i32)],
        name="unpack",
    )(*args)


def solution(mesh):
    sizes = tuple(mesh.shape[a] for a in ("gx", "gy", "gz"))

    def local(
        positions,
        atom_features,
        species,
        edge_neighbor,
        edge_live,
        send_list,
        species_scale,
        species_shift,
        w_center,
        w_neighbor,
        w_basis,
        w_env,
        w_latent,
        w_out,
        w_final,
    ):
        received, received_small, proj, center = send_out(
            atom_features, positions, send_list, w_center, w_neighbor, sizes
        )
        energy, grad_t, coord_grad, lists, faces, own_proj_grad, center_grad, own_pos_grad = edges(
            received,
            received_small,
            proj,
            center,
            positions,
            species.reshape(1, ATOMS),
            edge_neighbor,
            edge_live,
            species_scale,
            species_shift,
            w_basis,
            w_env.T,
            w_latent,
            w_out,
            w_final.reshape(1, OUT_WIDTH),
        )
        owner_rows, owner_small = send_back(grad_t, coord_grad, lists, faces, sizes)
        forces, feature_grad = unpack(
            owner_rows, owner_small, own_proj_grad, center_grad, own_pos_grad, send_list, w_center, w_neighbor
        )
        return energy.reshape(ATOMS), forces, feature_grad

    split = ("gx", "gy", "gz")
    return jax.shard_map(
        local,
        mesh=mesh,
        in_specs=(P(None, split), P(split, None), P(split), P(split, None), P(split, None), P(split, None))
        + (P(),) * 9,
        out_specs=(P(split), P(None, split), P(split, None)),
        check_vma=False,
    )
```
